32 devices in a mesh: rows: 16 (over z, y, x), half: 2 (over core).
Axes of the slice: x: 2, y: 2, z: 4, core: 2. Of those that a mesh axis runs over, the one named last changes fastest.
Arguments:
- pin_features: bfloat16 [16384, 1024], P(('rows', 'half')), may hold values from -6 to 6
- board_features: bfloat16 [16384, 512], P(('rows', 'half')), may hold values from -6 to 6
- node_kinds: int32 [16384], P(('rows', 'half')), may hold values 0 or 1
- neighbours: int32 [16384, 50], P(('rows', 'half')), may hold values from 0 to 1279, as said below
- visit_counts: int32 [16384, 50], P(('rows', 'half')), may hold values from 8 to 32
- served_rows: int32 [512, 16], P(('rows', 'half')), may hold values from 0 to 511
- board_proj: float32 [512, 1024], P(('rows', 'half')), may hold values from -0.25 to 0.25
- neigh_weight: float32 [2, 1024, 1024], P(None, ('rows', 'half')), may hold values from -0.1875 to 0.1875
- neigh_bias: float32 [2, 1024], P(None, ('rows', 'half')), may hold values from -3 to 3
- concat_weight: float32 [2, 2, 1024, 1024], P(None, 'half', 'rows'), may hold values from -0.1875 to 0.1875
- concat_bias: float32 [2, 1024], P(None, ('rows', 'half')), may hold values from -3 to 3
- mlp_weight_one: float32 [2, 1024, 1024], P(None, ('rows', 'half')), may hold values from -0.1875 to 0.1875
- mlp_bias_one: float32 [2, 1024], P(None, ('rows', 'half')), may hold values from -3 to 3
- mlp_weight_two: float32 [2, 1024, 1024], P(None, ('rows', 'half')), may hold values from -0.1875 to 0.1875
- mlp_bias_two: float32 [2, 1024], P(None, ('rows', 'half')), may hold values from -3 to 3
- out_grad: bfloat16 [16384, 1024], P(('rows', 'half')), may hold values from -6 to 6
Outputs:
- embeddings: bfloat16 [16384, 1024], P(('rows', 'half'))
- pin_grad: float32 [16384, 1024], P(('rows', 'half'))
- board_grad: float32 [16384, 512], P(('rows', 'half'))
- board_proj_grad: float32 [512, 1024], P(('rows', 'half'))
- neigh_weight_grad: float32 [2, 1024, 1024], P(None, ('rows', 'half'))
- neigh_bias_grad: float32 [2, 1024], P(None, ('rows', 'half'))
- concat_weight_grad: float32 [2, 2, 1024, 1024], P(None, 'half', 'rows')
- concat_bias_grad: float32 [2, 1024], P(None, ('rows', 'half'))
- mlp_weight_one_grad: float32 [2, 1024, 1024], P(None, ('rows', 'half'))
- mlp_bias_one_grad: float32 [2, 1024], P(None, ('rows', 'half'))
- mlp_weight_two_grad: float32 [2, 1024, 1024], P(None, ('rows', 'half'))
- mlp_bias_two_grad: float32 [2, 1024], P(None, ('rows', 'half'))
The draws below stay inside these ranges and needn't reach their ends.
Inputs may be any that keep to these rules, and one draw needn't show every extreme that they name: `neighbours`: A node's 50 entries are distinct; the first 25 are rows below 1024, the others rows from 1024 on. Rows below 1024 of a device's table are the nodes of its chip in order; from 1024 on come 16 rows from each chip in order of the rows axis, its own included, taken from that chip's device of the same half index.
All inputs are finite; a program needn't handle non-finite values. No bound on the sum of `node_kinds` on one device may be relied on, other than what follows from the above.
Results may differ from the reference program's by a relative error of at most 0.025.
Values may be sent and summed in bfloat16 or wider, within the bound.
No kernel may reach another device: no remote copies, remote signals or barrier semaphores. Data moves between devices by JAX's collectives and lax.ppermute only.
A program may use at most 192 MiB of HBM per device.

```python
import jax
import jax.numpy as jnp
from jax import lax

D = 1024
BOARD = 512
K = 50
L = 2
SLICE = 512
REMOTE = 256
NODES = 16384
CAP = 16
N_ROWS = 16
N_HALF = 2


def region_walk(key, count, region):
    starts = jax.random.randint(jax.random.fold_in(key, 1), (NODES, 1), 0, region)
    strides = jax.random.randint(jax.random.fold_in(key, 2), (NODES, count), 1, region // count + 1)
    return (starts + jnp.cumsum(strides, axis=1)) % region


def draw_neighbours(key, part):
    key = jax.random.fold_in(key, 11)
    near_count = K // 2
    near_rows = region_walk(jax.random.fold_in(key, 21), near_count, 2 * SLICE)
    far_rows = 2 * SLICE + region_walk(jax.random.fold_in(key, 22), K - near_count, REMOTE)
    return jnp.concatenate([near_rows, far_rows], axis=1).astype(jnp.int32)


def draw_visit_counts(key, part):
    key = jax.random.fold_in(key, 12)
    return jax.random.randint(key, (NODES, K), 8, 33).astype(jnp.int32)


def touch_ends(array, stream_key, smallest, top_value):
    longest = array.shape.index(max(array.shape))
    spots = []
    for shift in (0, 1):
        where = [jax.random.randint(jax.random.fold_in(stream_key, axis), (), 0, length) for axis, length in enumerate(array.shape)]
        where[longest] = (where[longest] + shift) % array.shape[longest]
        spots.append(tuple(where))
    return array.at[spots[0]].set(smallest).at[spots[1]].set(top_value)


def levels(key, dims, shards, least, top_value):
    def one(dim, parts):
        heights = jax.random.uniform(jax.random.fold_in(jax.random.fold_in(key, 6), dim), (parts,), jnp.float32, least / len(shards), top_value / len(shards))
        return jnp.repeat(jnp.exp(heights), dims[dim] // parts).reshape((-1,) + (1,) * (len(dims) - dim - 1))

    loudness = one(*shards[0])
    for cut in shards[1:]:
        loudness = loudness * one(*cut)
    return loudness


def centred(rng, dims, deviation, limit, shards=(), kind=jnp.bfloat16):
    gain = levels(rng, dims, shards, -0.22, 0.18) if shards else 1.0
    drawn = jax.random.normal(rng, dims, jnp.float32) * deviation * gain
    return jnp.minimum(jnp.maximum(drawn, -limit), limit).astype(kind)


def setup_inputs(seed: int = 0) -> dict:
    key_of = jax.random.split(jax.random.key(seed), 17)
    pin_features = centred(key_of[0], (NODES, D), 1.0, 6.0, ((0, 32),))
    board_features = centred(key_of[1], (NODES, BOARD), 1.0, 6.0, ((0, 32),))
    node_kinds = touch_ends((jax.random.randint(key_of[2], (NODES,), 0, 2) < 1).astype(jnp.int32), jax.random.fold_in(key_of[2], 1), 0, 1)
    neighbours = draw_neighbours(jax.random.fold_in(key_of[16], 71), 0)
    visit_counts = draw_visit_counts(jax.random.fold_in(key_of[16], 71), 0)
    served_rows = touch_ends(jax.random.randint(key_of[5], (N_ROWS * N_HALF * N_ROWS, CAP), 0, SLICE), jax.random.fold_in(key_of[5], 1), 0, SLICE - 1).astype(jnp.int32)
    board_proj = centred(key_of[6], (BOARD, D), BOARD ** -0.5, 0.25, ((0, 32),), jnp.float32)
    neigh_weight = centred(key_of[7], (L, D, D), D ** -0.5, 0.1875, ((1, 32),), jnp.float32)
    neigh_bias = centred(key_of[8], (L, D), 0.5, 3.0, ((1, 32),), jnp.float32)
    concat_weight = centred(key_of[9], (L, 2, D, D), D ** -0.5, 0.1875, ((1, 2), (2, 16)), jnp.float32)
    concat_bias = centred(key_of[10], (L, D), 0.5, 3.0, ((1, 32),), jnp.float32)
    mlp_weight_one = centred(key_of[11], (L, D, D), D ** -0.5, 0.1875, ((1, 32),), jnp.float32)
    mlp_bias_one = centred(key_of[12], (L, D), 0.5, 3.0, ((1, 32),), jnp.float32)
    mlp_weight_two = centred(key_of[13], (L, D, D), D ** -0.5, 0.1875, ((1, 32),), jnp.float32)
    mlp_bias_two = centred(key_of[14], (L, D), 0.5, 3.0, ((1, 32),), jnp.float32)
    out_grad = centred(key_of[15], (NODES, D), 1.0, 6.0, ((0, 32),))
    return {"pin_features": pin_features, "board_features": board_features, "node_kinds": node_kinds, "neighbours": neighbours, "visit_counts": visit_counts, "served_rows": served_rows, "board_proj": board_proj, "neigh_weight": neigh_weight, "neigh_bias": neigh_bias, "concat_weight": concat_weight, "concat_bias": concat_bias, "mlp_weight_one": mlp_weight_one, "mlp_bias_one": mlp_bias_one, "mlp_weight_two": mlp_weight_two, "mlp_bias_two": mlp_bias_two, "out_grad": out_grad}


@jax.custom_vjp
def low(v):
    return lax.optimization_barrier(v.astype(jnp.bfloat16)).astype(jnp.float32)

@jax.custom_vjp
def low_back(v):
    return v

def low_keep(v):
    return (low(v), None)

def low_pass(kept, grad):
    return (grad,)

def back_keep(v):
    return (v, None)

def back_low(kept, grad):
    return (low(grad),)
low.defvjp(low_keep, low_pass)
low_back.defvjp(back_keep, back_low)

def matmul(left, right):
    return jnp.dot(left, right, precision=lax.Precision.HIGHEST)

def activate(value):
    return jax.nn.gelu(value, approximate=True)

def normalize(value):
    return value * lax.rsqrt(lax.optimization_barrier(jnp.mean(value * value, axis=-1, keepdims=True)) + 1e-06)

def global_rows(neighbours, served_rows):
    node_count = neighbours.shape[0]
    device = (jnp.arange(node_count, dtype=jnp.int32) // SLICE)[:, None]
    chip = device // N_HALF
    core = device % N_HALF
    chip_rows = N_HALF * SLICE
    remote = jnp.maximum(neighbours - chip_rows, 0)
    owner = remote // CAP
    slot_index = remote % CAP
    owner_device = owner * N_HALF + core
    served = served_rows[owner_device * N_ROWS + chip, slot_index]
    far_rows = owner_device * SLICE + served
    near_rows = chip * chip_rows + neighbours
    return jnp.where(neighbours < chip_rows, near_rows, far_rows).astype(jnp.int32)

def aggregate(hidden, node_index, shares):
    blocks = node_index.shape[0] // SLICE
    index_blocks = node_index.reshape(blocks, SLICE, node_index.shape[1])
    share_blocks = shares.reshape(blocks, SLICE, shares.shape[1])

    def one_block(pair):
        picked = hidden[pair[0]]
        return jnp.einsum('jkd,jk->jd', picked, pair[1], precision=lax.Precision.HIGHEST)
    summed = lax.map(jax.checkpoint(one_block), (index_blocks, share_blocks))
    return summed.reshape(node_index.shape[0], hidden.shape[1])

def forward(params, pin_values, board_values, node_kinds, node_index, shares):
    board_proj, neigh_weight, neigh_bias, concat_weight, concat_bias, weight_one, bias_one, weight_two, bias_two = params
    projected = matmul(board_values, low(board_proj))
    features = jnp.where(node_kinds[:, None] == 1, pin_values, projected)
    features = low(low_back(features))
    result = features
    for layer_index in range(L):
        hidden_pre = matmul(features, low(neigh_weight[layer_index])) + low(neigh_bias[layer_index])
        hidden = low(activate(low_back(hidden_pre)))
        neigh_mean = low(low_back(aggregate(hidden, node_index, shares)))
        pre = matmul(features, low(concat_weight[layer_index, 0])) + matmul(neigh_mean, low(concat_weight[layer_index, 1])) + low(concat_bias[layer_index])
        unit_rows = low(normalize(activate(low_back(pre))))
        inner_pre = matmul(unit_rows, low(weight_one[layer_index])) + low(bias_one[layer_index])
        inner_act = low(activate(low_back(inner_pre)))
        result = matmul(inner_act, low(weight_two[layer_index])) + low(bias_two[layer_index])
        if layer_index + 1 < L:
            features = low(low_back(result))
    return result

def reference(pin_features, board_features, node_kinds, neighbours, visit_counts, served_rows, board_proj, neigh_weight, neigh_bias, concat_weight, concat_bias, mlp_weight_one, mlp_bias_one, mlp_weight_two, mlp_bias_two, out_grad):
    node_index = global_rows(neighbours, served_rows)
    counts = visit_counts.astype(jnp.float32)
    shares = low(counts / lax.optimization_barrier(jnp.sum(counts, axis=1, keepdims=True)))
    params = (board_proj, neigh_weight, neigh_bias, concat_weight, concat_bias, mlp_weight_one, mlp_bias_one, mlp_weight_two, mlp_bias_two)
    pin_values = pin_features.astype(jnp.float32)
    board_values = board_features.astype(jnp.float32)

    def run(params, pin_values, board_values):
        return forward(params, pin_values, board_values, node_kinds, node_index, shares)
    result, pullback = jax.vjp(run, params, pin_values, board_values)
    grads, pin_grad, board_grad = pullback(out_grad.astype(jnp.float32))
    return (result.astype(jnp.bfloat16), pin_grad, board_grad, grads[0], grads[1], grads[2], grads[3], grads[4], grads[5], grads[6], grads[7], grads[8])
```

```python
import functools

import jax
import jax.numpy as jnp
from jax import lax
from jax.experimental import pallas as pl
from jax.experimental.pallas import tpu as pltpu
from jax.sharding import PartitionSpec as P

LOW = jnp.bfloat16
AXES = ("rows", "half")
CURVE = 0.7978845608028654
CUBIC = 0.044715
VMEM_BYTES = 32 << 20


def activate(value):
    return 0.5 * value * (1.0 + jnp.tanh(CURVE * (value + CUBIC * value * value * value)))


def activate_slope(value):
    bend = jnp.tanh(CURVE * (value + CUBIC * value * value * value))
    return 0.5 * (1.0 + bend) + 0.5 * value * (1.0 - bend * bend) * CURVE * (
        1.0 + 3.0 * CUBIC * value * value
    )


def matmul(left, right):
    return jnp.dot(left, right, preferred_element_type=jnp.float32)


def matmul_t(left, right):
    return lax.dot_general(
        left, right, (((1,), (1,)), ((), ())), preferred_element_type=jnp.float32
    )


def t_matmul(left, right):
    return lax.dot_general(
        left, right, (((0,), (0,)), ((), ())), preferred_element_type=jnp.float32
    )


def column_sum(value):
    return jnp.sum(value.astype(jnp.float32), axis=0)


class Layout:
    def __init__(self, row_count):
        bits = row_count.bit_length() - 1
        side = 1 << (bits // 3)
        self.rows = row_count
        self.sizes = (side, side, row_count // (side * side))
        self.side, self.deep = side, self.sizes[2]

    def split(self, row):
        return [row % self.side, (row // self.side) % self.side, row // (self.side * self.side)]

    def join(self, place):
        return place[0] + self.side * (place[1] + self.side * place[2])

    def ring(self, dims):
        pairs = []
        for row in range(self.rows):
            for core in range(2):
                place = self.split(row)
                dim = dims[core]
                place[dim] = (place[dim] + 1) % self.sizes[dim]
                pairs.append((row * 2 + core, self.join(place) * 2 + core))
        return lambda value: lax.ppermute(value, AXES, pairs)

    def first(self):
        return self.ring((0, 1))

    def last(self):
        return self.ring((1, 0))

    def middle(self):
        return self.ring((2, 2))

    def order(self, row, core, sign, slots):
        place = self.split(row)
        k, j, i = slots
        middle = (place[2] + sign * k + self.deep) % self.deep
        ahead = jnp.where(core == 0, i, j)
        aside = jnp.where(core == 0, j, i)
        zero = (place[0] + sign * ahead + self.side) % self.side
        one = (place[1] + sign * aside + self.side) % self.side
        return self.join((zero, one, middle)).astype(jnp.int32)


def swap_cores(value):
    return lax.ppermute(value, "half", [(0, 1), (1, 0)])


def gather_pieces(layout, shard):
    forward, deeper, across = layout.first(), layout.middle(), layout.last()
    unit = [shard]
    for _ in range(layout.side - 1):
        unit.append(forward(unit[-1]))
    level = [jnp.stack(unit)]
    for _ in range(layout.deep - 1):
        level.append(deeper(level[-1]))
    own = []
    for item in level:
        own.append(item)
        for _ in range(layout.side - 1):
            own.append(across(own[-1]))
    return own, [swap_cores(item) for item in own]


def gather_orders(layout, row, core):
    k, j, i = jnp.meshgrid(
        jnp.arange(layout.deep), jnp.arange(layout.side), jnp.arange(layout.side), indexing="ij"
    )
    return [
        layout.order(row, which, -1, (k, j, i)).reshape(-1) for which in (core, 1 - core)
    ]


def place_kernel(count, inner, parts, core_ref, own_order, sib_order, *refs):
    own, sib = refs[:count], refs[count : 2 * count]
    outs, sems = refs[2 * count : -1], refs[-1]
    core = core_ref[0]
    copies = []
    for group, order, half in ((own, own_order, core), (sib, sib_order, 1 - core)):
        for number in range(count):
            for i in range(inner):
                row = order[number * inner + i]
                for (offset, rows, paired), out in zip(parts, outs):
                    target = out.at[half, row] if paired else out.at[row, half]
                    copies.append(
                        pltpu.make_async_copy(
                            group[number].at[i, pl.ds(offset, rows)], target, sems.at[len(copies)]
                        )
                    )
    for copy in copies:
        copy.start()
    for copy in copies:
        copy.wait()


def place(layout, own, sib, orders, core, parts):
    count, inner = len(own), layout.side
    width = own[0].shape[-1]
    shapes = [
        jax.ShapeDtypeStruct(
            ((2, layout.rows) if paired else (layout.rows, 2)) + (rows, width), LOW
        )
        for _, rows, paired in parts
    ]
    anywhere = pl.BlockSpec(memory_space=pl.ANY)
    outs = pl.pallas_call(
        functools.partial(place_kernel, count, inner, parts),
        grid_spec=pltpu.PrefetchScalarGridSpec(
            num_scalar_prefetch=3,
            grid=(1,),
            in_specs=[anywhere] * (2 * count),
            out_specs=[pl.BlockSpec(memory_space=pltpu.VMEM)] * len(parts),
            scratch_shapes=[pltpu.SemaphoreType.DMA((2 * count * inner * len(parts),))],
        ),
        out_shape=shapes,
        compiler_params=pltpu.CompilerParams(vmem_limit_bytes=VMEM_BYTES),
        name="place",
    )(core[None], *orders, *own, *sib)
    return [out.reshape(-1, width) for out in outs]


def gather_whole(shard, paired):
    if paired:
        return lax.all_gather(lax.all_gather(shard, "rows", tiled=True), "half", tiled=True)
    return lax.all_gather(shard, AXES, tiled=True)


def scatter_whole(grad, kind):
    if kind == "all":
        return lax.psum(grad, AXES)
    if kind == "paired":
        grad = lax.psum_scatter(grad, "half", scatter_dimension=0, tiled=True)
        return lax.psum_scatter(grad, "rows", scatter_dimension=0, tiled=True)
    return lax.psum_scatter(grad, AXES, scatter_dimension=0, tiled=True)


def sort_kernel(slots, parts, core_ref, own_order, sib_order, *refs):
    outer, inner = slots
    grads = refs[: len(parts)]
    keeps, sends = refs[len(parts) :][:outer], refs[len(parts) + outer :][:outer]
    sems = refs[-1]
    core = core_ref[0]
    copies = []
    for outs, order, half in ((sends, sib_order, 1 - core), (keeps, own_order, core)):
        for j in reversed(range(outer)):
            for n in range(inner):
                row = order[j * inner + n]
                for (offset, rows, kind), grad in zip(parts, grads):
                    if kind == "all":
                        source = grad
                    elif kind == "paired":
                        source = grad.at[half, row]
                    else:
                        source = grad.at[row, half]
                    copies.append(
                        pltpu.make_async_copy(
                            source, outs[j].at[n, pl.ds(offset, rows)], sems.at[len(copies)]
                        )
                    )
    for copy in copies:
        copy.start()
    for copy in copies:
        copy.wait()


def scatter_orders(layout, row, core):
    j, k, i = jnp.meshgrid(
        jnp.arange(layout.side), jnp.arange(layout.deep), jnp.arange(layout.side), indexing="ij"
    )
    return [layout.order(row, which, 1, (k, j, i)).reshape(-1) for which in (core, 1 - core)]


def sort_blocks(layout, grads, kinds, orders, core):
    width = grads[0].shape[-1]
    outer, inner = layout.side, layout.deep * layout.side
    shaped, parts, offset = [], [], 0
    for grad, kind in zip(grads, kinds):
        if kind == "all":
            rows = grad.shape[0]
        else:
            rows = grad.shape[0] // (2 * layout.rows)
            lead = (2, layout.rows) if kind == "paired" else (layout.rows, 2)
            grad = grad.reshape(*lead, rows, width)
        shaped.append(grad)
        parts.append((offset, rows, kind))
        offset += rows
    anywhere = pl.BlockSpec(memory_space=pl.ANY)
    outs = pl.pallas_call(
        functools.partial(sort_kernel, (outer, inner), tuple(parts)),
        grid_spec=pltpu.PrefetchScalarGridSpec(
            num_scalar_prefetch=3,
            grid=(1,),
            in_specs=[pl.BlockSpec(memory_space=pltpu.VMEM)] * len(parts),
            out_specs=[anywhere] * (2 * outer),
            scratch_shapes=[pltpu.SemaphoreType.DMA((2 * outer * inner * len(parts),))],
        ),
        out_shape=[jax.ShapeDtypeStruct((inner, offset, width), LOW)] * (2 * outer),
        compiler_params=pltpu.CompilerParams(vmem_limit_bytes=VMEM_BYTES),
        name="sort",
    )(core[None], *orders, *shaped)
    return outs[:outer], outs[outer:]


def ring_sum(chunks, send):
    total = chunks[-1]
    for chunk in reversed(chunks[:-1]):
        total = chunk + send(total.astype(LOW)).astype(jnp.float32)
    return total


def scatter_sum(layout, kept, sent):
    side = layout.side
    swapped = [None] * side
    for j in reversed(range(side)):
        swapped[j] = swap_cores(sent[j])
    across, deeper, forward = layout.last(), layout.middle(), layout.first()
    columns = [None] * layout.deep
    for k in reversed(range(layout.deep)):
        span = slice(k * side, (k + 1) * side)
        columns[k] = ring_sum(
            [
                kept[j][span].astype(jnp.float32) + swapped[j][span].astype(jnp.float32)
                for j in range(side)
            ],
            across,
        )
    total = ring_sum(columns, deeper)
    return ring_sum([total[i] for i in range(side)], forward)


def make_mixing(neighbours, counts, near_rows, table_rows):
    node_count, width = neighbours.shape
    near_count = width // 2
    block = 16

    def kernel(index_ref, count_ref, out_ref):
        index = index_ref[...]
        values = count_ref[...].astype(jnp.float32)
        shares = values / jnp.sum(values, axis=1, keepdims=True)
        spans = ((0, near_rows, 0, near_count), (near_rows, table_rows, near_count, width))
        for low, high, begin, end in spans:
            column = low + lax.broadcasted_iota(jnp.int32, (block, high - low), 1)
            total = jnp.zeros((block, high - low), jnp.float32)
            for k in range(begin, end):
                total = jnp.where(index[:, k : k + 1] == column, shares[:, k : k + 1], total)
            out_ref[:, low:high] = total.astype(LOW)

    return pl.pallas_call(
        kernel,
        grid=(node_count // block,),
        in_specs=[pl.BlockSpec((block, width), lambda n: (n, 0))] * 2,
        out_specs=pl.BlockSpec((block, table_rows), lambda n: (n, 0)),
        out_shape=jax.ShapeDtypeStruct((node_count, table_rows), LOW),
        name="mixing",
    )(neighbours, counts)


def local(
    pin_features,
    board_features,
    node_kinds,
    neighbours,
    visit_counts,
    served_rows,
    board_proj,
    neigh_weight,
    neigh_bias,
    concat_weight,
    concat_bias,
    mlp_weight_one,
    mlp_bias_one,
    mlp_weight_two,
    mlp_bias_two,
    out_grad,
):
    slice_rows, width = pin_features.shape
    layers = neigh_weight.shape[0]
    peers, slots = served_rows.shape
    near_rows = 2 * slice_rows
    far_rows = peers * slots
    table_rows = near_rows + far_rows
    layout = Layout(peers)
    row, core = lax.axis_index("rows"), lax.axis_index("half")
    device = row * 2 + core

    biases = jnp.concatenate([neigh_bias, concat_bias, mlp_bias_one, mlp_bias_two])
    own_bias = biases.shape[1]
    lane = lax.broadcasted_iota(jnp.int32, (biases.shape[0], width), 1)
    bias_rows = jnp.where(lane // own_bias == device, jnp.tile(biases, (1, width // own_bias)), 0.0)
    low = lambda value: value.astype(LOW)
    halves = concat_weight[:, 0]
    last = layers - 1
    proj_rows, neigh_rows, half_rows = board_proj.shape[0], neigh_weight.shape[1], halves.shape[1]
    aligned = all(rows % 16 == 0 for rows in (proj_rows, neigh_rows, half_rows))
    chunk_zero = jnp.concatenate([low(board_proj), low(neigh_weight[0]), low(bias_rows)])
    orders = gather_orders(layout, row, core)
    neigh_full, both_full, first_full, second_full = ([None] * layers for _ in range(4))

    if aligned:
        own, sib = gather_pieces(layout, chunk_zero)
        spec = ((0, proj_rows, False), (proj_rows, neigh_rows, False))
        proj_full, neigh_full[0] = place(layout, own, sib, orders, core, spec)
        bias_full = sum(
            jnp.sum(item[:, proj_rows + neigh_rows :].astype(jnp.float32), 0) for item in own + sib
        )
    else:
        proj_full = gather_whole(low(board_proj), False)
        neigh_full[0] = gather_whole(low(neigh_weight[0]), False)
        bias_full = lax.psum(low(bias_rows).astype(jnp.float32), AXES)
    bias_full = bias_full.reshape(4, layers, width)
    for layer in range(layers):
        blocks = [halves[layer], mlp_weight_one[layer], mlp_weight_two[layer]]
        spec = [(0, half_rows, True), (half_rows, neigh_rows, False)]
        spec.append((half_rows + neigh_rows, neigh_rows, False))
        if layer:
            blocks.append(neigh_weight[layer])
            spec.append((half_rows + 2 * neigh_rows, neigh_rows, False))
        if aligned:
            own, sib = gather_pieces(layout, low(jnp.concatenate(blocks)))
            outs = place(layout, own, sib, orders, core, tuple(spec))
        else:
            outs = [gather_whole(low(block), item[2]) for block, item in zip(blocks, spec)]
        both_full[layer], first_full[layer], second_full[layer] = outs[:3]
        if layer:
            neigh_full[layer] = outs[3]

    turned = jnp.where(
        neighbours < near_rows, (neighbours + near_rows - core * slice_rows) % near_rows, neighbours
    )
    mixing = make_mixing(turned, visit_counts, near_rows, table_rows)
    mix_own = mixing[:, :slice_rows]
    mix_sib = mixing[:, slice_rows:near_rows]
    mix_far = mixing[:, near_rows:]
    served = served_rows.reshape(-1)
    node = lax.broadcasted_iota(jnp.int32, (far_rows, slice_rows), 1)
    picking = (served[:, None] == node).astype(LOW)
    is_pin = (node_kinds == 1)[:, None]
    projected = matmul(board_features, proj_full)
    features = low(jnp.where(is_pin, pin_features.astype(jnp.float32), projected))
    saved = []
    result = None
    for layer in range(layers):
        hidden_pre = matmul(features, neigh_full[layer]) + bias_full[0, layer]
        hidden = low(activate(hidden_pre))
        other = swap_cores(hidden)
        outgoing = low(matmul(picking, hidden)).reshape(peers, slots, width)
        incoming = lax.all_to_all(outgoing, "rows", split_axis=0, concat_axis=0, tiled=True)
        neigh_mean = low(
            matmul(mix_own, hidden)
            + matmul(mix_sib, other)
            + matmul(mix_far, incoming.reshape(far_rows, width))
        )
        both = both_full[layer]
        pre = matmul(features, both[:width]) + matmul(neigh_mean, both[width:]) + bias_full[1, layer]
        gated = activate(pre)
        scale = lax.rsqrt(jnp.mean(gated * gated, axis=-1, keepdims=True) + 1e-06)
        unit = low(gated * scale)
        inner_pre = matmul(unit, first_full[layer]) + bias_full[2, layer]
        inner = low(activate(inner_pre))
        result = matmul(inner, second_full[layer]) + bias_full[3, layer]
        saved.append((features, hidden_pre, neigh_mean, pre, unit, inner_pre, inner))
        features = low(result)
    embeddings = features

    scatter = scatter_orders(layout, row, core)
    grad_result = out_grad
    sums = [[None] * layers for _ in range(4)]
    g_neigh, g_both, g_first, g_second = ([None] * layers for _ in range(4))
    waiting, waiting_kinds = [], []
    out_pieces = []
    grad_input = None

    def flush():
        if aligned:
            kept, sent = sort_blocks(layout, list(waiting), list(waiting_kinds), scatter, core)
            out_pieces.append(scatter_sum(layout, kept, sent))
        else:
            each = [scatter_whole(*item) for item in zip(waiting, waiting_kinds)]
            out_pieces.append(jnp.concatenate([item.astype(jnp.float32) for item in each]))
        waiting.clear()
        waiting_kinds.clear()

    def leave(grad, kind):
        waiting.append(low(grad))
        waiting_kinds.append(kind)

    for layer in reversed(range(layers)):
        features, hidden_pre, neigh_mean, pre, unit, inner_pre, inner = saved[layer]
        leave(t_matmul(inner, grad_result), "plain")
        sums[3][layer] = column_sum(grad_result)
        grad_inner = low(matmul_t(grad_result, second_full[layer]) * activate_slope(inner_pre))
        leave(t_matmul(unit, grad_inner), "plain")
        flush()
        sums[2][layer] = column_sum(grad_inner)
        grad_unit = matmul_t(grad_inner, first_full[layer])
        gated = activate(pre)
        scale = lax.rsqrt(jnp.mean(gated * gated, axis=-1, keepdims=True) + 1e-06)
        mean_dot = jnp.mean(gated * grad_unit, axis=-1, keepdims=True)
        grad_gated = scale * grad_unit - gated * (scale * scale * scale * mean_dot)
        grad_pre = low(grad_gated * activate_slope(pre))
        sums[1][layer] = column_sum(grad_pre)
        both = both_full[layer]
        grad_mean = low(matmul_t(grad_pre, both[width:]))
        grad_far = low(t_matmul(mix_far, grad_mean)).reshape(peers, slots, width)
        far_back = lax.all_to_all(grad_far, "rows", split_axis=0, concat_axis=0, tiled=True)
        sib_back = swap_cores(low(t_matmul(mix_sib, grad_mean)))
        leave(
            jnp.concatenate([t_matmul(features, grad_pre), t_matmul(neigh_mean, grad_pre)]),
            "paired",
        )
        flush()
        grad_hidden = (
            t_matmul(mix_own, grad_mean)
            + sib_back.astype(jnp.float32)
            + t_matmul(picking, far_back.reshape(far_rows, width))
        )
        grad_hidden_pre = low(grad_hidden * activate_slope(hidden_pre))
        leave(t_matmul(features, grad_hidden_pre), "plain")
        sums[0][layer] = column_sum(grad_hidden_pre)
        grad_input = low(
            matmul_t(grad_pre, both[:width]) + matmul_t(grad_hidden_pre, neigh_full[layer])
        )
        grad_result = grad_input
    pin_grad = jnp.where(is_pin, grad_input.astype(jnp.float32), 0.0)
    grad_board = jnp.where(is_pin, jnp.zeros_like(grad_input), grad_input)
    leave(t_matmul(board_features, grad_board), "plain")
    bias_sums = jnp.stack([total for group in sums for total in group])
    leave(jnp.concatenate([bias_sums, jnp.zeros((16 - bias_sums.shape[0], width))]), "all")
    flush()
    board_grad = matmul_t(grad_board, proj_full)

    for number, layer in enumerate(reversed(range(layers))):
        mlp = out_pieces[2 * number]
        base = neigh_rows if number else 0
        if number:
            g_neigh[layer + 1] = mlp[:neigh_rows]
        g_second[layer] = mlp[base : base + neigh_rows]
        g_first[layer] = mlp[base + neigh_rows : base + 2 * neigh_rows]
        g_both[layer] = out_pieces[2 * number + 1]
    tail = out_pieces[-1]
    g_neigh[0] = tail[:neigh_rows]
    proj_grad = tail[neigh_rows : neigh_rows + proj_rows]
    bias_grad = tail[neigh_rows + proj_rows :][: biases.shape[0]]
    bias_grad = lax.dynamic_slice_in_dim(bias_grad, device * own_bias, own_bias, 1)
    bias_grad = bias_grad.reshape(4, layers, own_bias)
    return (
        embeddings,
        pin_grad,
        board_grad,
        proj_grad,
        jnp.stack(g_neigh),
        bias_grad[0],
        jnp.stack(g_both)[:, None],
        bias_grad[1],
        jnp.stack(g_first),
        bias_grad[2],
        jnp.stack(g_second),
        bias_grad[3],
    )


def solution(mesh):
    nodes = P(("rows", "half"), None)
    weight = P(None, ("rows", "half"), None)
    bias = P(None, ("rows", "half"))
    concat = P(None, "half", "rows", None)
    placed = (nodes, nodes, P(("rows", "half")), nodes, nodes, nodes, nodes)
    placed += (weight, bias, concat, bias, weight, bias, weight, bias, nodes)
    return jax.shard_map(
        local,
        mesh=mesh,
        in_specs=placed,
        out_specs=(nodes, nodes, nodes, nodes)
        + (weight, bias, concat, bias, weight, bias, weight, bias),
        check_vma=False,
    )
```

```python
import jax
import jax.numpy as jnp
from jax import lax
from jax.experimental import pallas as pl
from jax.experimental.pallas import tpu as pltpu
from jax.sharding import PartitionSpec as P

LOW = jnp.bfloat16
AXES = ("rows", "half")
CURVE = 0.7978845608028654
CUBIC = 0.044715
TILE = 256


def activate(value):
    return jax.nn.gelu(value, approximate=True)


def unit_map(value):
    scaled = activate(value)
    return scaled * lax.rsqrt(jnp.mean(scaled * scaled, axis=-1, keepdims=True) + 1e-06)


def matmul(left, right):
    return jnp.dot(left, right, preferred_element_type=jnp.float32)


def column_sum(value):
    return jnp.sum(value.astype(jnp.float32), axis=0)


def fetch_shared(
    neigh_weight, neigh_bias, concat_bias, weight_one, bias_one, weight_two, bias_two, board_proj
):
    return (
        lax.all_gather(neigh_weight, ("rows", "half"), axis=1, tiled=True),
        lax.all_gather(neigh_bias, ("rows", "half"), axis=1, tiled=True),
        lax.all_gather(concat_bias, ("rows", "half"), axis=1, tiled=True),
        lax.all_gather(weight_one, ("rows", "half"), axis=1, tiled=True),
        lax.all_gather(bias_one, ("rows", "half"), axis=1, tiled=True),
        lax.all_gather(weight_two, ("rows", "half"), axis=1, tiled=True),
        lax.all_gather(bias_two, ("rows", "half"), axis=1, tiled=True),
        lax.all_gather(board_proj, ("rows", "half"), axis=0, tiled=True),
    )


def fetch_half(own_half):
    return lax.all_gather(own_half, "rows", axis=1, tiled=True)


def refetch_shared(
    neigh_weight, neigh_bias, concat_bias, weight_one, bias_one, weight_two, bias_two, board_proj
):
    return (
        lax.all_gather(neigh_weight, ("rows", "half"), axis=1, tiled=True),
        lax.all_gather(neigh_bias, ("rows", "half"), axis=1, tiled=True),
        lax.all_gather(concat_bias, ("rows", "half"), axis=1, tiled=True),
        lax.all_gather(weight_one, ("rows", "half"), axis=1, tiled=True),
        lax.all_gather(bias_one, ("rows", "half"), axis=1, tiled=True),
        lax.all_gather(weight_two, ("rows", "half"), axis=1, tiled=True),
        lax.all_gather(bias_two, ("rows", "half"), axis=1, tiled=True),
        lax.all_gather(board_proj, ("rows", "half"), axis=0, tiled=True),
    )


def refetch_half(own_half):
    return lax.all_gather(own_half, "rows", axis=1, tiled=True)


def plain(
    pin_features,
    board_features,
    node_kinds,
    neighbours,
    visit_counts,
    served_rows,
    board_proj,
    neigh_weight,
    neigh_bias,
    concat_weight,
    concat_bias,
    mlp_weight_one,
    mlp_bias_one,
    mlp_weight_two,
    mlp_bias_two,
    out_grad,
):
    slice_rows, feature_width = pin_features.shape
    layer_count = neigh_weight.shape[0]
    peer_count, slot_count = served_rows.shape
    chip_rows = 2 * slice_rows
    table_rows = chip_rows + peer_count * slot_count
    counts = visit_counts.astype(jnp.float32)
    shares = (counts / jnp.sum(counts, axis=1, keepdims=True)).astype(jnp.bfloat16)
    positions = jnp.broadcast_to(jnp.arange(slice_rows, dtype=jnp.int32)[:, None], neighbours.shape)
    mixing = jnp.zeros((slice_rows, table_rows), jnp.bfloat16).at[positions, neighbours].set(shares)
    served_flat = served_rows.reshape(-1)
    is_pin = (node_kinds == 1)[:, None]
    to_low = jnp.bfloat16
    master_pieces = (
        neigh_weight.astype(to_low),
        neigh_bias.astype(to_low),
        concat_bias.astype(to_low),
        mlp_weight_one.astype(to_low),
        mlp_bias_one.astype(to_low),
        mlp_weight_two.astype(to_low),
        mlp_bias_two.astype(to_low),
        board_proj.astype(to_low),
    )
    own_half = concat_weight[:, 0].astype(to_low)
    shared_full = fetch_shared(*master_pieces)
    half_full = fetch_half(own_half)
    (
        neigh_full,
        nbias_full,
        cbias_full,
        first_full,
        fbias_full,
        second_full,
        sbias_full,
        proj_full,
    ) = shared_full
    projected = matmul(board_features, proj_full)
    features = jnp.where(is_pin, pin_features.astype(jnp.float32), projected).astype(to_low)
    saved = []
    result = None
    for layer_index in range(layer_count):
        hidden_pre = matmul(features, neigh_full[layer_index]) + nbias_full[layer_index].astype(
            jnp.float32
        )
        hidden_full, hidden_pull = jax.vjp(activate, hidden_pre)
        hidden = hidden_full.astype(to_low)
        chip_hidden = lax.all_gather(hidden, "half", axis=0, tiled=True)
        outgoing = hidden[served_rows]
        incoming = lax.all_to_all(outgoing, "rows", split_axis=0, concat_axis=0, tiled=True)
        lookup_table = jnp.concatenate([chip_hidden, incoming.reshape(-1, feature_width)], axis=0)
        neigh_mean = matmul(mixing, lookup_table).astype(to_low)
        paired = lax.all_to_all(
            jnp.stack([features, neigh_mean]), "half", split_axis=0, concat_axis=1, tiled=True
        )[0]
        partial_value = matmul(paired, half_full[layer_index])
        pre_sum = lax.psum_scatter(
            partial_value.astype(jnp.bfloat16), "half", scatter_dimension=0, tiled=True
        ).astype(jnp.float32) + cbias_full[layer_index].astype(jnp.float32)
        unit_full, unit_pull = jax.vjp(unit_map, pre_sum)
        unit_rows = unit_full.astype(to_low)
        inner_pre = matmul(unit_rows, first_full[layer_index]) + fbias_full[layer_index].astype(
            jnp.float32
        )
        inner_full, inner_pull = jax.vjp(activate, inner_pre)
        inner_act = inner_full.astype(to_low)
        result = matmul(inner_act, second_full[layer_index]) + sbias_full[layer_index].astype(
            jnp.float32
        )
        saved.append((features, hidden_pull, paired, unit_rows, unit_pull, inner_act, inner_pull))
        features = result.astype(to_low)
    embeddings = result.astype(to_low)
    (
        neigh_full,
        nbias_full,
        cbias_full,
        first_full,
        fbias_full,
        second_full,
        sbias_full,
        proj_full,
    ) = refetch_shared(*master_pieces)
    half_full = refetch_half(own_half)
    grad_result = out_grad
    grads_neigh = [None] * layer_count
    grads_nbias = [None] * layer_count
    grads_half = [None] * layer_count
    grads_cbias = [None] * layer_count
    grads_first = [None] * layer_count
    grads_fbias = [None] * layer_count
    grads_second = [None] * layer_count
    grads_sbias = [None] * layer_count
    grad_input = None
    for layer_index in reversed(range(layer_count)):
        features, hidden_pull, paired, unit_rows, unit_pull, inner_act, inner_pull = saved[
            layer_index
        ]
        grads_second[layer_index] = matmul(inner_act.T, grad_result)
        grads_sbias[layer_index] = column_sum(grad_result)
        grad_inner = inner_pull(matmul(grad_result, second_full[layer_index].T))[0].astype(to_low)
        grads_first[layer_index] = matmul(unit_rows.T, grad_inner)
        grads_fbias[layer_index] = column_sum(grad_inner)
        grad_pre = unit_pull(matmul(grad_inner, first_full[layer_index].T))[0].astype(to_low)
        grads_cbias[layer_index] = column_sum(grad_pre)
        grad_pre_full = lax.all_gather(grad_pre, "half", axis=0, tiled=True)
        grads_half[layer_index] = matmul(paired.T, grad_pre_full)
        grad_paired = matmul(grad_pre_full, half_full[layer_index].T)
        returned = lax.all_to_all(
            grad_paired[None].astype(jnp.bfloat16), "half", split_axis=1, concat_axis=0, tiled=True
        ).astype(jnp.float32)
        grad_self = returned[0]
        grad_mean = returned[1].astype(to_low)
        grad_table = matmul(mixing.T, grad_mean)
        grad_chip = lax.psum_scatter(
            grad_table[:chip_rows].astype(jnp.bfloat16), "half", scatter_dimension=0, tiled=True
        ).astype(jnp.float32)
        grad_far = lax.all_to_all(
            grad_table[chip_rows:]
            .reshape(peer_count, slot_count, feature_width)
            .astype(jnp.bfloat16),
            "rows",
            split_axis=0,
            concat_axis=0,
            tiled=True,
        ).astype(jnp.float32)
        grad_hidden = grad_chip.at[served_flat].add(grad_far.reshape(-1, feature_width))
        grad_hidden_pre = hidden_pull(grad_hidden)[0].astype(to_low)
        grads_neigh[layer_index] = matmul(features.T, grad_hidden_pre)
        grads_nbias[layer_index] = column_sum(grad_hidden_pre)
        grad_input = (grad_self + matmul(grad_hidden_pre, neigh_full[layer_index].T)).astype(to_low)
        grad_result = grad_input
    pin_grad = jnp.where(is_pin, grad_input.astype(jnp.float32), 0.0)
    grad_board = jnp.where(is_pin, jnp.zeros_like(grad_input), grad_input)
    board_grad = matmul(grad_board, proj_full.T)
    proj_grad = matmul(board_features.T, grad_board)
    summed = (
        lax.psum_scatter(jnp.stack(grads_neigh), ("rows", "half"), scatter_dimension=1, tiled=True),
        lax.psum_scatter(jnp.stack(grads_nbias), ("rows", "half"), scatter_dimension=1, tiled=True),
        lax.psum_scatter(jnp.stack(grads_cbias), ("rows", "half"), scatter_dimension=1, tiled=True),
        lax.psum_scatter(jnp.stack(grads_first), ("rows", "half"), scatter_dimension=1, tiled=True),
        lax.psum_scatter(jnp.stack(grads_fbias), ("rows", "half"), scatter_dimension=1, tiled=True),
        lax.psum_scatter(
            jnp.stack(grads_second), ("rows", "half"), scatter_dimension=1, tiled=True
        ),
        lax.psum_scatter(jnp.stack(grads_sbias), ("rows", "half"), scatter_dimension=1, tiled=True),
        lax.psum_scatter(proj_grad, ("rows", "half"), scatter_dimension=0, tiled=True),
    )
    half_summed = lax.psum_scatter(jnp.stack(grads_half), "rows", scatter_dimension=1, tiled=True)
    (
        neigh_grad,
        nbias_grad,
        cbias_grad,
        first_grad,
        fbias_grad,
        second_grad,
        sbias_grad,
        board_proj_grad,
    ) = summed
    return (
        embeddings,
        pin_grad,
        board_grad,
        board_proj_grad,
        neigh_grad,
        nbias_grad,
        half_summed[:, None],
        cbias_grad,
        first_grad,
        fbias_grad,
        second_grad,
        sbias_grad,
    )


def low(value):
    return value.astype(LOW)


def wide(value):
    return value.astype(jnp.float32)


class Layout:
    def __init__(self, row_count):
        self.rows = row_count
        self.deep = row_count // 4
        self.sizes = (2, 2, self.deep)

    def split(self, row):
        return [row % 2, (row // 2) % 2, row // 4]

    def join(self, place):
        return place[0] + 2 * (place[1] + 2 * place[2])

    def ring(self, dims, value):
        pairs = []
        for row in range(self.rows):
            for core in range(2):
                place = self.split(row)
                dim = dims[core]
                place[dim] = (place[dim] + 1) % self.sizes[dim]
                pairs.append((row * 2 + core, self.join(place) * 2 + core))
        return lax.ppermute(value, AXES, pairs)

    def first(self, value):
        return self.ring((0, 1), value)

    def last(self, value):
        return self.ring((1, 0), value)

    def middle(self, value):
        return self.ring((2, 2), value)

    def order(self, row, core, sign, slots):
        place = self.split(row)
        k, j, i = (jnp.array(part, jnp.int32) for part in zip(*slots))
        ahead = jnp.where(core == 0, i, j)
        aside = jnp.where(core == 0, j, i)
        middle = (place[2] + sign * k + self.deep) % self.deep
        return self.join(((place[0] + ahead) % 2, (place[1] + aside) % 2, middle)).astype(jnp.int32)


def swap_cores(value):
    return lax.ppermute(value, "half", [(0, 1), (1, 0)])


class Gather:
    def __init__(self, layout, parts):
        self.layout = layout
        self.levels = [low(jnp.concatenate(parts))[None]]
        self.pairs, self.squares, self.swapped = [], [], []

    def deepen(self):
        self.levels.append(self.layout.middle(self.levels[-1]))

    def ahead(self):
        item = self.levels[len(self.pairs)]
        self.pairs.append(jnp.concatenate([item, self.layout.first(item)]))

    def aside(self):
        self.squares.append(self.layout.last(self.pairs[len(self.squares)]))

    def swap(self):
        number = len(self.swapped) // 2
        self.swapped += [swap_cores(self.pairs[number]), swap_cores(self.squares[number])]

    def pieces(self):
        own = [item for pair in zip(self.pairs, self.squares) for item in pair]
        return own + self.swapped

    def slots(self):
        return [
            (k, j, i) for k in range(self.layout.deep) for j in range(2) for i in range(2)
        ]

    @property
    def values(self):
        return (self.levels, self.pairs, self.squares, self.swapped)

    @values.setter
    def values(self, held):
        self.levels, self.pairs, self.squares, self.swapped = (list(item) for item in held)


class Scatter:
    def __init__(self, layout, kept, sent, deep_last):
        self.layout, self.deep_last = layout, deep_last
        self.values = [kept, sent]
        around = [self.deepen] * (layout.deep - 1)
        if deep_last:
            self.plan = [self.swap, self.aside, self.ahead, *around]
        else:
            self.plan = [self.swap, self.aside, *around, self.ahead]
        self.level = layout.deep - 1
        self.shape = (layout.deep, 2, *kept.shape[1:])

    def advance(self):
        self.plan.pop(0)()

    def near(self, *index):
        kept, got, came = self.values[:3]
        half = (2, *self.shape)
        return (
            wide(kept.reshape(half)[(0, *index)])
            + wide(got.reshape(half)[(0, *index)])
            + wide(came.reshape(self.shape)[index])
        )

    def swap(self):
        self.values = [self.values[0], swap_cores(self.values[1])]

    def aside(self):
        kept, got = self.values
        half = self.layout.rows // 2
        self.values = [kept, got, self.layout.last(low(wide(kept[half:]) + wide(got[half:])))]

    def total(self, *index):
        result = self.near(self.level, *index)
        if self.deep_last:
            result = self.near(self.level, 0) + wide(self.values[3][self.level])
        if self.level < self.layout.deep - 1:
            came = wide(self.values[-1])
            result = result + (came[index] if index else came)
        return result

    def deepen(self):
        got = self.layout.middle(low(self.total()))
        self.values = [*self.values[: 4 if self.deep_last else 3], got]
        self.level -= 1

    def ahead(self):
        if self.deep_last:
            send = self.near(slice(None), 1)
        else:
            send = self.total(1)
        self.values = [*self.values, self.layout.first(low(send))]

    def result(self):
        if self.deep_last:
            return self.total()
        got = self.values.pop()
        return self.total(0) + wide(got)


def tie(chains, *values):
    held, values = lax.optimization_barrier(([chain.values for chain in chains], values))
    for chain, item in zip(chains, held):
        chain.values = item
    return values[0] if len(values) == 1 else values


def dot(left, right):
    return jnp.dot(left, right, preferred_element_type=jnp.float32)


def dot_right(left, right):
    return lax.dot_general(
        left, right, (((1,), (1,)), ((), ())), preferred_element_type=jnp.float32
    )


def dot_left(left, right):
    return lax.dot_general(
        left, right, (((0,), (0,)), ((), ())), preferred_element_type=jnp.float32
    )


def gelu_pair(value):
    square = value * value
    bend = jnp.tanh(value * (CURVE + CURVE * CUBIC * square))
    half = 0.5 + 0.5 * bend
    slope = half + value * (0.5 - 0.5 * bend * bend) * (CURVE + 3.0 * CURVE * CUBIC * square)
    return value * half, slope


def tiles(size):
    def run(body):
        @pl.loop(0, size // TILE)
        def _(number):
            body(pl.ds(pl.multiple_of(number * TILE, TILE), TILE))

    return run


def call(name, body, tables, ins, far, outs, far_outs, scratch):
    counts = [len(group) for group in (tables, ins, far, outs, far_outs, scratch)]

    def kernel(*refs):
        groups = []
        for count in counts:
            groups.append(refs[:count])
            refs = refs[count:]
        body(*groups)

    def spec(space, count):
        return [pl.BlockSpec(memory_space=space)] * count

    return pl.pallas_call(
        kernel,
        in_specs=spec(pltpu.SMEM, counts[0]) + spec(pltpu.VMEM, counts[1]) + spec(pl.ANY, counts[2]),
        out_specs=spec(pltpu.VMEM, counts[3]) + spec(pl.ANY, counts[4]),
        out_shape=[jax.ShapeDtypeStruct(*item) for item in (*outs, *far_outs)],
        scratch_shapes=scratch,
        compiler_params=pltpu.CompilerParams(vmem_limit_bytes=48 << 20),
        cost_estimate=pl.CostEstimate(flops=1, bytes_accessed=1, transcendentals=0),
        name=name,
    )(*tables, *ins, *far)


def fetch(tables, pieces, part, target, sem):
    core, orders = tables[0][0], tables[1:3]
    offset, rows, paired = part
    count = len(pieces) // 2
    for group, order, half in ((pieces[:count], orders[0], core), (pieces[count:], orders[1], 1 - core)):
        index = 0
        for piece in group:
            for number in range(piece.shape[0]):
                row = order[index]
                index += 1
                block = half * (target.shape[0] // rows // 2) + row if paired else row * 2 + half
                begin = pl.multiple_of(block * rows, 16)
                pltpu.make_async_copy(
                    piece.at[number, pl.ds(offset, rows)], target.at[pl.ds(begin, rows)], sem
                ).start()


def fetched(target, sem):
    pltpu.make_async_copy(target, target, sem).wait()


def send_off(tables, grad, part, kept, sent, sems):
    core, orders = tables[0][0], tables[3:5]
    offset, rows, kind = part
    for out, order, half, sem in (
        (sent, orders[1], 1 - core, sems[1]),
        (kept, orders[0], core, sems[0]),
    ):
        for position in range(out.shape[0]):
            row = order[position]
            if kind == "all":
                block = 0
            elif kind == "paired":
                block = half * out.shape[0] + row
            else:
                block = row * 2 + half
            begin = pl.multiple_of(block * rows, 16)
            pltpu.make_async_copy(
                grad.at[pl.ds(begin, rows)], out.at[position, pl.ds(offset, rows)], sem
            ).start()


def sent_off(part, kept, sent, sems):
    offset, rows, _ = part
    for out, sem in zip((kept, sent), sems):
        view = out.at[:, pl.ds(offset, rows)]
        pltpu.make_async_copy(view, view, sem).wait()


def spread_hidden(features, weight, bias, picking, hidden, slope, outgoing):
    @tiles(weight.shape[1])
    def _(span):
        value, bent = gelu_pair(dot(features[...], weight[:, span]) + bias[:, span])
        hidden[:, span] = low(value)
        slope[:, span] = low(bent)

    outgoing[...] = low(dot(picking[...], hidden[...]))


def average(mixes, hidden, other, incoming, mean):
    own, sib, far = mixes

    @tiles(mean.shape[1])
    def _(span):
        mean[:, span] = low(
            dot(own[...], hidden[:, span])
            + dot(sib[...], other[:, span])
            + dot(far[...], incoming[:, span])
        )


def combine(features, mean, both, bias, gated, unit, slope, scale):
    width = features.shape[1]
    scale[...] = jnp.zeros_like(scale)

    @tiles(width)
    def _(span):
        pre = dot(features[...], both[:width, span]) + dot(mean[...], both[width:, span])
        value, bent = gelu_pair(pre + bias[:, span])
        gated[:, span] = value
        slope[:, span] = low(bent)
        scale[...] += jnp.sum(value * value, axis=1, keepdims=True)

    scale[...] = lax.rsqrt(scale[...] * (1.0 / width) + 1e-06)

    @tiles(width)
    def _(span):
        unit[:, span] = low(gated[:, span] * scale[...])


def perceive(unit, first, first_bias, inner, slope):
    @tiles(first.shape[1])
    def _(span):
        value, bent = gelu_pair(dot(unit[...], first[:, span]) + first_bias[:, span])
        inner[:, span] = low(value)
        slope[:, span] = low(bent)


def conclude(inner, second, second_bias, result):
    @tiles(second.shape[1])
    def _(span):
        result[:, span] = low(dot(inner[...], second[:, span]) + second_bias[:, span])


def weight_grad(left, right, grad, begin=0):
    @tiles(left.shape[1])
    def _(span):
        band = low(dot_left(left[:, span], right[...]))
        grad[pl.ds(pl.multiple_of(span.start + begin, TILE), TILE), :] = band


def column_sums(value, sums, row):
    @tiles(value.shape[1])
    def _(span):
        sums[row : row + 1, span] = jnp.sum(wide(value[:, span]), axis=0, keepdims=True)


def back_perceive(grad_result, second, slope, grad_inner):
    @tiles(grad_inner.shape[1])
    def _(span):
        grad_inner[:, span] = low(
            dot_right(grad_result[...], second[span, :]) * wide(slope[:, span])
        )


def back_unit(grad_inner, first, unit, scale, slope, grad_unit, mean_dot, grad_pre):
    width = unit.shape[1]
    mean_dot[...] = jnp.zeros_like(mean_dot)

    @tiles(width)
    def _(span):
        value = dot_right(grad_inner[...], first[span, :])
        grad_unit[:, span] = value
        mean_dot[...] += jnp.sum(value * wide(unit[:, span]), axis=1, keepdims=True)

    mean_dot[...] = mean_dot[...] * (1.0 / width)

    @tiles(width)
    def _(span):
        value = scale[...] * (grad_unit[:, span] - wide(unit[:, span]) * mean_dot[...])
        grad_pre[:, span] = low(value * wide(slope[:, span]))


def back_mean(grad_pre, both, mix_turned, grad_mean, far_out, sib_out):
    width = grad_mean.shape[1]

    @tiles(width)
    def _(span):
        rows = pl.ds(pl.multiple_of(span.start + width, TILE), TILE)
        grad_mean[:, span] = low(dot_right(grad_pre[...], both[rows, :]))

    sib, far = mix_turned
    far_out[...] = low(dot(far[...], grad_mean[...]))
    sib_out[...] = low(dot(sib[...], grad_mean[...]))


def back_hidden(own, pick, grad_mean, sib_back, far_back, slope, grad_hidden_pre):
    @tiles(grad_mean.shape[1])
    def _(span):
        value = dot(own[...], grad_mean[:, span]) + dot(pick[...], far_back[:, span])
        value = value + wide(sib_back[:, span])
        grad_hidden_pre[:, span] = low(value * wide(slope[:, span]))


def back_input(grad_self, grad_hidden_pre, weight, grad_input):
    @tiles(grad_input.shape[1])
    def _(span):
        grad_input[:, span] = low(
            grad_self[:, span] + dot_right(grad_hidden_pre[...], weight[span, :])
        )


def mix_rows(neighbours, counts, spans, so_far, begin, end):
    node_count, count = neighbours.shape
    block = 16

    def kernel(index_ref, count_ref, *refs):
        outs = refs[-len(spans) :]
        index = index_ref[...]
        values = count_ref[...].astype(jnp.float32)
        shares = values / jnp.sum(values, axis=1, keepdims=True)
        for number, ((first, last), out_ref) in enumerate(zip(spans, outs)):
            column = first + lax.broadcasted_iota(jnp.int32, (block, last - first), 1)
            total = jnp.zeros((block, last - first), jnp.float32)
            far = number == len(spans) - 1
            for k in range(count // 2 if far else 0, count if far else count // 2):
                total = jnp.where(index[:, k : k + 1] == column, shares[:, k : k + 1], total)
            out_ref[...] = total.astype(LOW)

    start = begin // block
    rows = lambda n: (n + start, 0)
    shapes = [jax.ShapeDtypeStruct((node_count, last - first), LOW) for first, last in spans]
    return pl.pallas_call(
        kernel,
        grid=((end - begin) // block,),
        in_specs=[pl.BlockSpec((block, count), rows)] * 2
        + [pl.BlockSpec(memory_space=pl.ANY)] * len(so_far),
        out_specs=[pl.BlockSpec((block, last - first), rows) for first, last in spans],
        out_shape=shapes,
        input_output_aliases={2 + n: n for n in range(len(so_far))},
        cost_estimate=pl.CostEstimate(flops=1, bytes_accessed=1, transcendentals=0),
        name="mixing",
    )(neighbours, counts, *so_far)


def local(
    pin_features,
    board_features,
    node_kinds,
    neighbours,
    visit_counts,
    served_rows,
    board_proj,
    neigh_weight,
    neigh_bias,
    concat_weight,
    concat_bias,
    mlp_weight_one,
    mlp_bias_one,
    mlp_weight_two,
    mlp_bias_two,
    out_grad,
):
    slice_rows, width = pin_features.shape
    board_width = board_features.shape[1]
    peers, slots = served_rows.shape
    near_rows, far_rows = 2 * slice_rows, peers * slots
    layout = Layout(peers)
    row, core = lax.axis_index("rows"), lax.axis_index("half")
    device = row * 2 + core
    biases = jnp.concatenate([neigh_bias, concat_bias, mlp_bias_one, mlp_bias_two])
    bias_count, own_bias = biases.shape
    lane = lax.broadcasted_iota(jnp.int32, (bias_count, width), 1)
    bias_rows = jnp.where(lane // own_bias == device, jnp.tile(biases, (1, width // own_bias)), 0.0)
    halves = concat_weight[:, 0]
    proj_rows, rows, half_rows = board_proj.shape[0], neigh_weight.shape[1], halves.shape[1]

    turned = jnp.where(
        neighbours < near_rows, (neighbours + near_rows - core * slice_rows) % near_rows, neighbours
    )
    spans = ((0, slice_rows), (slice_rows, near_rows), (near_rows, near_rows + far_rows))
    mixing = []

    def mix_more(part):
        size = slice_rows // 4
        return mix_rows(turned, visit_counts, spans, mixing, part * size, (part + 1) * size)

    served = served_rows.reshape(-1)
    node = lax.broadcasted_iota(jnp.int32, (far_rows, slice_rows), 1)
    picking = (served[:, None] == node).astype(LOW)
    node = lax.broadcasted_iota(jnp.int32, (slice_rows, far_rows), 0)
    pick_turned = (served[None, :] == node).astype(LOW)
    kinds = node_kinds[:, None]

    zero = Gather(layout, [board_proj, neigh_weight[0], bias_rows])
    one = Gather(layout, [halves[0], mlp_weight_one[0], mlp_weight_two[0], neigh_weight[1]])
    two = Gather(layout, [halves[1], mlp_weight_one[1], mlp_weight_two[1]])
    proj_part, neigh_zero = (0, proj_rows, False), (proj_rows, rows, False)
    both_part, first_part = (0, half_rows, True), (half_rows, rows, False)
    second_part, neigh_one = (half_rows + rows, rows, False), (half_rows + 2 * rows, rows, False)

    slots_in = zero.slots()
    slots_out = [(k, j, i) for j in range(2) for k in range(layout.deep) for i in range(2)]
    tables = [core[None].astype(jnp.int32)]
    tables += [layout.order(row, which, -1, slots_in) for which in (core, 1 - core)]
    tables += [layout.order(row, which, 1, slots_out) for which in (core, 1 - core)]

    nodes_low = ((slice_rows, width), LOW)
    nodes_wide = ((slice_rows, width), jnp.float32)
    far_low = ((far_rows, width), LOW)
    column = ((slice_rows, 1), jnp.float32)
    sum_rows = ((8, width), jnp.float32)
    matrix = pltpu.VMEM((width, width), LOW)
    matrices = pltpu.VMEM((2 * width, width), LOW)
    own_nodes = pltpu.VMEM(*nodes_low)
    own_wide = pltpu.VMEM(*nodes_wide)
    own_column = pltpu.VMEM(*column)
    dma = pltpu.SemaphoreType.DMA

    def leaving(count):
        return [((layout.rows, count, width), LOW)] * 2

    def exchange(outgoing):
        far = lax.all_to_all(
            outgoing.reshape(peers, slots, width), "rows", split_axis=0, concat_axis=0, tiled=True
        )
        return far.reshape(far_rows, width)

    for part in range(4):
        if part < layout.deep - 1:
            zero.deepen()
        zero.ahead()
        mixing = tie([zero], mix_more(part))
        zero.aside()
    for part in range(3, layout.deep - 1):
        zero.deepen()
    for part in range(4, layout.deep):
        zero.ahead()
        zero.aside()
    for chain, before in ((one, zero), (two, one)):
        chain.levels, before.levels = lax.optimization_barrier((chain.levels, before.levels))
        for _ in range(layout.deep - 1):
            chain.deepen()
        for _ in range(layout.deep):
            chain.ahead()
            chain.aside()
    for chain in (zero, one, two):
        for _ in range(layout.deep):
            chain.swap()
    begin = proj_rows + rows
    bias_full = sum(jnp.sum(wide(item[:, begin:]), 0) for item in zero.pieces())

    def hidden_body(tables, ins, pieces, outs, _, scratch):
        pin, board, kinds, bias, picking = ins
        features, hidden, slope, outgoing, proj = outs
        weight, sems = scratch
        fetch(tables, pieces, proj_part, proj, sems.at[0])
        fetch(tables, pieces, neigh_zero, weight, sems.at[1])
        fetched(proj, sems.at[0])

        @tiles(width)
        def _(span):
            projected = dot(board[...], proj[:, span])
            features[:, span] = low(jnp.where(kinds[...] == 1, wide(pin[:, span]), projected))

        fetched(weight, sems.at[1])
        spread_hidden(features, weight, bias.at[0:1], picking, hidden, slope, outgoing)

    features, hidden, hidden_slope, outgoing, proj_full = call(
        "hidden",
        hidden_body,
        tables,
        [pin_features, board_features, kinds, bias_full, picking],
        zero.pieces(),
        [nodes_low] * 3 + [far_low, ((board_width, width), LOW)],
        [],
        [matrix, dma((2,))],
    )
    incoming, other = exchange(outgoing), swap_cores(hidden)

    def middle_body(tables, ins, pieces, outs, _, scratch):
        mixes, (hidden, other, incoming, features, bias, picking) = ins[:3], ins[3:]
        mean, unit, slope_pre, scale, inner, slope_inner, result, ahead, slope_ahead, outgoing = outs
        both, first, second, weight, gated, sems = scratch
        for number, (part, target) in enumerate(
            ((both_part, both), (first_part, first), (second_part, second), (neigh_one, weight))
        ):
            fetch(tables, pieces, part, target, sems.at[number])
        average(mixes, hidden, other, incoming, mean)
        fetched(both, sems.at[0])
        combine(features, mean, both, bias.at[2:3], gated, unit, slope_pre, scale)
        fetched(first, sems.at[1])
        perceive(unit, first, bias.at[4:5], inner, slope_inner)
        fetched(second, sems.at[2])
        conclude(inner, second, bias.at[6:7], result)
        fetched(weight, sems.at[3])
        spread_hidden(result, weight, bias.at[1:2], picking, ahead, slope_ahead, outgoing)

    (
        mean_zero,
        unit,
        slope_pre,
        scale,
        inner,
        slope_inner,
        features_one,
        hidden_one,
        hidden_slope_one,
        outgoing,
    ) = call(
        "middle",
        middle_body,
        tables,
        [*mixing, hidden, other, incoming, features, bias_full, picking],
        one.pieces(),
        [nodes_low] * 3 + [column] + [nodes_low] * 5 + [far_low],
        [],
        [matrices, matrix, matrix, matrix, own_wide, dma((4,))],
    )
    incoming, other = exchange(outgoing), swap_cores(hidden_one)
    mix_turned = [item.T for item in mixing]

    second_grad, first_grad = (0, rows, "plain"), (rows, rows, "plain")

    def top_body(tables, ins, pieces, outs, leave, scratch):
        mixes, (hidden, other, incoming, features, bias, grad_result) = ins[:3], ins[3:9]
        mix_turned = ins[9:]
        mean, result, grad_pre, grad_mean, far_out, sib_out, sums = outs
        (
            both,
            first,
            second,
            second_out,
            first_out,
            gated,
            unit,
            slope_pre,
            scale,
            inner,
            slope_inner,
            grad_inner,
            mean_dot,
            sems,
            out_sems,
        ) = scratch
        for number, (part, target) in enumerate(
            ((both_part, both), (first_part, first), (second_part, second))
        ):
            fetch(tables, pieces, part, target, sems.at[number])
        average(mixes, hidden, other, incoming, mean)
        fetched(both, sems.at[0])
        combine(features, mean, both, bias.at[3:4], gated, unit, slope_pre, scale)
        fetched(first, sems.at[1])
        perceive(unit, first, bias.at[5:6], inner, slope_inner)
        fetched(second, sems.at[2])
        weight_grad(inner, grad_result, second_out)
        send_off(tables, second_out, second_grad, *leave, (out_sems.at[0], out_sems.at[1]))
        back_perceive(grad_result, second, slope_inner, grad_inner)
        weight_grad(unit, grad_inner, first_out)
        send_off(tables, first_out, first_grad, *leave, (out_sems.at[2], out_sems.at[3]))
        back_unit(grad_inner, first, unit, scale, slope_pre, gated, mean_dot, grad_pre)
        back_mean(grad_pre, both, mix_turned, grad_mean, far_out, sib_out)
        conclude(inner, second, bias.at[7:8], result)
        sums[...] = jnp.zeros_like(sums)
        column_sums(grad_result, sums, 0)
        column_sums(grad_inner, sums, 1)
        column_sums(grad_pre, sums, 2)
        sent_off(second_grad, *leave, (out_sems.at[0], out_sems.at[1]))
        sent_off(first_grad, *leave, (out_sems.at[2], out_sems.at[3]))

    (mean_one, embeddings, grad_pre, grad_mean, far_out, sib_out, sums_one, kept, sent) = call(
        "top",
        top_body,
        tables,
        [*mixing, hidden_one, other, incoming, features_one, bias_full, out_grad, *mix_turned[1:]],
        two.pieces(),
        [nodes_low] * 4 + [far_low, nodes_low, sum_rows],
        leaving(2 * rows),
        [matrices] + [matrix] * 4
        + [own_wide, own_nodes, own_nodes, own_column, own_nodes, own_nodes, own_nodes, own_column]
        + [dma((3,)), dma((4,))],
    )

    def sides(name, features, mean, grad_pre, pieces):
        part = (0, half_rows, "paired")

        def body(tables, ins, pieces, outs, leave, scratch):
            features, mean, grad_pre = ins
            both, grad, sems = scratch
            fetch(tables, pieces, both_part, both, sems.at[0])
            weight_grad(features, grad_pre, grad)
            weight_grad(mean, grad_pre, grad, width)
            send_off(tables, grad, part, *leave, (sems.at[1], sems.at[2]))
            fetched(both, sems.at[0])

            @tiles(width)
            def _(span):
                outs[0][:, span] = dot_right(grad_pre[...], both[span, :])

            sent_off(part, *leave, (sems.at[1], sems.at[2]))

        return call(
            name,
            body,
            tables,
            [features, mean, grad_pre],
            pieces,
            [nodes_wide],
            leaving(half_rows),
            [matrices, matrices, dma((3,))],
        )

    five = Scatter(layout, kept, sent, True)
    five.advance()
    far_back, sib_back = exchange(far_out), swap_cores(sib_out)
    grad_self, kept, sent = sides("sides1", features_one, mean_one, grad_pre, two.pieces())
    far_back, sib_back, grad_self, kept, sent = tie([five], far_back, sib_back, grad_self, kept, sent)
    six = Scatter(layout, kept, sent, False)

    neigh_grad = (0, rows, "plain")
    second_grad_zero, first_grad_zero = (rows, rows, "plain"), (2 * rows, rows, "plain")

    def bridge_body(tables, ins, pieces, outs, leave, scratch):
        own, pick, grad_mean_one, sib_back, far_back, slope_hidden, features, grad_self = ins[:8]
        inner, unit, slope_inner, slope_pre, scale = ins[8:13]
        mix_turned = ins[13:]
        grad_pre, grad_mean, far_out, sib_out, sums = outs
        (
            weight,
            both,
            first,
            second,
            weight_out,
            second_out,
            first_out,
            grad_hidden_pre,
            grad_input,
            grad_inner,
            grad_unit,
            mean_dot,
            sems,
            out_sems,
        ) = scratch
        for number, (part, target) in enumerate(
            ((neigh_one, weight), (second_part, second), (first_part, first), (both_part, both))
        ):
            fetch(tables, pieces, part, target, sems.at[number])
        pairs = [(out_sems.at[2 * n], out_sems.at[2 * n + 1]) for n in range(3)]
        back_hidden(own, pick, grad_mean_one, sib_back, far_back, slope_hidden, grad_hidden_pre)
        weight_grad(features, grad_hidden_pre, weight_out)
        send_off(tables, weight_out, neigh_grad, *leave, pairs[0])
        fetched(weight, sems.at[0])
        back_input(grad_self, grad_hidden_pre, weight, grad_input)
        weight_grad(inner, grad_input, second_out)
        send_off(tables, second_out, second_grad_zero, *leave, pairs[1])
        fetched(second, sems.at[1])
        back_perceive(grad_input, second, slope_inner, grad_inner)
        weight_grad(unit, grad_inner, first_out)
        send_off(tables, first_out, first_grad_zero, *leave, pairs[2])
        fetched(first, sems.at[2])
        back_unit(grad_inner, first, unit, scale, slope_pre, grad_unit, mean_dot, grad_pre)
        fetched(both, sems.at[3])
        back_mean(grad_pre, both, mix_turned, grad_mean, far_out, sib_out)
        sums[...] = jnp.zeros_like(sums)
        column_sums(grad_hidden_pre, sums, 0)
        column_sums(grad_input, sums, 1)
        column_sums(grad_inner, sums, 2)
        column_sums(grad_pre, sums, 3)
        for part, pair in zip((neigh_grad, second_grad_zero, first_grad_zero), pairs):
            sent_off(part, *leave, pair)

    five.advance()
    six.advance()
    (grad_pre, grad_mean, far_out, sib_out, sums_zero, kept, sent) = tie(
        [five, six],
        *call(
            "bridge",
            bridge_body,
            tables,
            [mix_turned[0], pick_turned, grad_mean, sib_back, far_back, hidden_slope_one]
            + [features_one, grad_self, inner, unit, slope_inner, slope_pre, scale, *mix_turned[1:]],
            one.pieces(),
            [nodes_low] * 2 + [far_low, nodes_low, sum_rows],
            leaving(3 * rows),
            [matrix, matrices] + [matrix] * 5
            + [own_nodes, own_nodes, own_nodes, own_wide, own_column, dma((4,)), dma((6,))],
        ),
    )
    seven = Scatter(layout, kept, sent, False)
    five.advance()
    six.advance()
    seven.advance()
    far_back, sib_back = exchange(far_out), swap_cores(sib_out)
    grad_self, kept, sent = sides("sides0", features, mean_zero, grad_pre, one.pieces())
    far_back, sib_back, grad_self, kept, sent = tie(
        [five, six, seven], far_back, sib_back, grad_self, kept, sent
    )
    eight = Scatter(layout, kept, sent, False)

    proj_grad = (rows, proj_rows, "plain")
    bias_grad = (rows + proj_rows, 16, "all")

    def bottom_body(tables, ins, pieces, outs, leave, scratch):
        own, pick, grad_mean, sib_back, far_back, slope_hidden, features, grad_self = ins[:8]
        board, kinds, sums_one, sums_zero = ins[8:]
        (grad_input,) = outs
        weight, weight_out, proj_out, bias_out, grad_hidden_pre, grad_board, sums, sems = scratch
        pairs = [(sems.at[2 * n + 1], sems.at[2 * n + 2]) for n in range(3)]
        fetch(tables, pieces, neigh_zero, weight, sems.at[0])
        back_hidden(own, pick, grad_mean, sib_back, far_back, slope_hidden, grad_hidden_pre)
        weight_grad(features, grad_hidden_pre, weight_out)
        send_off(tables, weight_out, neigh_grad, *leave, pairs[0])
        column_sums(grad_hidden_pre, sums, 0)
        bias_out[...] = low(
            jnp.concatenate(
                [
                    sums[0:1, :],
                    sums_zero[0:1, :],
                    sums_zero[3:4, :],
                    sums_one[2:3, :],
                    sums_zero[2:3, :],
                    sums_one[1:2, :],
                    sums_zero[1:2, :],
                    sums_one[0:1, :],
                    jnp.zeros((8, width), jnp.float32),
                ]
            )
        )
        send_off(tables, bias_out, bias_grad, *leave, pairs[1])
        fetched(weight, sems.at[0])
        back_input(grad_self, grad_hidden_pre, weight, grad_input)

        @tiles(width)
        def _(span):
            grad_board[:, span] = low(jnp.where(kinds[...] == 1, 0.0, wide(grad_input[:, span])))

        weight_grad(board, grad_board, proj_out)
        send_off(tables, proj_out, proj_grad, *leave, pairs[2])
        for part, pair in zip((neigh_grad, bias_grad, proj_grad), pairs):
            sent_off(part, *leave, pair)

    five.advance()
    six.advance()
    seven.advance()
    eight.advance()
    grad_input, kept, sent = tie(
        [five, six, seven, eight],
        *call(
            "bottom",
            bottom_body,
            tables,
            [mix_turned[0], pick_turned, grad_mean, sib_back, far_back, hidden_slope, features]
            + [grad_self, board_features, kinds, sums_one, sums_zero],
            zero.pieces(),
            [nodes_low],
            leaving(rows + proj_rows + 16),
            [matrix, matrix, pltpu.VMEM((board_width, width), LOW), pltpu.VMEM((16, width), LOW)]
            + [own_nodes, own_nodes, pltpu.VMEM(*sum_rows), dma((7,))],
        ),
    )
    nine = Scatter(layout, kept, sent, True)
    chains = [five, six, seven, eight, nine]
    while any(chain.plan for chain in chains):
        moving = [chain for chain in chains if chain.plan]
        for chain in moving:
            chain.advance()
        tie(moving)
    is_pin = kinds == 1
    pin_grad = jnp.where(is_pin, wide(grad_input), 0.0)
    grad_board = jnp.where(is_pin, jnp.zeros_like(grad_input), grad_input)
    board_grad = dot_right(grad_board, proj_full)

    five, six, seven, eight, nine = (chain.result() for chain in chains)
    bias_sums = nine[rows + proj_rows :][:bias_count]
    bias_sums = lax.dynamic_slice_in_dim(bias_sums, device * own_bias, own_bias, 1)
    bias_sums = bias_sums.reshape(4, -1, own_bias)
    return (
        embeddings,
        pin_grad,
        board_grad,
        nine[rows : rows + proj_rows],
        jnp.stack([nine[:rows], seven[:rows]]),
        bias_sums[0],
        jnp.stack([eight, six])[:, None],
        bias_sums[1],
        jnp.stack([seven[2 * rows :], five[rows:]]),
        bias_sums[2],
        jnp.stack([seven[rows : 2 * rows], five[:rows]]),
        bias_sums[3],
    )


def solution(mesh):
    nodes = P(("rows", "half"), None)
    weight = P(None, ("rows", "half"), None)
    bias = P(None, ("rows", "half"))
    concat = P(None, "half", "rows", None)
    placed = (nodes, nodes, P(("rows", "half")), nodes, nodes, nodes, nodes)
    placed += (weight, bias, concat, bias, weight, bias, weight, bias, nodes)
    results = (nodes, nodes, nodes, nodes) + (weight, bias, concat, bias, weight, bias, weight, bias)

    def whole(*args):
        devices = mesh.shape["rows"] * mesh.shape["half"]
        shards = (args[6].shape[0] // devices, args[7].shape[1] // devices)
        fits = mesh.shape["rows"] % 4 == 0 and not any(count % 16 for count in shards)
        return jax.shard_map(
            local if fits else plain,
            mesh=mesh,
            in_specs=placed,
            out_specs=results,
            check_vma=False,
        )(*args)

    return whole
```

```python
import jax
import jax.numpy as jnp
from jax import lax
from jax.experimental import pallas as pl
from jax.experimental.pallas import tpu as pltpu
from jax.sharding import PartitionSpec as P

LOW = jnp.bfloat16
AXES = ("rows", "half")
CURVE = 0.7978845608028654
CUBIC = 0.044715
TILE = 256


def activate(value):
    return jax.nn.gelu(value, approximate=True)


def unit_map(value):
    scaled = activate(value)
    return scaled * lax.rsqrt(jnp.mean(scaled * scaled, axis=-1, keepdims=True) + 1e-06)


def matmul(left, right):
    return jnp.dot(left, right, preferred_element_type=jnp.float32)


def column_sum(value):
    return jnp.sum(value.astype(jnp.float32), axis=0)


def fetch_shared(
    neigh_weight, neigh_bias, concat_bias, weight_one, bias_one, weight_two, bias_two, board_proj
):
    return (
        lax.all_gather(neigh_weight, ("rows", "half"), axis=1, tiled=True),
        lax.all_gather(neigh_bias, ("rows", "half"), axis=1, tiled=True),
        lax.all_gather(concat_bias, ("rows", "half"), axis=1, tiled=True),
        lax.all_gather(weight_one, ("rows", "half"), axis=1, tiled=True),
        lax.all_gather(bias_one, ("rows", "half"), axis=1, tiled=True),
        lax.all_gather(weight_two, ("rows", "half"), axis=1, tiled=True),
        lax.all_gather(bias_two, ("rows", "half"), axis=1, tiled=True),
        lax.all_gather(board_proj, ("rows", "half"), axis=0, tiled=True),
    )


def fetch_half(own_half):
    return lax.all_gather(own_half, "rows", axis=1, tiled=True)


def refetch_shared(
    neigh_weight, neigh_bias, concat_bias, weight_one, bias_one, weight_two, bias_two, board_proj
):
    return (
        lax.all_gather(neigh_weight, ("rows", "half"), axis=1, tiled=True),
        lax.all_gather(neigh_bias, ("rows", "half"), axis=1, tiled=True),
        lax.all_gather(concat_bias, ("rows", "half"), axis=1, tiled=True),
        lax.all_gather(weight_one, ("rows", "half"), axis=1, tiled=True),
        lax.all_gather(bias_one, ("rows", "half"), axis=1, tiled=True),
        lax.all_gather(weight_two, ("rows", "half"), axis=1, tiled=True),
        lax.all_gather(bias_two, ("rows", "half"), axis=1, tiled=True),
        lax.all_gather(board_proj, ("rows", "half"), axis=0, tiled=True),
    )


def refetch_half(own_half):
    return lax.all_gather(own_half, "rows", axis=1, tiled=True)


def plain(
    pin_features,
    board_features,
    node_kinds,
    neighbours,
    visit_counts,
    served_rows,
    board_proj,
    neigh_weight,
    neigh_bias,
    concat_weight,
    concat_bias,
    mlp_weight_one,
    mlp_bias_one,
    mlp_weight_two,
    mlp_bias_two,
    out_grad,
):
    slice_rows, feature_width = pin_features.shape
    layer_count = neigh_weight.shape[0]
    peer_count, slot_count = served_rows.shape
    chip_rows = 2 * slice_rows
    table_rows = chip_rows + peer_count * slot_count
    counts = visit_counts.astype(jnp.float32)
    shares = (counts / jnp.sum(counts, axis=1, keepdims=True)).astype(jnp.bfloat16)
    positions = jnp.broadcast_to(jnp.arange(slice_rows, dtype=jnp.int32)[:, None], neighbours.shape)
    mixing = jnp.zeros((slice_rows, table_rows), jnp.bfloat16).at[positions, neighbours].set(shares)
    served_flat = served_rows.reshape(-1)
    is_pin = (node_kinds == 1)[:, None]
    to_low = jnp.bfloat16
    master_pieces = (
        neigh_weight.astype(to_low),
        neigh_bias.astype(to_low),
        concat_bias.astype(to_low),
        mlp_weight_one.astype(to_low),
        mlp_bias_one.astype(to_low),
        mlp_weight_two.astype(to_low),
        mlp_bias_two.astype(to_low),
        board_proj.astype(to_low),
    )
    own_half = concat_weight[:, 0].astype(to_low)
    shared_full = fetch_shared(*master_pieces)
    half_full = fetch_half(own_half)
    (
        neigh_full,
        nbias_full,
        cbias_full,
        first_full,
        fbias_full,
        second_full,
        sbias_full,
        proj_full,
    ) = shared_full
    projected = matmul(board_features, proj_full)
    features = jnp.where(is_pin, pin_features.astype(jnp.float32), projected).astype(to_low)
    saved = []
    result = None
    for layer_index in range(layer_count):
        hidden_pre = matmul(features, neigh_full[layer_index]) + nbias_full[layer_index].astype(
            jnp.float32
        )
        hidden_full, hidden_pull = jax.vjp(activate, hidden_pre)
        hidden = hidden_full.astype(to_low)
        chip_hidden = lax.all_gather(hidden, "half", axis=0, tiled=True)
        outgoing = hidden[served_rows]
        incoming = lax.all_to_all(outgoing, "rows", split_axis=0, concat_axis=0, tiled=True)
        lookup_table = jnp.concatenate([chip_hidden, incoming.reshape(-1, feature_width)], axis=0)
        neigh_mean = matmul(mixing, lookup_table).astype(to_low)
        paired = lax.all_to_all(
            jnp.stack([features, neigh_mean]), "half", split_axis=0, concat_axis=1, tiled=True
        )[0]
        partial_value = matmul(paired, half_full[layer_index])
        pre_sum = lax.psum_scatter(
            partial_value.astype(jnp.bfloat16), "half", scatter_dimension=0, tiled=True
        ).astype(jnp.float32) + cbias_full[layer_index].astype(jnp.float32)
        unit_full, unit_pull = jax.vjp(unit_map, pre_sum)
        unit_rows = unit_full.astype(to_low)
        inner_pre = matmul(unit_rows, first_full[layer_index]) + fbias_full[layer_index].astype(
            jnp.float32
        )
        inner_full, inner_pull = jax.vjp(activate, inner_pre)
        inner_act = inner_full.astype(to_low)
        result = matmul(inner_act, second_full[layer_index]) + sbias_full[layer_index].astype(
            jnp.float32
        )
        saved.append((features, hidden_pull, paired, unit_rows, unit_pull, inner_act, inner_pull))
        features = result.astype(to_low)
    embeddings = result.astype(to_low)
    (
        neigh_full,
        nbias_full,
        cbias_full,
        first_full,
        fbias_full,
        second_full,
        sbias_full,
        proj_full,
    ) = refetch_shared(*master_pieces)
    half_full = refetch_half(own_half)
    grad_result = out_grad
    grads_neigh = [None] * layer_count
    grads_nbias = [None] * layer_count
    grads_half = [None] * layer_count
    grads_cbias = [None] * layer_count
    grads_first = [None] * layer_count
    grads_fbias = [None] * layer_count
    grads_second = [None] * layer_count
    grads_sbias = [None] * layer_count
    grad_input = None
    for layer_index in reversed(range(layer_count)):
        features, hidden_pull, paired, unit_rows, unit_pull, inner_act, inner_pull = saved[
            layer_index
        ]
        grads_second[layer_index] = matmul(inner_act.T, grad_result)
        grads_sbias[layer_index] = column_sum(grad_result)
        grad_inner = inner_pull(matmul(grad_result, second_full[layer_index].T))[0].astype(to_low)
        grads_first[layer_index] = matmul(unit_rows.T, grad_inner)
        grads_fbias[layer_index] = column_sum(grad_inner)
        grad_pre = unit_pull(matmul(grad_inner, first_full[layer_index].T))[0].astype(to_low)
        grads_cbias[layer_index] = column_sum(grad_pre)
        grad_pre_full = lax.all_gather(grad_pre, "half", axis=0, tiled=True)
        grads_half[layer_index] = matmul(paired.T, grad_pre_full)
        grad_paired = matmul(grad_pre_full, half_full[layer_index].T)
        returned = lax.all_to_all(
            grad_paired[None].astype(jnp.bfloat16), "half", split_axis=1, concat_axis=0, tiled=True
        ).astype(jnp.float32)
        grad_self = returned[0]
        grad_mean = returned[1].astype(to_low)
        grad_table = matmul(mixing.T, grad_mean)
        grad_chip = lax.psum_scatter(
            grad_table[:chip_rows].astype(jnp.bfloat16), "half", scatter_dimension=0, tiled=True
        ).astype(jnp.float32)
        grad_far = lax.all_to_all(
            grad_table[chip_rows:]
            .reshape(peer_count, slot_count, feature_width)
            .astype(jnp.bfloat16),
            "rows",
            split_axis=0,
            concat_axis=0,
            tiled=True,
        ).astype(jnp.float32)
        grad_hidden = grad_chip.at[served_flat].add(grad_far.reshape(-1, feature_width))
        grad_hidden_pre = hidden_pull(grad_hidden)[0].astype(to_low)
        grads_neigh[layer_index] = matmul(features.T, grad_hidden_pre)
        grads_nbias[layer_index] = column_sum(grad_hidden_pre)
        grad_input = (grad_self + matmul(grad_hidden_pre, neigh_full[layer_index].T)).astype(to_low)
        grad_result = grad_input
    pin_grad = jnp.where(is_pin, grad_input.astype(jnp.float32), 0.0)
    grad_board = jnp.where(is_pin, jnp.zeros_like(grad_input), grad_input)
    board_grad = matmul(grad_board, proj_full.T)
    proj_grad = matmul(board_features.T, grad_board)
    summed = (
        lax.psum_scatter(jnp.stack(grads_neigh), ("rows", "half"), scatter_dimension=1, tiled=True),
        lax.psum_scatter(jnp.stack(grads_nbias), ("rows", "half"), scatter_dimension=1, tiled=True),
        lax.psum_scatter(jnp.stack(grads_cbias), ("rows", "half"), scatter_dimension=1, tiled=True),
        lax.psum_scatter(jnp.stack(grads_first), ("rows", "half"), scatter_dimension=1, tiled=True),
        lax.psum_scatter(jnp.stack(grads_fbias), ("rows", "half"), scatter_dimension=1, tiled=True),
        lax.psum_scatter(
            jnp.stack(grads_second), ("rows", "half"), scatter_dimension=1, tiled=True
        ),
        lax.psum_scatter(jnp.stack(grads_sbias), ("rows", "half"), scatter_dimension=1, tiled=True),
        lax.psum_scatter(proj_grad, ("rows", "half"), scatter_dimension=0, tiled=True),
    )
    half_summed = lax.psum_scatter(jnp.stack(grads_half), "rows", scatter_dimension=1, tiled=True)
    (
        neigh_grad,
        nbias_grad,
        cbias_grad,
        first_grad,
        fbias_grad,
        second_grad,
        sbias_grad,
        board_proj_grad,
    ) = summed
    return (
        embeddings,
        pin_grad,
        board_grad,
        board_proj_grad,
        neigh_grad,
        nbias_grad,
        half_summed[:, None],
        cbias_grad,
        first_grad,
        fbias_grad,
        second_grad,
        sbias_grad,
    )


def low(value):
    return value.astype(LOW)


def wide(value):
    return value.astype(jnp.float32)


class Layout:
    def __init__(self, row_count):
        self.rows = row_count
        self.deep = row_count // 4
        self.sizes = (2, 2, self.deep)

    def split(self, row):
        return [row % 2, (row // 2) % 2, row // 4]

    def join(self, place):
        return place[0] + 2 * (place[1] + 2 * place[2])

    def ring(self, dims, value, step=1):
        pairs = []
        for row in range(self.rows):
            for core in range(2):
                place = self.split(row)
                dim = dims[core]
                place[dim] = (place[dim] + step) % self.sizes[dim]
                pairs.append((row * 2 + core, self.join(place) * 2 + core))
        return lax.ppermute(value, AXES, pairs)

    def first(self, value):
        return self.ring((0, 1), value)

    def last(self, value):
        return self.ring((1, 0), value)

    def middle(self, value, step=1):
        return self.ring((2, 2), value, step)

    def order(self, row, core, sign, slots):
        place = self.split(row)
        k, j, i = (jnp.array(part, jnp.int32) for part in zip(*slots))
        ahead = jnp.where(core == 0, i, j)
        aside = jnp.where(core == 0, j, i)
        middle = (place[2] + sign * k + self.deep) % self.deep
        return self.join(((place[0] + ahead) % 2, (place[1] + aside) % 2, middle)).astype(jnp.int32)


def swap_cores(value):
    return lax.ppermute(value, "half", [(0, 1), (1, 0)])


class Gather:
    def __init__(self, layout, parts):
        self.layout = layout
        self.own = low(jnp.concatenate(parts))[None]
        self.levels, self.slots = [self.own], [[(0, 0, 0)]]
        self.squares, self.swapped = [], []

    @property
    def values(self):
        return (self.own, self.levels, self.squares, self.swapped)

    @values.setter
    def values(self, held):
        self.own = held[0]
        self.levels, self.squares, self.swapped = (list(item) for item in held[1:])

    def deepen(self, *steps):
        for k in steps:
            self.levels.append(self.layout.middle(self.own, k))
            self.slots.append([(k, 0, 0)])

    def join(self, begin):
        self.levels[begin:] = [jnp.concatenate(self.levels[begin:])]
        self.slots[begin:] = [sum(self.slots[begin:], [])]

    def ahead(self, number):
        item = self.levels[number]
        self.levels[number] = jnp.concatenate([item, self.layout.first(item)])
        self.slots[number] = self.slots[number] + [(k, j, 1) for k, j, _ in self.slots[number]]

    def aside(self, number):
        self.squares.append(self.layout.last(self.levels[number]))

    def swap(self, number):
        self.swapped += [swap_cores(self.levels[number]), swap_cores(self.squares[number])]

    def pieces(self):
        own = [item for pair in zip(self.levels, self.squares) for item in pair]
        return own + self.swapped

    def order(self):
        result = []
        for slots in self.slots:
            result += slots + [(k, 1, i) for k, _, i in slots]
        return result


class Scatter:
    def __init__(self, layout, kept, sent):
        self.layout = layout
        self.values = [kept, sent]
        self.plan = [self.swap, self.aside, self.ahead, self.deepen]
        self.shape = (layout.deep, 2, *kept.shape[1:])

    def advance(self):
        self.plan.pop(0)()

    def near(self, *index):
        kept, got, came = self.values[:3]
        half = (2, *self.shape)
        return (
            wide(kept.reshape(half)[(0, *index)])
            + wide(got.reshape(half)[(0, *index)])
            + wide(came.reshape(self.shape)[index])
        )

    def swap(self):
        self.values = [self.values[0], swap_cores(self.values[1])]

    def aside(self):
        kept, got = self.values
        half = self.layout.rows // 2
        self.values = [kept, got, self.layout.last(low(wide(kept[half:]) + wide(got[half:])))]

    def ahead(self):
        self.values = [*self.values, self.layout.first(low(self.near(slice(None), 1)))]

    def level(self, k):
        return self.near(k, 0) + wide(self.values[3][k])

    def deepen(self):
        got = [self.layout.middle(low(self.level(k)), k) for k in range(1, self.layout.deep)]
        self.values = [*self.values, *got]

    def result(self):
        return self.level(0) + sum(wide(item) for item in self.values[4:])


def tie(chains, *values):
    held, values = lax.optimization_barrier(([chain.values for chain in chains], values))
    for chain, item in zip(chains, held):
        chain.values = item
    return values[0] if len(values) == 1 else values


def dot(left, right):
    return jnp.dot(left, right, preferred_element_type=jnp.float32)


def dot_right(left, right):
    return lax.dot_general(
        left, right, (((1,), (1,)), ((), ())), preferred_element_type=jnp.float32
    )


def dot_left(left, right):
    return lax.dot_general(
        left, right, (((0,), (0,)), ((), ())), preferred_element_type=jnp.float32
    )


def gelu_pair(value):
    square = value * value
    bend = jnp.tanh(value * (CURVE + CURVE * CUBIC * square))
    half = 0.5 + 0.5 * bend
    slope = half + value * (0.5 - 0.5 * bend * bend) * (CURVE + 3.0 * CURVE * CUBIC * square)
    return value * half, slope


def bands(size):
    return [slice(begin, begin + TILE) for begin in range(0, size, TILE)]


class View:
    def __init__(self, ref, offset, rows, half=None):
        self.ref, self.half = ref, slice(None) if half is None else half
        self.span = slice(offset, offset + rows)
        self.rows = rows * (2 if half is None else 1)
        self.size = ref.shape[0] * self.rows

    def columns(self, band):
        return self.ref[:, self.half, self.span, band].reshape(self.size, TILE)

    def chips(self, band):
        return slice(band.start // self.rows, band.stop // self.rows)

    def band(self, band):
        return self.ref[self.chips(band), self.half, self.span, :].reshape(TILE, -1)

    def store(self, band, value):
        place = (self.chips(band), self.half, self.span)
        self.ref[place] = value.reshape(self.ref[place].shape)


def call(name, body, tables, ins, far, outs, far_outs, scratch):
    counts = [len(group) for group in (tables, ins, far, outs, far_outs, scratch)]

    def kernel(*refs):
        groups = []
        for count in counts:
            groups.append(refs[:count])
            refs = refs[count:]
        body(*groups)

    def spec(space, count):
        return [pl.BlockSpec(memory_space=space)] * count

    return pl.pallas_call(
        kernel,
        in_specs=spec(pltpu.SMEM, counts[0]) + spec(pltpu.VMEM, counts[1]) + spec(pl.ANY, counts[2]),
        out_specs=spec(pltpu.VMEM, counts[3]) + spec(pl.ANY, counts[4]),
        out_shape=[jax.ShapeDtypeStruct(*item) for item in (*outs, *far_outs)],
        scratch_shapes=scratch,
        compiler_params=pltpu.CompilerParams(vmem_limit_bytes=60 << 20),
        cost_estimate=pl.CostEstimate(flops=1, bytes_accessed=1, transcendentals=0),
        name=name,
    )(*tables, *ins, *far)


def fetch(tables, pieces, offset, target, sem):
    core, orders = tables[0][0], tables[1:3]
    count = len(pieces) // 2
    for group, order, half in ((pieces[:count], orders[0], core), (pieces[count:], orders[1], 1 - core)):
        index = 0
        for piece in group:
            for number in range(piece.shape[0]):
                pltpu.make_async_copy(
                    piece.at[number, pl.ds(offset, target.shape[2])],
                    target.at[order[index], half],
                    sem,
                ).start()
                index += 1


def fetched(target, sem):
    pltpu.make_async_copy(target, target, sem).wait()


def send_off(tables, grads, kept, sent, sems):
    core, orders = tables[0][0], tables[3:5]
    for out, order, half, sem in (
        (sent, orders[1], 1 - core, sems[1]),
        (kept, orders[0], core, sems[0]),
    ):
        for position in range(out.shape[0]):
            pltpu.make_async_copy(grads.at[order[position], half], out.at[position], sem).start()


def sent_off(kept, sent, sems):
    for out, sem in zip((kept, sent), sems):
        pltpu.make_async_copy(out, out, sem).wait()


def spread_hidden(features, weight, bias, picking, hidden, slope, outgoing):
    for band in bands(weight.size):
        value, bent = gelu_pair(dot(features[...], weight.columns(band)) + bias[:, band])
        hidden[:, band] = low(value)
        slope[:, band] = low(bent)
        outgoing[:, band] = low(dot(picking[...], low(value)))


def average(mixes, hidden, other, incoming, mean):
    own, sib, far = mixes
    for band in bands(mean.shape[1]):
        mean[:, band] = low(
            dot(own[...], hidden[:, band])
            + dot(sib[...], other[:, band])
            + dot(far[...], incoming[:, band])
        )


def lane_sums(value):
    return sum(value[:, begin : begin + 128] for begin in range(0, value.shape[1], 128))


def combine(features, mean, own, neigh, bias, gated, unit, slope, scale):
    width = features.shape[1]
    squares = 0.0
    for band in bands(width):
        pre = dot(features[...], own.columns(band)) + dot(mean[...], neigh.columns(band))
        value, bent = gelu_pair(pre + bias[:, band])
        gated[:, band] = value
        slope[:, band] = low(bent)
        squares = squares + lane_sums(value * value)
    total = jnp.sum(squares, axis=1, keepdims=True)
    scale[...] = lax.rsqrt(total * (1.0 / width) + 1e-06)
    for band in bands(width):
        unit[:, band] = low(gated[:, band] * scale[...])


def perceive(unit, first, first_bias, inner, slope):
    for band in bands(first.size):
        value, bent = gelu_pair(dot(unit[...], first.columns(band)) + first_bias[:, band])
        inner[:, band] = low(value)
        slope[:, band] = low(bent)


def conclude(inner, second, second_bias, result):
    for band in bands(second.size):
        result[:, band] = low(dot(inner[...], second.columns(band)) + second_bias[:, band])


def weight_grad(left, right, grad):
    for band in bands(left.shape[1]):
        grad.store(band, low(dot_left(left[:, band], right[...])))


def column_sums(value, sums, row):
    for band in bands(value.shape[1]):
        sums[row : row + 1, band] = jnp.sum(wide(value[:, band]), axis=0, keepdims=True)


def back_perceive(grad_result, second, slope, grad_inner):
    for band in bands(second.size):
        grad_inner[:, band] = low(dot_right(grad_result[...], second.band(band)) * wide(slope[:, band]))


def back_unit(grad_inner, first, unit, scale, slope, grad_unit, grad_pre):
    width = unit.shape[1]
    products = 0.0
    for band in bands(width):
        value = dot_right(grad_inner[...], first.band(band))
        grad_unit[:, band] = value
        products = products + lane_sums(value * wide(unit[:, band]))
    mean_dot = jnp.sum(products, axis=1, keepdims=True) * (1.0 / width)
    for band in bands(width):
        value = scale[...] * (grad_unit[:, band] - wide(unit[:, band]) * mean_dot)
        grad_pre[:, band] = low(value * wide(slope[:, band]))


def back_mean(grad_pre, neigh, mix_turned, grad_mean, far_out, sib_out):
    sib, far = mix_turned
    for band in bands(grad_mean.shape[1]):
        value = low(dot_right(grad_pre[...], neigh.band(band)))
        grad_mean[:, band] = value
        far_out[:, band] = low(dot(far[...], value))
        sib_out[:, band] = low(dot(sib[...], value))


def back_hidden(own, pick, grad_mean, sib_back, far_back, slope, grad_hidden_pre):
    for band in bands(grad_mean.shape[1]):
        value = dot(own[...], grad_mean[:, band]) + dot(pick[...], far_back[:, band])
        value = value + wide(sib_back[:, band])
        grad_hidden_pre[:, band] = low(value * wide(slope[:, band]))


def back_input(grad_self, grad_hidden_pre, weight, grad_input):
    for band in bands(grad_input.shape[1]):
        grad_input[:, band] = low(
            grad_self[:, band] + dot_right(grad_hidden_pre[...], weight.band(band))
        )


def mix_rows(neighbours, counts, spans, so_far, begin, end):
    node_count, count = neighbours.shape
    block = 16

    def kernel(index_ref, count_ref, *refs):
        outs = refs[-len(spans) :]
        index = index_ref[...]
        values = count_ref[...].astype(jnp.float32)
        shares = values / jnp.sum(values, axis=1, keepdims=True)
        for number, ((first, last), out_ref) in enumerate(zip(spans, outs)):
            column = first + lax.broadcasted_iota(jnp.int32, (block, last - first), 1)
            total = jnp.zeros((block, last - first), jnp.float32)
            far = number == len(spans) - 1
            for k in range(count // 2 if far else 0, count if far else count // 2):
                total = jnp.where(index[:, k : k + 1] == column, shares[:, k : k + 1], total)
            out_ref[...] = total.astype(LOW)

    start = begin // block
    rows = lambda n: (n + start, 0)
    shapes = [jax.ShapeDtypeStruct((node_count, last - first), LOW) for first, last in spans]
    return pl.pallas_call(
        kernel,
        grid=((end - begin) // block,),
        in_specs=[pl.BlockSpec((block, count), rows)] * 2
        + [pl.BlockSpec(memory_space=pl.ANY)] * len(so_far),
        out_specs=[pl.BlockSpec((block, last - first), rows) for first, last in spans],
        out_shape=shapes,
        input_output_aliases={2 + n: n for n in range(len(so_far))},
        cost_estimate=pl.CostEstimate(flops=1, bytes_accessed=1, transcendentals=0),
        name="mixing",
    )(neighbours, counts, *so_far)


def local(
    pin_features,
    board_features,
    node_kinds,
    neighbours,
    visit_counts,
    served_rows,
    board_proj,
    neigh_weight,
    neigh_bias,
    concat_weight,
    concat_bias,
    mlp_weight_one,
    mlp_bias_one,
    mlp_weight_two,
    mlp_bias_two,
    out_grad,
):
    slice_rows, width = pin_features.shape
    board_width = board_features.shape[1]
    peers, slots = served_rows.shape
    near_rows, far_rows = 2 * slice_rows, peers * slots
    layout = Layout(peers)
    row, core = lax.axis_index("rows"), lax.axis_index("half")
    device = row * 2 + core
    biases = jnp.concatenate([neigh_bias, concat_bias, mlp_bias_one, mlp_bias_two])
    bias_count, own_bias = biases.shape
    lane = lax.broadcasted_iota(jnp.int32, (bias_count, width), 1)
    bias_rows = jnp.where(lane // own_bias == device, jnp.tile(biases, (1, width // own_bias)), 0.0)
    halves = concat_weight[:, 0]
    proj_rows, rows, half_rows = board_proj.shape[0], neigh_weight.shape[1], halves.shape[1]

    turned = jnp.where(
        neighbours < near_rows, (neighbours + near_rows - core * slice_rows) % near_rows, neighbours
    )
    spans = ((0, slice_rows), (slice_rows, near_rows), (near_rows, near_rows + far_rows))
    mixing = []

    def mix_more(part):
        size = slice_rows // 4
        return mix_rows(turned, visit_counts, spans, mixing, part * size, (part + 1) * size)

    served = served_rows.reshape(-1)
    node = lax.broadcasted_iota(jnp.int32, (far_rows, slice_rows), 1)
    picking = (served[:, None] == node).astype(LOW)
    node = lax.broadcasted_iota(jnp.int32, (slice_rows, far_rows), 0)
    pick_turned = (served[None, :] == node).astype(LOW)
    kinds = node_kinds[:, None]

    zero = Gather(layout, [board_proj, neigh_weight[0], bias_rows])
    one = Gather(layout, [halves[0], mlp_weight_one[0], mlp_weight_two[0], neigh_weight[1]])
    two = Gather(layout, [halves[1], mlp_weight_one[1], mlp_weight_two[1]])

    slots_out = [(k, j, i) for j in range(2) for k in range(layout.deep) for i in range(2)]
    core_table = [core[None].astype(jnp.int32)]
    out_tables = [layout.order(row, which, 1, slots_out) for which in (core, 1 - core)]

    def tables(chain=None):
        slots = slots_out if chain is None else chain.order()
        order = [layout.order(row, which, -1, slots) for which in (core, 1 - core)]
        return core_table + order + out_tables

    nodes_low = ((slice_rows, width), LOW)
    nodes_wide = ((slice_rows, width), jnp.float32)
    far_low = ((far_rows, width), LOW)
    column = ((slice_rows, 1), jnp.float32)
    sum_rows = ((8, width), jnp.float32)
    blocks = lambda count: pltpu.VMEM((layout.rows, 2, count, width), LOW)
    own_nodes = pltpu.VMEM(*nodes_low)
    own_wide = pltpu.VMEM(*nodes_wide)
    own_column = pltpu.VMEM(*column)
    dma = pltpu.SemaphoreType.DMA

    def leaving(count):
        return [((layout.rows, count, width), LOW)] * 2

    def exchange(outgoing):
        far = lax.all_to_all(
            outgoing.reshape(peers, slots, width), "rows", split_axis=0, concat_axis=0, tiled=True
        )
        return far.reshape(far_rows, width)

    depths = range(1, layout.deep)
    zero.deepen(*depths)
    one.ahead(0)
    mixing = tie([zero, one], mix_more(0))
    zero.join(0)
    zero.ahead(0)
    one.deepen(*depths[:1])
    one.aside(0)
    mixing = tie([zero, one], mix_more(1))
    zero.aside(0)
    two.ahead(0)
    one.deepen(*depths[1:2])
    mixing = tie([zero, one, two], mix_more(2))
    zero.swap(0)
    two.aside(0)
    one.deepen(*depths[2:])
    two.deepen(*depths[:1])
    mixing = tie([zero, one, two], mix_more(3))
    one.join(1)
    bias_full = sum(jnp.sum(wide(item[:, proj_rows + rows :]), 0) for item in zero.pieces())

    def hidden_body(tables, ins, pieces, outs, _, scratch):
        pin, board, kinds, bias, picking = ins
        features, hidden, slope, outgoing, proj_out = outs
        weights, sems = scratch
        fetch(tables, pieces, 0, weights, sems.at[0])
        fetched(weights, sems.at[0])
        proj, weight = View(weights, 0, proj_rows), View(weights, proj_rows, rows)
        for band in bands(width):
            projected = dot(board[...], proj.columns(band))
            features[:, band] = low(jnp.where(kinds[...] == 1, wide(pin[:, band]), projected))
        for band in bands(board_width):
            proj_out[band, :] = proj.band(band)
        spread_hidden(features, weight, bias.at[0:1], picking, hidden, slope, outgoing)

    one.ahead(1)
    one.swap(0)
    two.deepen(*depths[1:])
    features, hidden, hidden_slope, outgoing, proj_full = tie(
        [one, two],
        *call(
            "hidden",
            hidden_body,
            tables(zero),
            [pin_features, board_features, kinds, bias_full, picking],
            zero.pieces(),
            [nodes_low] * 3 + [far_low, ((board_width, width), LOW)],
            [],
            [blocks(proj_rows + rows), dma((1,))],
        ),
    )
    incoming, other = exchange(outgoing), swap_cores(hidden)
    one.aside(1)
    two.swap(0)
    incoming, other = tie([one, two], incoming, other)
    two.join(1)
    one.swap(1)
    two.ahead(1)
    tie([one, two])

    def middle_body(tables, ins, pieces, outs, _, scratch):
        mixes, (hidden, other, incoming, features, bias, picking) = ins[:3], ins[3:]
        mean, unit, slope_pre, scale, inner, slope_inner, result, ahead, slope_ahead, outgoing = outs
        both, rest, gated, sems = scratch
        fetch(tables, pieces, 0, both, sems.at[0])
        fetch(tables, pieces, half_rows, rest, sems.at[1])
        first, second, weight = (View(rest, n * rows, rows) for n in range(3))
        own, neigh = (View(both, 0, half_rows, half) for half in range(2))
        average(mixes, hidden, other, incoming, mean)
        fetched(both, sems.at[0])
        combine(features, mean, own, neigh, bias.at[2:3], gated, unit, slope_pre, scale)
        fetched(rest, sems.at[1])
        perceive(unit, first, bias.at[4:5], inner, slope_inner)
        conclude(inner, second, bias.at[6:7], result)
        spread_hidden(result, weight, bias.at[1:2], picking, ahead, slope_ahead, outgoing)

    two.aside(1)
    (
        mean_zero,
        unit,
        slope_pre,
        scale,
        inner,
        slope_inner,
        features_one,
        hidden_one,
        hidden_slope_one,
        outgoing,
    ) = tie(
        [two],
        *call(
            "middle",
            middle_body,
            tables(one),
            [*mixing, hidden, other, incoming, features, bias_full, picking],
            one.pieces(),
            [nodes_low] * 3 + [column] + [nodes_low] * 5 + [far_low],
            [],
            [blocks(half_rows), blocks(3 * rows), own_wide, dma((2,))],
        ),
    )
    incoming, other = exchange(outgoing), swap_cores(hidden_one)
    two.swap(1)
    mix_turned = [item.T for item in mixing]
    incoming, other, mix_turned = tie([two], incoming, other, mix_turned)

    def top_body(tables, ins, pieces, outs, leave, scratch):
        mixes, (hidden, other, incoming, features, bias, grad_result) = ins[:3], ins[3:]
        mean, result, unit, slope_pre, scale, grad_inner, sums = outs
        weights, grads, gated, inner, slope_inner, sems = scratch
        fetch(tables, pieces, 0, weights, sems.at[0])
        own, neigh = (View(weights, 0, half_rows, half) for half in range(2))
        first, second = View(weights, half_rows, rows), View(weights, half_rows + rows, rows)
        average(mixes, hidden, other, incoming, mean)
        fetched(weights, sems.at[0])
        combine(features, mean, own, neigh, bias.at[3:4], gated, unit, slope_pre, scale)
        perceive(unit, first, bias.at[5:6], inner, slope_inner)
        weight_grad(inner, grad_result, View(grads, 0, rows))
        back_perceive(grad_result, second, slope_inner, grad_inner)
        weight_grad(unit, grad_inner, View(grads, rows, rows))
        send_off(tables, grads, *leave, (sems.at[1], sems.at[2]))
        conclude(inner, second, bias.at[7:8], result)
        sums[...] = jnp.zeros_like(sums)
        column_sums(grad_result, sums, 0)
        column_sums(grad_inner, sums, 1)
        sent_off(*leave, (sems.at[1], sems.at[2]))

    mean_one, embeddings, unit_one, slope_pre_one, scale_one, grad_inner, sums_one, kept, sent = call(
        "top",
        top_body,
        tables(two),
        [*mixing, hidden_one, other, incoming, features_one, bias_full, out_grad],
        two.pieces(),
        [nodes_low] * 4 + [column, nodes_low, sum_rows],
        leaving(2 * rows),
        [blocks(half_rows + 2 * rows), blocks(2 * rows), own_wide, own_nodes, own_nodes, dma((3,))],
    )
    five = Scatter(layout, kept, sent)

    def norm_body(tables, ins, pieces, outs, _, scratch):
        grad_inner, unit, scale, slope_pre, *mix_turned = ins
        grad_pre, grad_mean, far_out, sib_out, sums = outs
        weights, grad_unit, sems = scratch
        fetch(tables, pieces, 0, weights, sems.at[0])
        fetched(weights, sems.at[0])
        first = View(weights, half_rows, rows)
        back_unit(grad_inner, first, unit, scale, slope_pre, grad_unit, grad_pre)
        neigh = View(weights, 0, half_rows, 1)
        back_mean(grad_pre, neigh, mix_turned, grad_mean, far_out, sib_out)
        sums[...] = jnp.zeros_like(sums)
        column_sums(grad_pre, sums, 0)

    def norm(name, chain, *ins):
        return call(
            name,
            norm_body,
            tables(chain),
            [*ins, *mix_turned[1:]],
            chain.pieces(),
            [nodes_low] * 2 + [far_low, nodes_low, sum_rows],
            [],
            [blocks(half_rows + rows), own_wide, dma((1,))],
        )

    def sides(name, chain, features, mean, grad_pre):
        def body(tables, ins, pieces, outs, leave, scratch):
            features, mean, grad_pre = ins
            both, grads, sems = scratch
            fetch(tables, pieces, 0, both, sems.at[0])
            weight_grad(features, grad_pre, View(grads, 0, half_rows, 0))
            weight_grad(mean, grad_pre, View(grads, 0, half_rows, 1))
            send_off(tables, grads, *leave, (sems.at[1], sems.at[2]))
            fetched(both, sems.at[0])
            own = View(both, 0, half_rows, 0)
            for band in bands(width):
                outs[0][:, band] = dot_right(grad_pre[...], own.band(band))
            sent_off(*leave, (sems.at[1], sems.at[2]))

        return call(
            name,
            body,
            tables(chain),
            [features, mean, grad_pre],
            chain.pieces(),
            [nodes_wide],
            leaving(half_rows),
            [blocks(half_rows), blocks(half_rows), dma((3,))],
        )

    five.advance()
    grad_pre, grad_mean, far_out, sib_out, sums_pre_one = tie(
        [five], *norm("norm1", two, grad_inner, unit_one, scale_one, slope_pre_one)
    )
    five.advance()
    far_back, sib_back = exchange(far_out), swap_cores(sib_out)
    grad_self, kept, sent = sides("sides1", two, features_one, mean_one, grad_pre)
    far_back, sib_back, grad_self, kept, sent = tie([five], far_back, sib_back, grad_self, kept, sent)
    six = Scatter(layout, kept, sent)

    def bridge_body(tables, ins, pieces, outs, leave, scratch):
        own, pick, grad_mean, sib_back, far_back, slope_hidden, features, grad_self = ins[:8]
        inner, unit, slope_inner = ins[8:]
        grad_inner, sums = outs
        weights, grads, grad_hidden_pre, grad_input, sems = scratch
        fetch(tables, pieces, half_rows + rows, weights, sems.at[0])
        back_hidden(own, pick, grad_mean, sib_back, far_back, slope_hidden, grad_hidden_pre)
        weight_grad(features, grad_hidden_pre, View(grads, 0, rows))
        fetched(weights, sems.at[0])
        back_input(grad_self, grad_hidden_pre, View(weights, rows, rows), grad_input)
        weight_grad(inner, grad_input, View(grads, rows, rows))
        back_perceive(grad_input, View(weights, 0, rows), slope_inner, grad_inner)
        weight_grad(unit, grad_inner, View(grads, 2 * rows, rows))
        send_off(tables, grads, *leave, (sems.at[1], sems.at[2]))
        sums[...] = jnp.zeros_like(sums)
        column_sums(grad_hidden_pre, sums, 0)
        column_sums(grad_input, sums, 1)
        column_sums(grad_inner, sums, 2)
        sent_off(*leave, (sems.at[1], sems.at[2]))

    five.advance()
    six.advance()
    grad_inner, sums_zero, kept, sent = tie(
        [five, six],
        *call(
            "bridge",
            bridge_body,
            tables(one),
            [mix_turned[0], pick_turned, grad_mean, sib_back, far_back, hidden_slope_one]
            + [features_one, grad_self, inner, unit, slope_inner],
            one.pieces(),
            [nodes_low, sum_rows],
            leaving(3 * rows),
            [blocks(2 * rows), blocks(3 * rows), own_nodes, own_nodes, dma((3,))],
        ),
    )
    seven = Scatter(layout, kept, sent)
    five.advance()
    six.advance()
    seven.advance()
    grad_pre, grad_mean, far_out, sib_out, sums_pre_zero = tie(
        [five, six, seven], *norm("norm0", one, grad_inner, unit, scale, slope_pre)
    )
    six.advance()
    seven.advance()
    far_back, sib_back = exchange(far_out), swap_cores(sib_out)
    grad_self, kept, sent = sides("sides0", one, features, mean_zero, grad_pre)
    far_back, sib_back, grad_self, kept, sent = tie(
        [six, seven], far_back, sib_back, grad_self, kept, sent
    )
    eight = Scatter(layout, kept, sent)

    def bottom_body(tables, ins, pieces, outs, leave, scratch):
        own, pick, grad_mean, sib_back, far_back, slope_hidden, features, grad_self = ins[:8]
        board, kinds, sums_one, pre_one, sums_zero, pre_zero = ins[8:]
        (grad_input,) = outs
        weights, grads, grad_hidden_pre, grad_board, sums, sems = scratch
        fetch(tables, pieces, proj_rows, weights, sems.at[0])
        back_hidden(own, pick, grad_mean, sib_back, far_back, slope_hidden, grad_hidden_pre)
        weight_grad(features, grad_hidden_pre, View(grads, 0, rows))
        column_sums(grad_hidden_pre, sums, 0)
        fetched(weights, sems.at[0])
        back_input(grad_self, grad_hidden_pre, View(weights, 0, rows), grad_input)
        for band in bands(width):
            grad_board[:, band] = low(jnp.where(kinds[...] == 1, 0.0, wide(grad_input[:, band])))
        weight_grad(board, grad_board, View(grads, rows, proj_rows))
        totals = [sums[0:1, :], sums_zero[0:1, :], pre_zero[0:1, :], pre_one[0:1, :]]
        totals += [sums_zero[2:3, :], sums_one[1:2, :], sums_zero[1:2, :], sums_one[0:1, :]]
        totals = low(jnp.concatenate([*totals, jnp.zeros((8, width), jnp.float32)]))
        for chip in range(layout.rows):
            for half in range(2):
                grads[chip, half, rows + proj_rows :, :] = totals
        send_off(tables, grads, *leave, (sems.at[1], sems.at[2]))
        sent_off(*leave, (sems.at[1], sems.at[2]))

    six.advance()
    seven.advance()
    eight.advance()
    grad_input, kept, sent = tie(
        [six, seven, eight],
        *call(
            "bottom",
            bottom_body,
            tables(zero),
            [mix_turned[0], pick_turned, grad_mean, sib_back, far_back, hidden_slope, features]
            + [grad_self, board_features, kinds, sums_one, sums_pre_one, sums_zero, sums_pre_zero],
            zero.pieces(),
            [nodes_low],
            leaving(rows + proj_rows + 16),
            [blocks(rows), blocks(rows + proj_rows + 16), own_nodes, own_nodes]
            + [pltpu.VMEM(*sum_rows), dma((3,))],
        ),
    )
    nine = Scatter(layout, kept, sent)
    chains = [five, six, seven, eight, nine]
    while any(chain.plan for chain in chains):
        moving = [chain for chain in chains if chain.plan]
        for chain in moving:
            chain.advance()
        tie(moving)
    is_pin = kinds == 1
    pin_grad = jnp.where(is_pin, wide(grad_input), 0.0)
    grad_board = jnp.where(is_pin, jnp.zeros_like(grad_input), grad_input)
    board_grad = dot_right(grad_board, proj_full)

    five, six, seven, eight, nine = (chain.result() for chain in chains)
    bias_sums = nine[rows + proj_rows :][:bias_count]
    bias_sums = lax.dynamic_slice_in_dim(bias_sums, device * own_bias, own_bias, 1)
    bias_sums = bias_sums.reshape(4, -1, own_bias)
    return (
        embeddings,
        pin_grad,
        board_grad,
        nine[rows : rows + proj_rows],
        jnp.stack([nine[:rows], seven[:rows]]),
        bias_sums[0],
        jnp.stack([eight, six])[:, None],
        bias_sums[1],
        jnp.stack([seven[2 * rows :], five[rows:]]),
        bias_sums[2],
        jnp.stack([seven[rows : 2 * rows], five[:rows]]),
        bias_sums[3],
    )


def solution(mesh):
    nodes = P(("rows", "half"), None)
    weight = P(None, ("rows", "half"), None)
    bias = P(None, ("rows", "half"))
    concat = P(None, "half", "rows", None)
    placed = (nodes, nodes, P(("rows", "half")), nodes, nodes, nodes, nodes)
    placed += (weight, bias, concat, bias, weight, bias, weight, bias, nodes)
    results = (nodes, nodes, nodes, nodes) + (weight, bias, concat, bias, weight, bias, weight, bias)

    def whole(*args):
        devices = mesh.shape["rows"] * mesh.shape["half"]
        shards = (args[6].shape[0] // devices, args[7].shape[1] // devices)
        fits = mesh.shape["rows"] % 4 == 0 and not any(count % 16 for count in shards)
        return jax.shard_map(
            local if fits else plain,
            mesh=mesh,
            in_specs=placed,
            out_specs=results,
            check_vma=False,
        )(*args)

    return whole
```

```python
import jax
import jax.numpy as jnp
from jax import lax
from jax.experimental import pallas as pl
from jax.experimental.pallas import tpu as pltpu
from jax.sharding import PartitionSpec as P

LOW = jnp.bfloat16
AXES = ("rows", "half")
CURVE = 0.7978845608028654
CUBIC = 0.044715
TILE = 256


def activate(value):
    return jax.nn.gelu(value, approximate=True)


def unit_map(value):
    scaled = activate(value)
    return scaled * lax.rsqrt(jnp.mean(scaled * scaled, axis=-1, keepdims=True) + 1e-06)


def matmul(left, right):
    return jnp.dot(left, right, preferred_element_type=jnp.float32)


def column_sum(value):
    return jnp.sum(value.astype(jnp.float32), axis=0)


def fetch_shared(
    neigh_weight, neigh_bias, concat_bias, weight_one, bias_one, weight_two, bias_two, board_proj
):
    return (
        lax.all_gather(neigh_weight, ("rows", "half"), axis=1, tiled=True),
        lax.all_gather(neigh_bias, ("rows", "half"), axis=1, tiled=True),
        lax.all_gather(concat_bias, ("rows", "half"), axis=1, tiled=True),
        lax.all_gather(weight_one, ("rows", "half"), axis=1, tiled=True),
        lax.all_gather(bias_one, ("rows", "half"), axis=1, tiled=True),
        lax.all_gather(weight_two, ("rows", "half"), axis=1, tiled=True),
        lax.all_gather(bias_two, ("rows", "half"), axis=1, tiled=True),
        lax.all_gather(board_proj, ("rows", "half"), axis=0, tiled=True),
    )


def fetch_half(own_half):
    return lax.all_gather(own_half, "rows", axis=1, tiled=True)


def refetch_shared(
    neigh_weight, neigh_bias, concat_bias, weight_one, bias_one, weight_two, bias_two, board_proj
):
    return (
        lax.all_gather(neigh_weight, ("rows", "half"), axis=1, tiled=True),
        lax.all_gather(neigh_bias, ("rows", "half"), axis=1, tiled=True),
        lax.all_gather(concat_bias, ("rows", "half"), axis=1, tiled=True),
        lax.all_gather(weight_one, ("rows", "half"), axis=1, tiled=True),
        lax.all_gather(bias_one, ("rows", "half"), axis=1, tiled=True),
        lax.all_gather(weight_two, ("rows", "half"), axis=1, tiled=True),
        lax.all_gather(bias_two, ("rows", "half"), axis=1, tiled=True),
        lax.all_gather(board_proj, ("rows", "half"), axis=0, tiled=True),
    )


def refetch_half(own_half):
    return lax.all_gather(own_half, "rows", axis=1, tiled=True)


def plain(
    pin_features,
    board_features,
    node_kinds,
    neighbours,
    visit_counts,
    served_rows,
    board_proj,
    neigh_weight,
    neigh_bias,
    concat_weight,
    concat_bias,
    mlp_weight_one,
    mlp_bias_one,
    mlp_weight_two,
    mlp_bias_two,
    out_grad,
):
    slice_rows, feature_width = pin_features.shape
    layer_count = neigh_weight.shape[0]
    peer_count, slot_count = served_rows.shape
    chip_rows = 2 * slice_rows
    table_rows = chip_rows + peer_count * slot_count
    counts = visit_counts.astype(jnp.float32)
    shares = (counts / jnp.sum(counts, axis=1, keepdims=True)).astype(jnp.bfloat16)
    positions = jnp.broadcast_to(jnp.arange(slice_rows, dtype=jnp.int32)[:, None], neighbours.shape)
    mixing = jnp.zeros((slice_rows, table_rows), jnp.bfloat16).at[positions, neighbours].set(shares)
    served_flat = served_rows.reshape(-1)
    is_pin = (node_kinds == 1)[:, None]
    to_low = jnp.bfloat16
    master_pieces = (
        neigh_weight.astype(to_low),
        neigh_bias.astype(to_low),
        concat_bias.astype(to_low),
        mlp_weight_one.astype(to_low),
        mlp_bias_one.astype(to_low),
        mlp_weight_two.astype(to_low),
        mlp_bias_two.astype(to_low),
        board_proj.astype(to_low),
    )
    own_half = concat_weight[:, 0].astype(to_low)
    shared_full = fetch_shared(*master_pieces)
    half_full = fetch_half(own_half)
    (
        neigh_full,
        nbias_full,
        cbias_full,
        first_full,
        fbias_full,
        second_full,
        sbias_full,
        proj_full,
    ) = shared_full
    projected = matmul(board_features, proj_full)
    features = jnp.where(is_pin, pin_features.astype(jnp.float32), projected).astype(to_low)
    saved = []
    result = None
    for layer_index in range(layer_count):
        hidden_pre = matmul(features, neigh_full[layer_index]) + nbias_full[layer_index].astype(
            jnp.float32
        )
        hidden_full, hidden_pull = jax.vjp(activate, hidden_pre)
        hidden = hidden_full.astype(to_low)
        chip_hidden = lax.all_gather(hidden, "half", axis=0, tiled=True)
        outgoing = hidden[served_rows]
        incoming = lax.all_to_all(outgoing, "rows", split_axis=0, concat_axis=0, tiled=True)
        lookup_table = jnp.concatenate([chip_hidden, incoming.reshape(-1, feature_width)], axis=0)
        neigh_mean = matmul(mixing, lookup_table).astype(to_low)
        paired = lax.all_to_all(
            jnp.stack([features, neigh_mean]), "half", split_axis=0, concat_axis=1, tiled=True
        )[0]
        partial_value = matmul(paired, half_full[layer_index])
        pre_sum = lax.psum_scatter(
            partial_value.astype(jnp.bfloat16), "half", scatter_dimension=0, tiled=True
        ).astype(jnp.float32) + cbias_full[layer_index].astype(jnp.float32)
        unit_full, unit_pull = jax.vjp(unit_map, pre_sum)
        unit_rows = unit_full.astype(to_low)
        inner_pre = matmul(unit_rows, first_full[layer_index]) + fbias_full[layer_index].astype(
            jnp.float32
        )
        inner_full, inner_pull = jax.vjp(activate, inner_pre)
        inner_act = inner_full.astype(to_low)
        result = matmul(inner_act, second_full[layer_index]) + sbias_full[layer_index].astype(
            jnp.float32
        )
        saved.append((features, hidden_pull, paired, unit_rows, unit_pull, inner_act, inner_pull))
        features = result.astype(to_low)
    embeddings = result.astype(to_low)
    (
        neigh_full,
        nbias_full,
        cbias_full,
        first_full,
        fbias_full,
        second_full,
        sbias_full,
        proj_full,
    ) = refetch_shared(*master_pieces)
    half_full = refetch_half(own_half)
    grad_result = out_grad
    grads_neigh = [None] * layer_count
    grads_nbias = [None] * layer_count
    grads_half = [None] * layer_count
    grads_cbias = [None] * layer_count
    grads_first = [None] * layer_count
    grads_fbias = [None] * layer_count
    grads_second = [None] * layer_count
    grads_sbias = [None] * layer_count
    grad_input = None
    for layer_index in reversed(range(layer_count)):
        features, hidden_pull, paired, unit_rows, unit_pull, inner_act, inner_pull = saved[
            layer_index
        ]
        grads_second[layer_index] = matmul(inner_act.T, grad_result)
        grads_sbias[layer_index] = column_sum(grad_result)
        grad_inner = inner_pull(matmul(grad_result, second_full[layer_index].T))[0].astype(to_low)
        grads_first[layer_index] = matmul(unit_rows.T, grad_inner)
        grads_fbias[layer_index] = column_sum(grad_inner)
        grad_pre = unit_pull(matmul(grad_inner, first_full[layer_index].T))[0].astype(to_low)
        grads_cbias[layer_index] = column_sum(grad_pre)
        grad_pre_full = lax.all_gather(grad_pre, "half", axis=0, tiled=True)
        grads_half[layer_index] = matmul(paired.T, grad_pre_full)
        grad_paired = matmul(grad_pre_full, half_full[layer_index].T)
        returned = lax.all_to_all(
            grad_paired[None].astype(jnp.bfloat16), "half", split_axis=1, concat_axis=0, tiled=True
        ).astype(jnp.float32)
        grad_self = returned[0]
        grad_mean = returned[1].astype(to_low)
        grad_table = matmul(mixing.T, grad_mean)
        grad_chip = lax.psum_scatter(
            grad_table[:chip_rows].astype(jnp.bfloat16), "half", scatter_dimension=0, tiled=True
        ).astype(jnp.float32)
        grad_far = lax.all_to_all(
            grad_table[chip_rows:]
            .reshape(peer_count, slot_count, feature_width)
            .astype(jnp.bfloat16),
            "rows",
            split_axis=0,
            concat_axis=0,
            tiled=True,
        ).astype(jnp.float32)
        grad_hidden = grad_chip.at[served_flat].add(grad_far.reshape(-1, feature_width))
        grad_hidden_pre = hidden_pull(grad_hidden)[0].astype(to_low)
        grads_neigh[layer_index] = matmul(features.T, grad_hidden_pre)
        grads_nbias[layer_index] = column_sum(grad_hidden_pre)
        grad_input = (grad_self + matmul(grad_hidden_pre, neigh_full[layer_index].T)).astype(to_low)
        grad_result = grad_input
    pin_grad = jnp.where(is_pin, grad_input.astype(jnp.float32), 0.0)
    grad_board = jnp.where(is_pin, jnp.zeros_like(grad_input), grad_input)
    board_grad = matmul(grad_board, proj_full.T)
    proj_grad = matmul(board_features.T, grad_board)
    summed = (
        lax.psum_scatter(jnp.stack(grads_neigh), ("rows", "half"), scatter_dimension=1, tiled=True),
        lax.psum_scatter(jnp.stack(grads_nbias), ("rows", "half"), scatter_dimension=1, tiled=True),
        lax.psum_scatter(jnp.stack(grads_cbias), ("rows", "half"), scatter_dimension=1, tiled=True),
        lax.psum_scatter(jnp.stack(grads_first), ("rows", "half"), scatter_dimension=1, tiled=True),
        lax.psum_scatter(jnp.stack(grads_fbias), ("rows", "half"), scatter_dimension=1, tiled=True),
        lax.psum_scatter(
            jnp.stack(grads_second), ("rows", "half"), scatter_dimension=1, tiled=True
        ),
        lax.psum_scatter(jnp.stack(grads_sbias), ("rows", "half"), scatter_dimension=1, tiled=True),
        lax.psum_scatter(proj_grad, ("rows", "half"), scatter_dimension=0, tiled=True),
    )
    half_summed = lax.psum_scatter(jnp.stack(grads_half), "rows", scatter_dimension=1, tiled=True)
    (
        neigh_grad,
        nbias_grad,
        cbias_grad,
        first_grad,
        fbias_grad,
        second_grad,
        sbias_grad,
        board_proj_grad,
    ) = summed
    return (
        embeddings,
        pin_grad,
        board_grad,
        board_proj_grad,
        neigh_grad,
        nbias_grad,
        half_summed[:, None],
        cbias_grad,
        first_grad,
        fbias_grad,
        second_grad,
        sbias_grad,
    )


def low(value):
    return value.astype(LOW)


def wide(value):
    return value.astype(jnp.float32)


class Layout:
    def __init__(self, row_count):
        self.rows = row_count
        self.deep = row_count // 4
        self.sizes = (2, 2, self.deep)

    def split(self, row):
        return [row % 2, (row // 2) % 2, row // 4]

    def join(self, place):
        return place[0] + 2 * (place[1] + 2 * place[2])

    def ring(self, dims, value, step=1):
        pairs = []
        for row in range(self.rows):
            for core in range(2):
                place = self.split(row)
                dim = dims[core]
                place[dim] = (place[dim] + step) % self.sizes[dim]
                pairs.append((row * 2 + core, self.join(place) * 2 + core))
        return lax.ppermute(value, AXES, pairs)

    def first(self, value):
        return self.ring((0, 1), value)

    def last(self, value):
        return self.ring((1, 0), value)

    def middle(self, value, step=1):
        return self.ring((2, 2), value, step)

    def orders(self, row, core, slots_in, slots_out):
        slots = jnp.array([slots_in, slots_in, slots_in, slots_out, slots_out], jnp.int32)
        line = lax.broadcasted_iota(jnp.int32, slots.shape[:2], 0)
        whose = jnp.where(line % 2 == 1, core, 1 - core)
        sign = jnp.where(line < 3, -1, 1)
        place = self.split(row)
        k, j, i = (slots[:, :, part] for part in range(3))
        ahead, aside = jnp.where(whose == 0, i, j), jnp.where(whose == 0, j, i)
        middle = (place[2] + sign * k + self.deep) % self.deep
        order = self.join(((place[0] + ahead) % 2, (place[1] + aside) % 2, middle))
        return jnp.where(line == 0, core, order).astype(jnp.int32)


def swap_cores(value):
    return lax.ppermute(value, "half", [(0, 1), (1, 0)])


class Gather:
    def __init__(self, layout, parts):
        self.layout = layout
        self.own = low(jnp.concatenate(parts))[None]
        self.levels, self.slots = [self.own], [[(0, 0, 0)]]
        self.squares, self.near, self.far = [], [], []

    @property
    def values(self):
        return (self.own, self.levels, self.squares, self.near, self.far)

    @values.setter
    def values(self, held):
        self.own = held[0]
        self.levels, self.squares, self.near, self.far = (list(item) for item in held[1:])

    def deepen(self, *steps):
        for k in steps:
            self.levels.append(self.layout.middle(self.own, k))
            self.slots.append([(k, 0, 0)])

    def join(self, begin):
        self.levels[begin:] = [jnp.concatenate(self.levels[begin:])]
        self.slots[begin:] = [sum(self.slots[begin:], [])]

    def ahead(self, number):
        item = self.levels[number]
        self.levels[number] = jnp.concatenate([item, self.layout.first(item)])
        self.slots[number] = self.slots[number] + [(k, j, 1) for k, j, _ in self.slots[number]]

    def aside(self, number):
        self.squares.append(self.layout.last(self.levels[number]))

    def swap(self, number):
        self.near.append(swap_cores(self.levels[number]))

    def swap_far(self, number):
        self.far.append(swap_cores(self.squares[number]))

    def pieces(self):
        own = [item for pair in zip(self.levels, self.squares) for item in pair]
        return own + [item for pair in zip(self.near, self.far) for item in pair]

    def order(self):
        result = []
        for slots in self.slots:
            result += slots + [(k, 1, i) for k, _, i in slots]
        return result


class Scatter:
    def __init__(self, layout, kept, sent):
        self.layout = layout
        self.values = [kept, sent]
        self.plan = [self.swap, self.aside, self.ahead, self.deepen]
        self.shape = (layout.deep, 2, *kept.shape[1:])

    def advance(self):
        self.plan.pop(0)()

    def near(self, *index):
        kept, got, came = self.values[:3]
        half = (2, *self.shape)
        return (
            wide(kept.reshape(half)[(0, *index)])
            + wide(got.reshape(half)[(0, *index)])
            + wide(came.reshape(self.shape)[index])
        )

    def swap(self):
        self.values = [self.values[0], swap_cores(self.values[1])]

    def aside(self):
        kept, got = self.values
        half = self.layout.rows // 2
        self.values = [kept, got, self.layout.last(low(wide(kept[half:]) + wide(got[half:])))]

    def ahead(self):
        self.values = [*self.values, self.layout.first(low(self.near(slice(None), 1)))]

    def level(self, k):
        return self.near(k, 0) + wide(self.values[3][k])

    def deepen(self):
        got = [self.layout.middle(low(self.level(k)), k) for k in range(1, self.layout.deep)]
        self.values = [*self.values, *got]

    def result(self):
        return self.level(0) + sum(wide(item) for item in self.values[4:])


def tie(chains, *values):
    held, values = lax.optimization_barrier(([chain.values for chain in chains], values))
    for chain, item in zip(chains, held):
        chain.values = item
    return values[0] if len(values) == 1 else values


def dot(left, right):
    return jnp.dot(left, right, preferred_element_type=jnp.float32)


def dot_right(left, right):
    return lax.dot_general(
        left, right, (((1,), (1,)), ((), ())), preferred_element_type=jnp.float32
    )


def dot_left(left, right):
    return lax.dot_general(
        left, right, (((0,), (0,)), ((), ())), preferred_element_type=jnp.float32
    )


def gelu_pair(value):
    square = value * value
    bend = jnp.tanh(value * (CURVE + CURVE * CUBIC * square))
    half = 0.5 + 0.5 * bend
    slope = half + value * (0.5 - 0.5 * bend * bend) * (CURVE + 3.0 * CURVE * CUBIC * square)
    return value * half, slope


def bands(size):
    return [slice(begin, begin + TILE) for begin in range(0, size, TILE)]


class View:
    def __init__(self, ref, offset, rows, half=None):
        self.ref, self.half = ref, slice(None) if half is None else half
        self.span = slice(offset, offset + rows)
        self.rows = rows * (2 if half is None else 1)
        self.size = ref.shape[0] * self.rows

    def columns(self, band):
        return self.ref[:, self.half, self.span, band].reshape(self.size, TILE)

    def chips(self, band):
        return slice(band.start // self.rows, band.stop // self.rows)

    def band(self, band):
        return self.ref[self.chips(band), self.half, self.span, :].reshape(TILE, -1)

    def store(self, band, value):
        place = (self.chips(band), self.half, self.span)
        self.ref[place] = value.reshape(self.ref[place].shape)


def call(name, body, tables, ins, far, outs, far_outs, scratch):
    counts = [len(group) for group in (tables, ins, far, outs, far_outs, scratch)]

    def kernel(*refs):
        groups = []
        for count in counts:
            groups.append(refs[:count])
            refs = refs[count:]
        body(*groups)

    def spec(space, count):
        return [pl.BlockSpec(memory_space=space)] * count

    return pl.pallas_call(
        kernel,
        in_specs=spec(pltpu.SMEM, counts[0]) + spec(pltpu.VMEM, counts[1]) + spec(pl.ANY, counts[2]),
        out_specs=spec(pltpu.VMEM, counts[3]) + spec(pl.ANY, counts[4]),
        out_shape=[jax.ShapeDtypeStruct(*item) for item in (*outs, *far_outs)],
        scratch_shapes=scratch,
        compiler_params=pltpu.CompilerParams(vmem_limit_bytes=60 << 20),
        cost_estimate=pl.CostEstimate(flops=1, bytes_accessed=1, transcendentals=0),
        name=name,
    )(*tables, *ins, *far)


def fetch(tables, pieces, offset, target, sem):
    (table,) = tables
    core = table[0, 0]
    count = len(pieces) // 2
    for group, line, half in ((pieces[:count], 1, core), (pieces[count:], 2, 1 - core)):
        index = 0
        for piece in group:
            for number in range(piece.shape[0]):
                pltpu.make_async_copy(
                    piece.at[number, pl.ds(offset, target.shape[2])],
                    target.at[table[line, index], half],
                    sem,
                ).start()
                index += 1


def fetched(target, sem):
    pltpu.make_async_copy(target, target, sem).wait()


def send_off(tables, grads, kept, sent, sems):
    (table,) = tables
    core = table[0, 0]
    for out, line, half, sem in (
        (sent, 4, 1 - core, sems[1]),
        (kept, 3, core, sems[0]),
    ):
        for position in range(out.shape[0]):
            pltpu.make_async_copy(grads.at[table[line, position], half], out.at[position], sem).start()


def sent_off(kept, sent, sems):
    for out, sem in zip((kept, sent), sems):
        pltpu.make_async_copy(out, out, sem).wait()


def spread_hidden(features, weight, bias, picking, hidden, slope, outgoing):
    for band in bands(weight.size):
        value, bent = gelu_pair(dot(features[...], weight.columns(band)) + bias[:, band])
        hidden[:, band] = low(value)
        slope[:, band] = low(bent)
        outgoing[:, band] = low(dot(picking[...], low(value)))


def average(mixes, hidden, other, incoming, mean):
    own, sib, far = mixes
    for band in bands(mean.shape[1]):
        mean[:, band] = low(
            dot(own[...], hidden[:, band])
            + dot(sib[...], other[:, band])
            + dot(far[...], incoming[:, band])
        )


def lane_sums(value):
    return sum(value[:, begin : begin + 128] for begin in range(0, value.shape[1], 128))


def combine(features, mean, own, neigh, bias, gated, unit, slope, scale):
    width = features.shape[1]
    squares = 0.0
    for band in bands(width):
        pre = dot(features[...], own.columns(band)) + dot(mean[...], neigh.columns(band))
        value, bent = gelu_pair(pre + bias[:, band])
        gated[:, band] = value
        slope[:, band] = low(bent)
        squares = squares + lane_sums(value * value)
    total = jnp.sum(squares, axis=1, keepdims=True)
    scale[...] = lax.rsqrt(total * (1.0 / width) + 1e-06)
    for band in bands(width):
        unit[:, band] = low(gated[:, band] * scale[...])


def perceive(unit, first, first_bias, inner, slope):
    for band in bands(first.size):
        value, bent = gelu_pair(dot(unit[...], first.columns(band)) + first_bias[:, band])
        inner[:, band] = low(value)
        slope[:, band] = low(bent)


def conclude(inner, second, second_bias, result):
    for band in bands(second.size):
        result[:, band] = low(dot(inner[...], second.columns(band)) + second_bias[:, band])


def weight_grad(left, right, grad):
    for band in bands(left.shape[1]):
        grad.store(band, low(dot_left(left[:, band], right[...])))


def column_sums(value, sums, row):
    for band in bands(value.shape[1]):
        sums[row : row + 1, band] = jnp.sum(wide(value[:, band]), axis=0, keepdims=True)


def back_perceive(grad_result, second, slope, grad_inner):
    for band in bands(second.size):
        grad_inner[:, band] = low(dot_right(grad_result[...], second.band(band)) * wide(slope[:, band]))


def back_unit(grad_inner, first, unit, scale, slope, grad_unit, grad_pre):
    width = unit.shape[1]
    products = 0.0
    for band in bands(width):
        value = dot_right(grad_inner[...], first.band(band))
        grad_unit[:, band] = value
        products = products + lane_sums(value * wide(unit[:, band]))
    mean_dot = jnp.sum(products, axis=1, keepdims=True) * (1.0 / width)
    for band in bands(width):
        value = scale[...] * (grad_unit[:, band] - wide(unit[:, band]) * mean_dot)
        grad_pre[:, band] = low(value * wide(slope[:, band]))


def back_mean(grad_pre, neigh, mix_turned, grad_mean, far_out, sib_out):
    sib, far = mix_turned
    for band in bands(grad_mean.shape[1]):
        value = low(dot_right(grad_pre[...], neigh.band(band)))
        grad_mean[:, band] = value
        far_out[:, band] = low(dot(far[...], value))
        sib_out[:, band] = low(dot(sib[...], value))


def back_hidden(own, pick, grad_mean, sib_back, far_back, slope, grad_hidden_pre):
    for band in bands(grad_mean.shape[1]):
        value = dot(own[...], grad_mean[:, band]) + dot(pick[...], far_back[:, band])
        value = value + wide(sib_back[:, band])
        grad_hidden_pre[:, band] = low(value * wide(slope[:, band]))


def back_input(grad_self, grad_hidden_pre, weight, grad_input):
    for band in bands(grad_input.shape[1]):
        grad_input[:, band] = low(
            grad_self[:, band] + dot_right(grad_hidden_pre[...], weight.band(band))
        )


def mix_rows(neighbours, counts, spans, so_far, begin, end):
    node_count, count = neighbours.shape
    block = 16

    def kernel(index_ref, count_ref, *refs):
        outs = refs[-len(spans) :]
        index = index_ref[...]
        values = count_ref[...].astype(jnp.float32)
        shares = values / jnp.sum(values, axis=1, keepdims=True)
        for number, ((first, last), out_ref) in enumerate(zip(spans, outs)):
            column = first + lax.broadcasted_iota(jnp.int32, (block, last - first), 1)
            total = jnp.zeros((block, last - first), jnp.float32)
            far = number == len(spans) - 1
            for k in range(count // 2 if far else 0, count if far else count // 2):
                total = jnp.where(index[:, k : k + 1] == column, shares[:, k : k + 1], total)
            out_ref[...] = total.astype(LOW)

    start = begin // block
    rows = lambda n: (n + start, 0)
    shapes = [jax.ShapeDtypeStruct((node_count, last - first), LOW) for first, last in spans]
    return pl.pallas_call(
        kernel,
        grid=((end - begin) // block,),
        in_specs=[pl.BlockSpec((block, count), rows)] * 2
        + [pl.BlockSpec(memory_space=pl.ANY)] * len(so_far),
        out_specs=[pl.BlockSpec((block, last - first), rows) for first, last in spans],
        out_shape=shapes,
        input_output_aliases={2 + n: n for n in range(len(so_far))},
        cost_estimate=pl.CostEstimate(flops=1, bytes_accessed=1, transcendentals=0),
        name="mixing",
    )(neighbours, counts, *so_far)


def local(
    pin_features,
    board_features,
    node_kinds,
    neighbours,
    visit_counts,
    served_rows,
    board_proj,
    neigh_weight,
    neigh_bias,
    concat_weight,
    concat_bias,
    mlp_weight_one,
    mlp_bias_one,
    mlp_weight_two,
    mlp_bias_two,
    out_grad,
):
    slice_rows, width = pin_features.shape
    board_width = board_features.shape[1]
    peers, slots = served_rows.shape
    near_rows, far_rows = 2 * slice_rows, peers * slots
    layout = Layout(peers)
    row, core = lax.axis_index("rows"), lax.axis_index("half")
    device = row * 2 + core
    biases = jnp.concatenate([neigh_bias, concat_bias, mlp_bias_one, mlp_bias_two])
    bias_count, own_bias = biases.shape
    lane = lax.broadcasted_iota(jnp.int32, (bias_count, width), 1)
    bias_rows = jnp.where(lane // own_bias == device, jnp.tile(biases, (1, width // own_bias)), 0.0)
    halves = concat_weight[:, 0]
    proj_rows, rows, half_rows = board_proj.shape[0], neigh_weight.shape[1], halves.shape[1]

    turned = jnp.where(
        neighbours < near_rows, (neighbours + near_rows - core * slice_rows) % near_rows, neighbours
    )
    spans = ((0, slice_rows), (slice_rows, near_rows), (near_rows, near_rows + far_rows))
    mixing = []

    def mix_more(part):
        size = slice_rows // 4
        return mix_rows(turned, visit_counts, spans, mixing, part * size, (part + 1) * size)

    served = served_rows.reshape(-1)
    node = lax.broadcasted_iota(jnp.int32, (far_rows, slice_rows), 1)
    picking = (served[:, None] == node).astype(LOW)
    node = lax.broadcasted_iota(jnp.int32, (slice_rows, far_rows), 0)
    pick_turned = (served[None, :] == node).astype(LOW)
    kinds = node_kinds[:, None]

    zero = Gather(layout, [board_proj, neigh_weight[0], bias_rows])
    one = Gather(layout, [halves[0], mlp_weight_one[0], mlp_weight_two[0], neigh_weight[1]])
    two = Gather(layout, [halves[1], mlp_weight_one[1], mlp_weight_two[1]])

    slots_out = [(k, j, i) for j in range(2) for k in range(layout.deep) for i in range(2)]

    def tables(chain):
        return [layout.orders(row, core, chain.order(), slots_out)]

    nodes_low = ((slice_rows, width), LOW)
    nodes_wide = ((slice_rows, width), jnp.float32)
    far_low = ((far_rows, width), LOW)
    column = ((slice_rows, 1), jnp.float32)
    sum_rows = ((8, width), jnp.float32)
    blocks = lambda count: pltpu.VMEM((layout.rows, 2, count, width), LOW)
    own_nodes = pltpu.VMEM(*nodes_low)
    own_wide = pltpu.VMEM(*nodes_wide)
    own_column = pltpu.VMEM(*column)
    dma = pltpu.SemaphoreType.DMA

    def leaving(count):
        return [((layout.rows, count, width), LOW)] * 2

    def exchange(outgoing):
        far = lax.all_to_all(
            outgoing.reshape(peers, slots, width), "rows", split_axis=0, concat_axis=0, tiled=True
        )
        return far.reshape(far_rows, width)

    def bias_part(blocks):
        return sum(jnp.sum(wide(item[:, proj_rows + rows :]), 0) for item in blocks)

    depths = range(1, layout.deep)
    zero.deepen(*depths)
    one.ahead(0)
    mixing = tie([zero, one], mix_more(0))
    zero.join(0)
    zero.ahead(0)
    one.deepen(*depths[:1])
    one.aside(0)
    mixing, picking, kinds = tie([zero, one], mix_more(1), picking, kinds)
    zero.aside(0)
    zero.swap(0)
    two.ahead(0)
    one.deepen(*depths[1:2])
    mixing = tie([zero, one, two], mix_more(2))
    zero.swap_far(0)
    two.aside(0)
    one.deepen(*depths[2:])
    two.deepen(*depths[:1])
    bias_full = bias_part(zero.levels + zero.squares + zero.near)
    mixing, bias_full = tie([zero, one, two], mix_more(3), bias_full)
    bias_full = bias_full + bias_part(zero.far)
    one.join(1)

    def hidden_body(tables, ins, pieces, outs, _, scratch):
        pin, board, kinds, bias, picking = ins
        features, hidden, slope, outgoing, proj_out = outs
        weights, sems = scratch
        fetch(tables, pieces, 0, weights, sems.at[0])
        fetched(weights, sems.at[0])
        proj, weight = View(weights, 0, proj_rows), View(weights, proj_rows, rows)
        for band in bands(width):
            projected = dot(board[...], proj.columns(band))
            features[:, band] = low(jnp.where(kinds[...] == 1, wide(pin[:, band]), projected))
        for band in bands(board_width):
            proj_out[band, :] = proj.band(band)
        spread_hidden(features, weight, bias.at[0:1], picking, hidden, slope, outgoing)

    one.ahead(1)
    one.swap(0)
    one.swap_far(0)
    two.deepen(*depths[1:])
    features, hidden, hidden_slope, outgoing, proj_full = tie(
        [one, two],
        *call(
            "hidden",
            hidden_body,
            tables(zero),
            [pin_features, board_features, kinds, bias_full, picking],
            zero.pieces(),
            [nodes_low] * 3 + [far_low, ((board_width, width), LOW)],
            [],
            [blocks(proj_rows + rows), dma((1,))],
        ),
    )
    incoming, other = exchange(outgoing), swap_cores(hidden)
    one.aside(1)
    one.swap(1)
    two.join(1)
    two.ahead(1)
    two.swap(0)
    two.swap_far(0)
    incoming, other = tie([one, two], incoming, other)
    one.swap_far(1)
    tie([one])

    def middle_body(tables, ins, pieces, outs, _, scratch):
        mixes, (hidden, other, incoming, features, bias, picking) = ins[:3], ins[3:]
        mean, unit, slope_pre, scale, inner, slope_inner, result, ahead, slope_ahead, outgoing = outs
        both, rest, gated, sems = scratch
        fetch(tables, pieces, 0, both, sems.at[0])
        fetch(tables, pieces, half_rows, rest, sems.at[1])
        first, second, weight = (View(rest, n * rows, rows) for n in range(3))
        own, neigh = (View(both, 0, half_rows, half) for half in range(2))
        average(mixes, hidden, other, incoming, mean)
        fetched(both, sems.at[0])
        combine(features, mean, own, neigh, bias.at[2:3], gated, unit, slope_pre, scale)
        fetched(rest, sems.at[1])
        perceive(unit, first, bias.at[4:5], inner, slope_inner)
        conclude(inner, second, bias.at[6:7], result)
        spread_hidden(result, weight, bias.at[1:2], picking, ahead, slope_ahead, outgoing)

    two.aside(1)
    two.swap(1)
    (
        mean_zero,
        unit,
        slope_pre,
        scale,
        inner,
        slope_inner,
        features_one,
        hidden_one,
        hidden_slope_one,
        outgoing,
    ) = tie(
        [two],
        *call(
            "middle",
            middle_body,
            tables(one),
            [*mixing, hidden, other, incoming, features, bias_full, picking],
            one.pieces(),
            [nodes_low] * 3 + [column] + [nodes_low] * 5 + [far_low],
            [],
            [blocks(half_rows), blocks(3 * rows), own_wide, dma((2,))],
        ),
    )
    incoming, other = exchange(outgoing), swap_cores(hidden_one)
    two.swap_far(1)
    mix_turned = [item.T for item in mixing]
    incoming, other, mix_turned = tie([two], incoming, other, mix_turned)

    def top_body(tables, ins, pieces, outs, leave, scratch):
        mixes, (hidden, other, incoming, features, bias, grad_result) = ins[:3], ins[3:]
        mean, result, unit, slope_pre, scale, grad_inner, sums = outs
        weights, grads, gated, inner, slope_inner, sems = scratch
        fetch(tables, pieces, 0, weights, sems.at[0])
        own, neigh = (View(weights, 0, half_rows, half) for half in range(2))
        first, second = View(weights, half_rows, rows), View(weights, half_rows + rows, rows)
        average(mixes, hidden, other, incoming, mean)
        fetched(weights, sems.at[0])
        combine(features, mean, own, neigh, bias.at[3:4], gated, unit, slope_pre, scale)
        perceive(unit, first, bias.at[5:6], inner, slope_inner)
        weight_grad(inner, grad_result, View(grads, 0, rows))
        back_perceive(grad_result, second, slope_inner, grad_inner)
        weight_grad(unit, grad_inner, View(grads, rows, rows))
        send_off(tables, grads, *leave, (sems.at[1], sems.at[2]))
        conclude(inner, second, bias.at[7:8], result)
        sums[...] = jnp.zeros_like(sums)
        column_sums(grad_result, sums, 0)
        column_sums(grad_inner, sums, 1)
        sent_off(*leave, (sems.at[1], sems.at[2]))

    mean_one, embeddings, unit_one, slope_pre_one, scale_one, grad_inner, sums_one, kept, sent = call(
        "top",
        top_body,
        tables(two),
        [*mixing, hidden_one, other, incoming, features_one, bias_full, out_grad],
        two.pieces(),
        [nodes_low] * 4 + [column, nodes_low, sum_rows],
        leaving(2 * rows),
        [blocks(half_rows + 2 * rows), blocks(2 * rows), own_wide, own_nodes, own_nodes, dma((3,))],
    )
    five = Scatter(layout, kept, sent)

    def norm_body(tables, ins, pieces, outs, _, scratch):
        grad_inner, unit, scale, slope_pre, *mix_turned = ins
        grad_pre, grad_mean, far_out, sib_out, sums = outs
        weights, grad_unit, sems = scratch
        fetch(tables, pieces, 0, weights, sems.at[0])
        fetched(weights, sems.at[0])
        first = View(weights, half_rows, rows)
        back_unit(grad_inner, first, unit, scale, slope_pre, grad_unit, grad_pre)
        neigh = View(weights, 0, half_rows, 1)
        back_mean(grad_pre, neigh, mix_turned, grad_mean, far_out, sib_out)
        sums[...] = jnp.zeros_like(sums)
        column_sums(grad_pre, sums, 0)

    def norm(name, chain, *ins):
        return call(
            name,
            norm_body,
            tables(chain),
            [*ins, *mix_turned[1:]],
            chain.pieces(),
            [nodes_low] * 2 + [far_low, nodes_low, sum_rows],
            [],
            [blocks(half_rows + rows), own_wide, dma((1,))],
        )

    def sides(name, chain, features, mean, grad_pre):
        def body(tables, ins, pieces, outs, leave, scratch):
            features, mean, grad_pre = ins
            both, grads, sems = scratch
            fetch(tables, pieces, 0, both, sems.at[0])
            weight_grad(features, grad_pre, View(grads, 0, half_rows, 0))
            weight_grad(mean, grad_pre, View(grads, 0, half_rows, 1))
            send_off(tables, grads, *leave, (sems.at[1], sems.at[2]))
            fetched(both, sems.at[0])
            own = View(both, 0, half_rows, 0)
            for band in bands(width):
                outs[0][:, band] = dot_right(grad_pre[...], own.band(band))
            sent_off(*leave, (sems.at[1], sems.at[2]))

        return call(
            name,
            body,
            tables(chain),
            [features, mean, grad_pre],
            chain.pieces(),
            [nodes_wide],
            leaving(half_rows),
            [blocks(half_rows), blocks(half_rows), dma((3,))],
        )

    five.advance()
    grad_pre, grad_mean, far_out, sib_out, sums_pre_one = tie(
        [five], *norm("norm1", two, grad_inner, unit_one, scale_one, slope_pre_one)
    )
    five.advance()
    far_back, sib_back = exchange(far_out), swap_cores(sib_out)
    grad_self, kept, sent = sides("sides1", two, features_one, mean_one, grad_pre)
    far_back, sib_back, grad_self, kept, sent = tie([five], far_back, sib_back, grad_self, kept, sent)
    six = Scatter(layout, kept, sent)

    def bridge_body(tables, ins, pieces, outs, leave, scratch):
        own, pick, grad_mean, sib_back, far_back, slope_hidden, features, grad_self = ins[:8]
        inner, unit, slope_inner = ins[8:]
        grad_inner, sums = outs
        weights, grads, grad_hidden_pre, grad_input, sems = scratch
        fetch(tables, pieces, half_rows + rows, weights, sems.at[0])
        back_hidden(own, pick, grad_mean, sib_back, far_back, slope_hidden, grad_hidden_pre)
        weight_grad(features, grad_hidden_pre, View(grads, 0, rows))
        fetched(weights, sems.at[0])
        back_input(grad_self, grad_hidden_pre, View(weights, rows, rows), grad_input)
        weight_grad(inner, grad_input, View(grads, rows, rows))
        back_perceive(grad_input, View(weights, 0, rows), slope_inner, grad_inner)
        weight_grad(unit, grad_inner, View(grads, 2 * rows, rows))
        send_off(tables, grads, *leave, (sems.at[1], sems.at[2]))
        sums[...] = jnp.zeros_like(sums)
        column_sums(grad_hidden_pre, sums, 0)
        column_sums(grad_input, sums, 1)
        column_sums(grad_inner, sums, 2)
        sent_off(*leave, (sems.at[1], sems.at[2]))

    five.advance()
    six.advance()
    grad_inner, sums_zero, kept, sent = tie(
        [five, six],
        *call(
            "bridge",
            bridge_body,
            tables(one),
            [mix_turned[0], pick_turned, grad_mean, sib_back, far_back, hidden_slope_one]
            + [features_one, grad_self, inner, unit, slope_inner],
            one.pieces(),
            [nodes_low, sum_rows],
            leaving(3 * rows),
            [blocks(2 * rows), blocks(3 * rows), own_nodes, own_nodes, dma((3,))],
        ),
    )
    seven = Scatter(layout, kept, sent)
    five.advance()
    six.advance()
    seven.advance()
    grad_pre, grad_mean, far_out, sib_out, sums_pre_zero = tie(
        [five, six, seven], *norm("norm0", one, grad_inner, unit, scale, slope_pre)
    )
    seven.advance()
    far_back, sib_back = exchange(far_out), swap_cores(sib_out)
    grad_self, kept, sent = sides("sides0", one, features, mean_zero, grad_pre)
    far_back, sib_back, grad_self, kept, sent = tie(
        [six, seven], far_back, sib_back, grad_self, kept, sent
    )
    eight = Scatter(layout, kept, sent)

    def bottom_body(tables, ins, pieces, outs, leave, scratch):
        own, pick, grad_mean, sib_back, far_back, slope_hidden, features, grad_self = ins[:8]
        board, kinds, sums_one, pre_one, sums_zero, pre_zero = ins[8:]
        (grad_input,) = outs
        weights, grads, grad_hidden_pre, grad_board, sums, sems = scratch
        fetch(tables, pieces, proj_rows, weights, sems.at[0])
        back_hidden(own, pick, grad_mean, sib_back, far_back, slope_hidden, grad_hidden_pre)
        weight_grad(features, grad_hidden_pre, View(grads, 0, rows))
        column_sums(grad_hidden_pre, sums, 0)
        fetched(weights, sems.at[0])
        back_input(grad_self, grad_hidden_pre, View(weights, 0, rows), grad_input)
        for band in bands(width):
            grad_board[:, band] = low(jnp.where(kinds[...] == 1, 0.0, wide(grad_input[:, band])))
        weight_grad(board, grad_board, View(grads, rows, proj_rows))
        totals = [sums[0:1, :], sums_zero[0:1, :], pre_zero[0:1, :], pre_one[0:1, :]]
        totals += [sums_zero[2:3, :], sums_one[1:2, :], sums_zero[1:2, :], sums_one[0:1, :]]
        totals = low(jnp.concatenate([*totals, jnp.zeros((8, width), jnp.float32)]))
        for chip in range(layout.rows):
            for half in range(2):
                grads[chip, half, rows + proj_rows :, :] = totals
        send_off(tables, grads, *leave, (sems.at[1], sems.at[2]))
        sent_off(*leave, (sems.at[1], sems.at[2]))

    six.advance()
    seven.advance()
    eight.advance()
    grad_input, kept, sent = tie(
        [six, seven, eight],
        *call(
            "bottom",
            bottom_body,
            tables(zero),
            [mix_turned[0], pick_turned, grad_mean, sib_back, far_back, hidden_slope, features]
            + [grad_self, board_features, kinds, sums_one, sums_pre_one, sums_zero, sums_pre_zero],
            zero.pieces(),
            [nodes_low],
            leaving(rows + proj_rows + 16),
            [blocks(rows), blocks(rows + proj_rows + 16), own_nodes, own_nodes]
            + [pltpu.VMEM(*sum_rows), dma((3,))],
        ),
    )
    nine = Scatter(layout, kept, sent)
    chains = [five, six, seven, eight, nine]
    eight.advance()
    nine.advance()
    six.advance()
    tie([nine])
    nine.advance()
    tie([eight, six])
    eight.advance()
    seven.advance()
    tie([nine, eight, seven])
    nine.advance()
    eight.advance()
    tie([nine])
    nine.advance()
    is_pin = kinds == 1
    pin_grad = jnp.where(is_pin, wide(grad_input), 0.0)
    grad_board = jnp.where(is_pin, jnp.zeros_like(grad_input), grad_input)
    board_grad = dot_right(grad_board, proj_full)

    five, six, seven, eight, nine = (chain.result() for chain in chains)
    bias_sums = nine[rows + proj_rows :][:bias_count]
    bias_sums = lax.dynamic_slice_in_dim(bias_sums, device * own_bias, own_bias, 1)
    bias_sums = bias_sums.reshape(4, -1, own_bias)
    return (
        embeddings,
        pin_grad,
        board_grad,
        nine[rows : rows + proj_rows],
        jnp.stack([nine[:rows], seven[:rows]]),
        bias_sums[0],
        jnp.stack([eight, six])[:, None],
        bias_sums[1],
        jnp.stack([seven[2 * rows :], five[rows:]]),
        bias_sums[2],
        jnp.stack([seven[rows : 2 * rows], five[:rows]]),
        bias_sums[3],
    )


def solution(mesh):
    nodes = P(("rows", "half"), None)
    weight = P(None, ("rows", "half"), None)
    bias = P(None, ("rows", "half"))
    concat = P(None, "half", "rows", None)
    placed = (nodes, nodes, P(("rows", "half")), nodes, nodes, nodes, nodes)
    placed += (weight, bias, concat, bias, weight, bias, weight, bias, nodes)
    results = (nodes, nodes, nodes, nodes) + (weight, bias, concat, bias, weight, bias, weight, bias)

    def whole(*args):
        devices = mesh.shape["rows"] * mesh.shape["half"]
        shards = (args[6].shape[0] // devices, args[7].shape[1] // devices)
        fits = mesh.shape["rows"] % 4 == 0 and not any(count % 16 for count in shards)
        return jax.shard_map(
            local if fits else plain,
            mesh=mesh,
            in_specs=placed,
            out_specs=results,
            check_vma=False,
        )(*args)

    return whole
```

```python
import jax
import jax.numpy as jnp
from jax import lax
from jax.experimental import pallas as pl
from jax.experimental.pallas import tpu as pltpu
from jax.sharding import PartitionSpec as P

LOW = jnp.bfloat16
AXES = ("rows", "half")
CURVE = 0.7978845608028654
CUBIC = 0.044715
TILE = 256


def activate(value):
    return jax.nn.gelu(value, approximate=True)


def unit_map(value):
    scaled = activate(value)
    return scaled * lax.rsqrt(jnp.mean(scaled * scaled, axis=-1, keepdims=True) + 1e-06)


def matmul(left, right):
    return jnp.dot(left, right, preferred_element_type=jnp.float32)


def column_sum(value):
    return jnp.sum(value.astype(jnp.float32), axis=0)


def fetch_shared(
    neigh_weight, neigh_bias, concat_bias, weight_one, bias_one, weight_two, bias_two, board_proj
):
    return (
        lax.all_gather(neigh_weight, ("rows", "half"), axis=1, tiled=True),
        lax.all_gather(neigh_bias, ("rows", "half"), axis=1, tiled=True),
        lax.all_gather(concat_bias, ("rows", "half"), axis=1, tiled=True),
        lax.all_gather(weight_one, ("rows", "half"), axis=1, tiled=True),
        lax.all_gather(bias_one, ("rows", "half"), axis=1, tiled=True),
        lax.all_gather(weight_two, ("rows", "half"), axis=1, tiled=True),
        lax.all_gather(bias_two, ("rows", "half"), axis=1, tiled=True),
        lax.all_gather(board_proj, ("rows", "half"), axis=0, tiled=True),
    )


def fetch_half(own_half):
    return lax.all_gather(own_half, "rows", axis=1, tiled=True)


def refetch_shared(
    neigh_weight, neigh_bias, concat_bias, weight_one, bias_one, weight_two, bias_two, board_proj
):
    return (
        lax.all_gather(neigh_weight, ("rows", "half"), axis=1, tiled=True),
        lax.all_gather(neigh_bias, ("rows", "half"), axis=1, tiled=True),
        lax.all_gather(concat_bias, ("rows", "half"), axis=1, tiled=True),
        lax.all_gather(weight_one, ("rows", "half"), axis=1, tiled=True),
        lax.all_gather(bias_one, ("rows", "half"), axis=1, tiled=True),
        lax.all_gather(weight_two, ("rows", "half"), axis=1, tiled=True),
        lax.all_gather(bias_two, ("rows", "half"), axis=1, tiled=True),
        lax.all_gather(board_proj, ("rows", "half"), axis=0, tiled=True),
    )


def refetch_half(own_half):
    return lax.all_gather(own_half, "rows", axis=1, tiled=True)


def plain(
    pin_features,
    board_features,
    node_kinds,
    neighbours,
    visit_counts,
    served_rows,
    board_proj,
    neigh_weight,
    neigh_bias,
    concat_weight,
    concat_bias,
    mlp_weight_one,
    mlp_bias_one,
    mlp_weight_two,
    mlp_bias_two,
    out_grad,
):
    slice_rows, feature_width = pin_features.shape
    layer_count = neigh_weight.shape[0]
    peer_count, slot_count = served_rows.shape
    chip_rows = 2 * slice_rows
    table_rows = chip_rows + peer_count * slot_count
    counts = visit_counts.astype(jnp.float32)
    shares = (counts / jnp.sum(counts, axis=1, keepdims=True)).astype(jnp.bfloat16)
    positions = jnp.broadcast_to(jnp.arange(slice_rows, dtype=jnp.int32)[:, None], neighbours.shape)
    mixing = jnp.zeros((slice_rows, table_rows), jnp.bfloat16).at[positions, neighbours].set(shares)
    served_flat = served_rows.reshape(-1)
    is_pin = (node_kinds == 1)[:, None]
    to_low = jnp.bfloat16
    master_pieces = (
        neigh_weight.astype(to_low),
        neigh_bias.astype(to_low),
        concat_bias.astype(to_low),
        mlp_weight_one.astype(to_low),
        mlp_bias_one.astype(to_low),
        mlp_weight_two.astype(to_low),
        mlp_bias_two.astype(to_low),
        board_proj.astype(to_low),
    )
    own_half = concat_weight[:, 0].astype(to_low)
    shared_full = fetch_shared(*master_pieces)
    half_full = fetch_half(own_half)
    (
        neigh_full,
        nbias_full,
        cbias_full,
        first_full,
        fbias_full,
        second_full,
        sbias_full,
        proj_full,
    ) = shared_full
    projected = matmul(board_features, proj_full)
    features = jnp.where(is_pin, pin_features.astype(jnp.float32), projected).astype(to_low)
    saved = []
    result = None
    for layer_index in range(layer_count):
        hidden_pre = matmul(features, neigh_full[layer_index]) + nbias_full[layer_index].astype(
            jnp.float32
        )
        hidden_full, hidden_pull = jax.vjp(activate, hidden_pre)
        hidden = hidden_full.astype(to_low)
        chip_hidden = lax.all_gather(hidden, "half", axis=0, tiled=True)
        outgoing = hidden[served_rows]
        incoming = lax.all_to_all(outgoing, "rows", split_axis=0, concat_axis=0, tiled=True)
        lookup_table = jnp.concatenate([chip_hidden, incoming.reshape(-1, feature_width)], axis=0)
        neigh_mean = matmul(mixing, lookup_table).astype(to_low)
        paired = lax.all_to_all(
            jnp.stack([features, neigh_mean]), "half", split_axis=0, concat_axis=1, tiled=True
        )[0]
        partial_value = matmul(paired, half_full[layer_index])
        pre_sum = lax.psum_scatter(
            partial_value.astype(jnp.bfloat16), "half", scatter_dimension=0, tiled=True
        ).astype(jnp.float32) + cbias_full[layer_index].astype(jnp.float32)
        unit_full, unit_pull = jax.vjp(unit_map, pre_sum)
        unit_rows = unit_full.astype(to_low)
        inner_pre = matmul(unit_rows, first_full[layer_index]) + fbias_full[layer_index].astype(
            jnp.float32
        )
        inner_full, inner_pull = jax.vjp(activate, inner_pre)
        inner_act = inner_full.astype(to_low)
        result = matmul(inner_act, second_full[layer_index]) + sbias_full[layer_index].astype(
            jnp.float32
        )
        saved.append((features, hidden_pull, paired, unit_rows, unit_pull, inner_act, inner_pull))
        features = result.astype(to_low)
    embeddings = result.astype(to_low)
    (
        neigh_full,
        nbias_full,
        cbias_full,
        first_full,
        fbias_full,
        second_full,
        sbias_full,
        proj_full,
    ) = refetch_shared(*master_pieces)
    half_full = refetch_half(own_half)
    grad_result = out_grad
    grads_neigh = [None] * layer_count
    grads_nbias = [None] * layer_count
    grads_half = [None] * layer_count
    grads_cbias = [None] * layer_count
    grads_first = [None] * layer_count
    grads_fbias = [None] * layer_count
    grads_second = [None] * layer_count
    grads_sbias = [None] * layer_count
    grad_input = None
    for layer_index in reversed(range(layer_count)):
        features, hidden_pull, paired, unit_rows, unit_pull, inner_act, inner_pull = saved[
            layer_index
        ]
        grads_second[layer_index] = matmul(inner_act.T, grad_result)
        grads_sbias[layer_index] = column_sum(grad_result)
        grad_inner = inner_pull(matmul(grad_result, second_full[layer_index].T))[0].astype(to_low)
        grads_first[layer_index] = matmul(unit_rows.T, grad_inner)
        grads_fbias[layer_index] = column_sum(grad_inner)
        grad_pre = unit_pull(matmul(grad_inner, first_full[layer_index].T))[0].astype(to_low)
        grads_cbias[layer_index] = column_sum(grad_pre)
        grad_pre_full = lax.all_gather(grad_pre, "half", axis=0, tiled=True)
        grads_half[layer_index] = matmul(paired.T, grad_pre_full)
        grad_paired = matmul(grad_pre_full, half_full[layer_index].T)
        returned = lax.all_to_all(
            grad_paired[None].astype(jnp.bfloat16), "half", split_axis=1, concat_axis=0, tiled=True
        ).astype(jnp.float32)
        grad_self = returned[0]
        grad_mean = returned[1].astype(to_low)
        grad_table = matmul(mixing.T, grad_mean)
        grad_chip = lax.psum_scatter(
            grad_table[:chip_rows].astype(jnp.bfloat16), "half", scatter_dimension=0, tiled=True
        ).astype(jnp.float32)
        grad_far = lax.all_to_all(
            grad_table[chip_rows:]
            .reshape(peer_count, slot_count, feature_width)
            .astype(jnp.bfloat16),
            "rows",
            split_axis=0,
            concat_axis=0,
            tiled=True,
        ).astype(jnp.float32)
        grad_hidden = grad_chip.at[served_flat].add(grad_far.reshape(-1, feature_width))
        grad_hidden_pre = hidden_pull(grad_hidden)[0].astype(to_low)
        grads_neigh[layer_index] = matmul(features.T, grad_hidden_pre)
        grads_nbias[layer_index] = column_sum(grad_hidden_pre)
        grad_input = (grad_self + matmul(grad_hidden_pre, neigh_full[layer_index].T)).astype(to_low)
        grad_result = grad_input
    pin_grad = jnp.where(is_pin, grad_input.astype(jnp.float32), 0.0)
    grad_board = jnp.where(is_pin, jnp.zeros_like(grad_input), grad_input)
    board_grad = matmul(grad_board, proj_full.T)
    proj_grad = matmul(board_features.T, grad_board)
    summed = (
        lax.psum_scatter(jnp.stack(grads_neigh), ("rows", "half"), scatter_dimension=1, tiled=True),
        lax.psum_scatter(jnp.stack(grads_nbias), ("rows", "half"), scatter_dimension=1, tiled=True),
        lax.psum_scatter(jnp.stack(grads_cbias), ("rows", "half"), scatter_dimension=1, tiled=True),
        lax.psum_scatter(jnp.stack(grads_first), ("rows", "half"), scatter_dimension=1, tiled=True),
        lax.psum_scatter(jnp.stack(grads_fbias), ("rows", "half"), scatter_dimension=1, tiled=True),
        lax.psum_scatter(
            jnp.stack(grads_second), ("rows", "half"), scatter_dimension=1, tiled=True
        ),
        lax.psum_scatter(jnp.stack(grads_sbias), ("rows", "half"), scatter_dimension=1, tiled=True),
        lax.psum_scatter(proj_grad, ("rows", "half"), scatter_dimension=0, tiled=True),
    )
    half_summed = lax.psum_scatter(jnp.stack(grads_half), "rows", scatter_dimension=1, tiled=True)
    (
        neigh_grad,
        nbias_grad,
        cbias_grad,
        first_grad,
        fbias_grad,
        second_grad,
        sbias_grad,
        board_proj_grad,
    ) = summed
    return (
        embeddings,
        pin_grad,
        board_grad,
        board_proj_grad,
        neigh_grad,
        nbias_grad,
        half_summed[:, None],
        cbias_grad,
        first_grad,
        fbias_grad,
        second_grad,
        sbias_grad,
    )


def low(value):
    return value.astype(LOW)


def wide(value):
    return value.astype(jnp.float32)


class Layout:
    def __init__(self, row_count):
        self.rows = row_count
        self.deep = row_count // 4
        self.sizes = (2, 2, self.deep)

    def split(self, row):
        return [row % 2, (row // 2) % 2, row // 4]

    def join(self, place):
        return place[0] + 2 * (place[1] + 2 * place[2])

    def ring(self, dims, value, step=1):
        pairs = []
        for row in range(self.rows):
            for core in range(2):
                place = self.split(row)
                dim = dims[core]
                place[dim] = (place[dim] + step) % self.sizes[dim]
                pairs.append((row * 2 + core, self.join(place) * 2 + core))
        return lax.ppermute(value, AXES, pairs)

    def first(self, value):
        return self.ring((0, 1), value)

    def last(self, value):
        return self.ring((1, 0), value)

    def middle(self, value, step=1):
        return self.ring((2, 2), value, step)

    def orders(self, row, core, slots_in, slots_out):
        slots = jnp.array([slots_in, slots_in, slots_in, slots_out, slots_out], jnp.int32)
        line = lax.broadcasted_iota(jnp.int32, slots.shape[:2], 0)
        whose = jnp.where(line % 2 == 1, core, 1 - core)
        sign = jnp.where(line < 3, -1, 1)
        place = self.split(row)
        k, j, i = (slots[:, :, part] for part in range(3))
        ahead, aside = jnp.where(whose == 0, i, j), jnp.where(whose == 0, j, i)
        middle = (place[2] + sign * k + self.deep) % self.deep
        order = self.join(((place[0] + ahead) % 2, (place[1] + aside) % 2, middle))
        return jnp.where(line == 0, core, order).astype(jnp.int32)


def swap_cores(value):
    return lax.ppermute(value, "half", [(0, 1), (1, 0)])


class Gather:
    def __init__(self, layout, parts):
        self.layout = layout
        self.own = low(jnp.concatenate(parts))[None]
        self.levels, self.slots = [self.own], [[(0, 0, 0)]]
        self.squares, self.near, self.far = [], [], []

    @property
    def values(self):
        return (self.own, self.levels, self.squares, self.near, self.far)

    @values.setter
    def values(self, held):
        self.own = held[0]
        self.levels, self.squares, self.near, self.far = (list(item) for item in held[1:])

    def deepen(self, *steps):
        for k in steps:
            self.levels.append(self.layout.middle(self.own, k))
            self.slots.append([(k, 0, 0)])

    def join(self, begin):
        self.levels[begin:] = [jnp.concatenate(self.levels[begin:])]
        self.slots[begin:] = [sum(self.slots[begin:], [])]

    def ahead(self, number):
        item = self.levels[number]
        self.levels[number] = jnp.concatenate([item, self.layout.first(item)])
        self.slots[number] = self.slots[number] + [(k, j, 1) for k, j, _ in self.slots[number]]

    def aside(self, number):
        self.squares.append(self.layout.last(self.levels[number]))

    def swap(self, number):
        self.near.append(swap_cores(self.levels[number]))

    def swap_far(self, number):
        self.far.append(swap_cores(self.squares[number]))

    def pieces(self):
        own = [item for pair in zip(self.levels, self.squares) for item in pair]
        return own + [item for pair in zip(self.near, self.far) for item in pair]

    def order(self):
        result = []
        for slots in self.slots:
            result += slots + [(k, 1, i) for k, _, i in slots]
        return result


class Scatter:
    def __init__(self, layout, kept, sent):
        self.layout = layout
        self.values = [kept, sent]
        self.plan = [self.swap, self.aside, self.ahead, self.deepen]
        self.shape = (layout.deep, 2, *kept.shape[1:])

    def advance(self):
        self.plan.pop(0)()

    def near(self, *index):
        kept, got, came = self.values[:3]
        half = (2, *self.shape)
        return (
            wide(kept.reshape(half)[(0, *index)])
            + wide(got.reshape(half)[(0, *index)])
            + wide(came.reshape(self.shape)[index])
        )

    def swap(self):
        self.values = [self.values[0], swap_cores(self.values[1])]

    def aside(self):
        kept, got = self.values
        half = self.layout.rows // 2
        self.values = [kept, got, self.layout.last(low(wide(kept[half:]) + wide(got[half:])))]

    def ahead(self):
        self.values = [*self.values, self.layout.first(low(self.near(slice(None), 1)))]

    def level(self, k):
        return self.near(k, 0) + wide(self.values[3][k])

    def deepen(self):
        got = [self.layout.middle(low(self.level(k)), k) for k in range(1, self.layout.deep)]
        self.values = [*self.values, *got]

    def result(self):
        return self.level(0) + sum(wide(item) for item in self.values[4:])


def tie(chains, *values):
    held, values = lax.optimization_barrier(([chain.values for chain in chains], values))
    for chain, item in zip(chains, held):
        chain.values = item
    return values[0] if len(values) == 1 else values


def dot(left, right):
    return jnp.dot(left, right, preferred_element_type=jnp.float32)


def dot_right(left, right):
    return lax.dot_general(
        left, right, (((1,), (1,)), ((), ())), preferred_element_type=jnp.float32
    )


def dot_left(left, right):
    return lax.dot_general(
        left, right, (((0,), (0,)), ((), ())), preferred_element_type=jnp.float32
    )


def gelu_pair(value):
    square = value * value
    bend = jnp.tanh(value * (CURVE + CURVE * CUBIC * square))
    half = 0.5 + 0.5 * bend
    slope = half + value * (0.5 - 0.5 * bend * bend) * (CURVE + 3.0 * CURVE * CUBIC * square)
    return value * half, slope


def bands(size):
    return [slice(begin, begin + TILE) for begin in range(0, size, TILE)]


class View:
    def __init__(self, ref, offset, rows, half=None):
        self.ref, self.half = ref, slice(None) if half is None else half
        self.span = slice(offset, offset + rows)
        self.rows = rows * (2 if half is None else 1)
        self.size = ref.shape[0] * self.rows

    def columns(self, band):
        return self.ref[:, self.half, self.span, band].reshape(self.size, TILE)

    def chips(self, band):
        return slice(band.start // self.rows, band.stop // self.rows)

    def band(self, band):
        return self.ref[self.chips(band), self.half, self.span, :].reshape(TILE, -1)

    def store(self, band, value):
        place = (self.chips(band), self.half, self.span)
        self.ref[place] = value.reshape(self.ref[place].shape)


def call(name, body, tables, ins, far, outs, far_outs, scratch):
    counts = [len(group) for group in (tables, ins, far, outs, far_outs, scratch)]

    def kernel(*refs):
        groups = []
        for count in counts:
            groups.append(refs[:count])
            refs = refs[count:]
        body(*groups)

    def spec(space, count):
        return [pl.BlockSpec(memory_space=space)] * count

    return pl.pallas_call(
        kernel,
        in_specs=spec(pltpu.SMEM, counts[0]) + spec(pltpu.VMEM, counts[1]) + spec(pl.ANY, counts[2]),
        out_specs=spec(pltpu.VMEM, counts[3]) + spec(pl.ANY, counts[4]),
        out_shape=[jax.ShapeDtypeStruct(*item) for item in (*outs, *far_outs)],
        scratch_shapes=scratch,
        compiler_params=pltpu.CompilerParams(vmem_limit_bytes=60 << 20),
        cost_estimate=pl.CostEstimate(flops=1, bytes_accessed=1, transcendentals=0),
        name=name,
    )(*tables, *ins, *far)


def fetch(tables, pieces, offset, target, sem, only=None):
    (table,) = tables
    core = table[0, 0]
    count = len(pieces) // 2

    def start(group, line, half):
        blocks = [piece.at[number] for piece in group for number in range(piece.shape[0])]
        for index, block in enumerate(blocks):
            pltpu.make_async_copy(
                block.at[pl.ds(offset, target.shape[2])], target.at[table[line, index], half], sem
            ).start()

    for group, line, half in ((pieces[:count], 1, core), (pieces[count:], 2, 1 - core)):
        if only is None:
            start(group, line, half)
        else:
            pl.when(half == only)(lambda: start(group, line, 0))


def fetched(target, sem):
    pltpu.make_async_copy(target, target, sem).wait()


def send_off(tables, grads, kept, sent, sems):
    (table,) = tables
    core = table[0, 0]
    for out, line, half, sem in (
        (sent, 4, 1 - core, sems[1]),
        (kept, 3, core, sems[0]),
    ):
        for position in range(out.shape[0]):
            pltpu.make_async_copy(grads.at[table[line, position], half], out.at[position], sem).start()


def sent_off(kept, sent, sems):
    for out, sem in zip((kept, sent), sems):
        pltpu.make_async_copy(out, out, sem).wait()


def spread_hidden(features, weight, bias, picking, hidden, slope, outgoing):
    for band in bands(weight.size):
        value, bent = gelu_pair(dot(features[...], weight.columns(band)) + bias[:, band])
        hidden[:, band] = low(value)
        slope[:, band] = low(bent)
        outgoing[:, band] = low(dot(picking[...], low(value)))


def average(mixes, hidden, other, incoming, mean):
    own, sib, far = mixes
    for band in bands(mean.shape[1]):
        mean[:, band] = low(
            dot(own[...], hidden[:, band])
            + dot(sib[...], other[:, band])
            + dot(far[...], incoming[:, band])
        )


def lane_sums(value):
    return sum(value[:, begin : begin + 128] for begin in range(0, value.shape[1], 128))


def combine(features, mean, own, neigh, bias, gated, unit, slope, scale):
    width = features.shape[1]
    squares = 0.0
    for band in bands(width):
        pre = dot(features[...], own.columns(band)) + dot(mean[...], neigh.columns(band))
        value, bent = gelu_pair(pre + bias[:, band])
        gated[:, band] = value
        slope[:, band] = low(bent)
        squares = squares + lane_sums(value * value)
    total = jnp.sum(squares, axis=1, keepdims=True)
    scale[...] = lax.rsqrt(total * (1.0 / width) + 1e-06)
    for band in bands(width):
        unit[:, band] = low(gated[:, band] * scale[...])


def perceive(unit, first, first_bias, inner, slope):
    for band in bands(first.size):
        value, bent = gelu_pair(dot(unit[...], first.columns(band)) + first_bias[:, band])
        inner[:, band] = low(value)
        slope[:, band] = low(bent)


def conclude(inner, second, second_bias, result):
    for band in bands(second.size):
        result[:, band] = low(dot(inner[...], second.columns(band)) + second_bias[:, band])


def weight_grad(left, right, grad):
    for band in bands(left.shape[1]):
        grad.store(band, low(dot_left(left[:, band], right[...])))


def column_sums(value, sums, row):
    for band in bands(value.shape[1]):
        sums[row : row + 1, band] = jnp.sum(wide(value[:, band]), axis=0, keepdims=True)


def back_perceive(grad_result, second, slope, grad_inner):
    for band in bands(second.size):
        grad_inner[:, band] = low(dot_right(grad_result[...], second.band(band)) * wide(slope[:, band]))


def back_unit(grad_inner, first, unit, scale, slope, grad_unit, grad_pre):
    width = unit.shape[1]
    products = 0.0
    for band in bands(width):
        value = dot_right(grad_inner[...], first.band(band))
        grad_unit[:, band] = value
        products = products + lane_sums(value * wide(unit[:, band]))
    mean_dot = jnp.sum(products, axis=1, keepdims=True) * (1.0 / width)
    for band in bands(width):
        value = scale[...] * (grad_unit[:, band] - wide(unit[:, band]) * mean_dot)
        grad_pre[:, band] = low(value * wide(slope[:, band]))


def back_mean(grad_pre, neigh, mix_turned, grad_mean, far_out, sib_out):
    sib, far = mix_turned
    for band in bands(grad_mean.shape[1]):
        value = low(dot_right(grad_pre[...], neigh.band(band)))
        grad_mean[:, band] = value
        far_out[:, band] = low(dot(far[...], value))
        sib_out[:, band] = low(dot(sib[...], value))


def back_hidden(own, pick, grad_mean, sib_back, far_back, slope, grad_hidden_pre):
    for band in bands(grad_mean.shape[1]):
        value = dot(own[...], grad_mean[:, band]) + dot(pick[...], far_back[:, band])
        value = value + wide(sib_back[:, band])
        grad_hidden_pre[:, band] = low(value * wide(slope[:, band]))


def back_input(grad_self, grad_hidden_pre, weight, grad_input):
    for band in bands(grad_input.shape[1]):
        grad_input[:, band] = low(
            wide(grad_self[:, band]) + dot_right(grad_hidden_pre[...], weight.band(band))
        )


def mix_rows(neighbours, counts, spans, so_far, begin, end):
    node_count, count = neighbours.shape
    block = 16

    def kernel(index_ref, count_ref, *refs):
        outs = refs[-len(spans) :]
        index = index_ref[...]
        values = count_ref[...].astype(jnp.float32)
        shares = values / jnp.sum(values, axis=1, keepdims=True)
        for number, ((first, last), out_ref) in enumerate(zip(spans, outs)):
            column = first + lax.broadcasted_iota(jnp.int32, (block, last - first), 1)
            total = jnp.zeros((block, last - first), jnp.float32)
            far = number == len(spans) - 1
            for k in range(count // 2 if far else 0, count if far else count // 2):
                total = jnp.where(index[:, k : k + 1] == column, shares[:, k : k + 1], total)
            out_ref[...] = total.astype(LOW)

    start = begin // block
    rows = lambda n: (n + start, 0)
    shapes = [jax.ShapeDtypeStruct((node_count, last - first), LOW) for first, last in spans]
    return pl.pallas_call(
        kernel,
        grid=((end - begin) // block,),
        in_specs=[pl.BlockSpec((block, count), rows)] * 2
        + [pl.BlockSpec(memory_space=pl.ANY)] * len(so_far),
        out_specs=[pl.BlockSpec((block, last - first), rows) for first, last in spans],
        out_shape=shapes,
        input_output_aliases={2 + n: n for n in range(len(so_far))},
        cost_estimate=pl.CostEstimate(flops=1, bytes_accessed=1, transcendentals=0),
        name="mixing",
    )(neighbours, counts, *so_far)


def local(
    pin_features,
    board_features,
    node_kinds,
    neighbours,
    visit_counts,
    served_rows,
    board_proj,
    neigh_weight,
    neigh_bias,
    concat_weight,
    concat_bias,
    mlp_weight_one,
    mlp_bias_one,
    mlp_weight_two,
    mlp_bias_two,
    out_grad,
):
    slice_rows, width = pin_features.shape
    board_width = board_features.shape[1]
    peers, slots = served_rows.shape
    near_rows, far_rows = 2 * slice_rows, peers * slots
    layout = Layout(peers)
    row, core = lax.axis_index("rows"), lax.axis_index("half")
    device = row * 2 + core
    biases = jnp.concatenate([neigh_bias, concat_bias, mlp_bias_one, mlp_bias_two])
    bias_count, own_bias = biases.shape
    lane = lax.broadcasted_iota(jnp.int32, (bias_count, width), 1)
    bias_rows = jnp.where(lane // own_bias == device, jnp.tile(biases, (1, width // own_bias)), 0.0)
    halves = concat_weight[:, 0]
    proj_rows, rows, half_rows = board_proj.shape[0], neigh_weight.shape[1], halves.shape[1]

    turned = jnp.where(
        neighbours < near_rows, (neighbours + near_rows - core * slice_rows) % near_rows, neighbours
    )
    spans = ((0, slice_rows), (slice_rows, near_rows), (near_rows, near_rows + far_rows))
    mixing = []

    def mix_more(part):
        size = slice_rows // 4
        return mix_rows(turned, visit_counts, spans, mixing, part * size, (part + 1) * size)

    served = served_rows.reshape(-1)
    node = lax.broadcasted_iota(jnp.int32, (far_rows, slice_rows), 1)
    picking = (served[:, None] == node).astype(LOW)
    node = lax.broadcasted_iota(jnp.int32, (slice_rows, far_rows), 0)
    pick_turned = (served[None, :] == node).astype(LOW)
    kinds = node_kinds[:, None]

    zero = Gather(layout, [board_proj, neigh_weight[0], bias_rows])
    one = Gather(layout, [halves[0], mlp_weight_one[0], mlp_weight_two[0], neigh_weight[1]])
    two = Gather(layout, [halves[1], mlp_weight_one[1], mlp_weight_two[1]])

    slots_out = [(k, j, i) for j in range(2) for k in range(layout.deep) for i in range(2)]

    def tables(chain):
        return [layout.orders(row, core, chain.order(), slots_out)]

    nodes_low = ((slice_rows, width), LOW)
    nodes_wide = ((slice_rows, width), jnp.float32)
    far_low = ((far_rows, width), LOW)
    column = ((slice_rows, 1), jnp.float32)
    sum_rows = ((8, width), jnp.float32)
    blocks = lambda count: pltpu.VMEM((layout.rows, 2, count, width), LOW)
    half_blocks = pltpu.VMEM((layout.rows, 1, half_rows, width), LOW)
    own_nodes = pltpu.VMEM(*nodes_low)
    own_wide = pltpu.VMEM(*nodes_wide)
    own_column = pltpu.VMEM(*column)
    dma = pltpu.SemaphoreType.DMA

    def leaving(count):
        return [((layout.rows, count, width), LOW)] * 2

    def exchange(outgoing):
        far = lax.all_to_all(
            outgoing.reshape(peers, slots, width), "rows", split_axis=0, concat_axis=0, tiled=True
        )
        return far.reshape(far_rows, width)

    def bias_part(blocks):
        return sum(jnp.sum(wide(item[:, proj_rows + rows :]), 0) for item in blocks)

    depths = range(1, layout.deep)
    zero.deepen(*depths)
    one.ahead(0)
    mixing = tie([zero, one], mix_more(0))
    zero.join(0)
    zero.ahead(0)
    one.deepen(*depths[:1])
    one.aside(0)
    mixing, picking, kinds = tie([zero, one], mix_more(1), picking, kinds)
    zero.aside(0)
    zero.swap(0)
    two.ahead(0)
    one.deepen(*depths[1:2])
    mixing = tie([zero, one, two], mix_more(2))
    zero.swap_far(0)
    two.aside(0)
    one.deepen(*depths[2:])
    two.deepen(*depths[:1])
    bias_full = bias_part(zero.levels + zero.squares + zero.near)
    mixing, bias_full = tie([zero, one, two], mix_more(3), bias_full)
    bias_full = bias_full + bias_part(zero.far)
    one.join(1)

    def hidden_body(tables, ins, pieces, outs, _, scratch):
        pin, board, kinds, bias, picking = ins
        features, hidden, slope, outgoing, proj_out = outs
        weights, sems = scratch
        fetch(tables, pieces, 0, weights, sems.at[0])
        fetched(weights, sems.at[0])
        proj, weight = View(weights, 0, proj_rows), View(weights, proj_rows, rows)
        for band in bands(width):
            projected = dot(board[...], proj.columns(band))
            features[:, band] = low(jnp.where(kinds[...] == 1, wide(pin[:, band]), projected))
        for band in bands(board_width):
            proj_out[band, :] = proj.band(band)
        spread_hidden(features, weight, bias.at[0:1], picking, hidden, slope, outgoing)

    one.ahead(1)
    one.swap(0)
    one.swap_far(0)
    two.deepen(*depths[1:])
    features, hidden, hidden_slope, outgoing, proj_full = tie(
        [one, two],
        *call(
            "hidden",
            hidden_body,
            tables(zero),
            [pin_features, board_features, kinds, bias_full, picking],
            zero.pieces(),
            [nodes_low] * 3 + [far_low, ((board_width, width), LOW)],
            [],
            [blocks(proj_rows + rows), dma((1,))],
        ),
    )
    incoming, other = exchange(outgoing), swap_cores(hidden)
    one.aside(1)
    one.swap(1)
    two.join(1)
    two.ahead(1)
    two.swap(0)
    two.swap_far(0)
    incoming, other = tie([one, two], incoming, other)
    one.swap_far(1)
    tie([one])

    def middle_body(tables, ins, pieces, outs, _, scratch):
        mixes, (hidden, other, incoming, features, bias, picking) = ins[:3], ins[3:]
        mean, unit, slope_pre, scale, inner, slope_inner, result, ahead, slope_ahead, outgoing = outs
        both, rest, gated, sems = scratch
        fetch(tables, pieces, 0, both, sems.at[0])
        fetch(tables, pieces, half_rows, rest, sems.at[1])
        first, second, weight = (View(rest, n * rows, rows) for n in range(3))
        own, neigh = (View(both, 0, half_rows, half) for half in range(2))
        average(mixes, hidden, other, incoming, mean)
        fetched(both, sems.at[0])
        combine(features, mean, own, neigh, bias.at[2:3], gated, unit, slope_pre, scale)
        fetched(rest, sems.at[1])
        perceive(unit, first, bias.at[4:5], inner, slope_inner)
        conclude(inner, second, bias.at[6:7], result)
        spread_hidden(result, weight, bias.at[1:2], picking, ahead, slope_ahead, outgoing)

    two.aside(1)
    two.swap(1)
    (
        mean_zero,
        unit,
        slope_pre,
        scale,
        inner,
        slope_inner,
        features_one,
        hidden_one,
        hidden_slope_one,
        outgoing,
    ) = tie(
        [two],
        *call(
            "middle",
            middle_body,
            tables(one),
            [*mixing, hidden, other, incoming, features, bias_full, picking],
            one.pieces(),
            [nodes_low] * 3 + [column] + [nodes_low] * 5 + [far_low],
            [],
            [blocks(half_rows), blocks(3 * rows), own_wide, dma((2,))],
        ),
    )
    incoming, other = exchange(outgoing), swap_cores(hidden_one)
    two.swap_far(1)
    mix_turned = [item.T for item in mixing]
    incoming, other, mix_turned = tie([two], incoming, other, mix_turned)

    def top_body(tables, ins, pieces, outs, leave, scratch):
        mixes, (hidden, other, incoming, features, bias, grad_result) = ins[:3], ins[3:]
        mean, result, unit, slope_pre, scale, grad_inner, sums = outs
        weights, grads, gated, inner, slope_inner, sems = scratch
        fetch(tables, pieces, 0, weights, sems.at[0])
        own, neigh = (View(weights, 0, half_rows, half) for half in range(2))
        first, second = View(weights, half_rows, rows), View(weights, half_rows + rows, rows)
        average(mixes, hidden, other, incoming, mean)
        fetched(weights, sems.at[0])
        combine(features, mean, own, neigh, bias.at[3:4], gated, unit, slope_pre, scale)
        perceive(unit, first, bias.at[5:6], inner, slope_inner)
        weight_grad(inner, grad_result, View(grads, 0, rows))
        back_perceive(grad_result, second, slope_inner, grad_inner)
        weight_grad(unit, grad_inner, View(grads, rows, rows))
        send_off(tables, grads, *leave, (sems.at[1], sems.at[2]))
        conclude(inner, second, bias.at[7:8], result)
        sums[...] = jnp.zeros_like(sums)
        column_sums(grad_result, sums, 0)
        column_sums(grad_inner, sums, 1)
        sent_off(*leave, (sems.at[1], sems.at[2]))

    mean_one, embeddings, unit_one, slope_pre_one, scale_one, grad_inner, sums_one, kept, sent = call(
        "top",
        top_body,
        tables(two),
        [*mixing, hidden_one, other, incoming, features_one, bias_full, out_grad],
        two.pieces(),
        [nodes_low] * 4 + [column, nodes_low, sum_rows],
        leaving(2 * rows),
        [blocks(half_rows + 2 * rows), blocks(2 * rows), own_wide, own_nodes, own_nodes, dma((3,))],
    )
    five = Scatter(layout, kept, sent)

    def norm_body(tables, ins, pieces, outs, _, scratch):
        grad_inner, unit, scale, slope_pre, *mix_turned = ins
        grad_pre, grad_mean, far_out, sib_out, sums = outs
        weights, halves, grad_unit, sems = scratch
        fetch(tables, pieces, half_rows, weights, sems.at[0])
        fetch(tables, pieces, 0, halves, sems.at[1], 1)
        fetched(weights, sems.at[0])
        first = View(weights, 0, rows)
        back_unit(grad_inner, first, unit, scale, slope_pre, grad_unit, grad_pre)
        fetched(halves, sems.at[1])
        neigh = View(halves, 0, half_rows, 0)
        back_mean(grad_pre, neigh, mix_turned, grad_mean, far_out, sib_out)
        sums[...] = jnp.zeros_like(sums)
        column_sums(grad_pre, sums, 0)

    def norm(name, chain, *ins):
        return call(
            name,
            norm_body,
            tables(chain),
            [*ins, *mix_turned[1:]],
            chain.pieces(),
            [nodes_low] * 2 + [far_low, nodes_low, sum_rows],
            [],
            [blocks(rows), half_blocks, own_wide, dma((2,))],
        )

    def sides(name, chain, features, mean, grad_pre):
        def body(tables, ins, pieces, outs, leave, scratch):
            features, mean, grad_pre = ins
            both, grads, sems = scratch
            fetch(tables, pieces, 0, both, sems.at[0], 0)
            weight_grad(features, grad_pre, View(grads, 0, half_rows, 0))
            weight_grad(mean, grad_pre, View(grads, 0, half_rows, 1))
            send_off(tables, grads, *leave, (sems.at[1], sems.at[2]))
            fetched(both, sems.at[0])
            own = View(both, 0, half_rows, 0)
            for band in bands(width):
                outs[0][:, band] = low(dot_right(grad_pre[...], own.band(band)))
            sent_off(*leave, (sems.at[1], sems.at[2]))

        return call(
            name,
            body,
            tables(chain),
            [features, mean, grad_pre],
            chain.pieces(),
            [nodes_low],
            leaving(half_rows),
            [half_blocks, blocks(half_rows), dma((3,))],
        )

    five.advance()
    grad_pre, grad_mean, far_out, sib_out, sums_pre_one = tie(
        [five], *norm("norm1", two, grad_inner, unit_one, scale_one, slope_pre_one)
    )
    five.advance()
    far_back, sib_back = exchange(far_out), swap_cores(sib_out)
    grad_self, kept, sent = sides("sides1", two, features_one, mean_one, grad_pre)
    far_back, sib_back, grad_self, kept, sent = tie([five], far_back, sib_back, grad_self, kept, sent)
    six = Scatter(layout, kept, sent)

    def bridge_body(tables, ins, pieces, outs, leave, scratch):
        own, pick, grad_mean, sib_back, far_back, slope_hidden, features, grad_self = ins[:8]
        inner, unit, slope_inner = ins[8:]
        grad_inner, sums = outs
        weights, grads, grad_hidden_pre, grad_input, sems = scratch
        fetch(tables, pieces, half_rows + rows, weights, sems.at[0])
        back_hidden(own, pick, grad_mean, sib_back, far_back, slope_hidden, grad_hidden_pre)
        weight_grad(features, grad_hidden_pre, View(grads, 0, rows))
        fetched(weights, sems.at[0])
        back_input(grad_self, grad_hidden_pre, View(weights, rows, rows), grad_input)
        weight_grad(inner, grad_input, View(grads, rows, rows))
        back_perceive(grad_input, View(weights, 0, rows), slope_inner, grad_inner)
        weight_grad(unit, grad_inner, View(grads, 2 * rows, rows))
        send_off(tables, grads, *leave, (sems.at[1], sems.at[2]))
        sums[...] = jnp.zeros_like(sums)
        column_sums(grad_hidden_pre, sums, 0)
        column_sums(grad_input, sums, 1)
        column_sums(grad_inner, sums, 2)
        sent_off(*leave, (sems.at[1], sems.at[2]))

    five.advance()
    six.advance()
    grad_inner, sums_zero, kept, sent = tie(
        [five, six],
        *call(
            "bridge",
            bridge_body,
            tables(one),
            [mix_turned[0], pick_turned, grad_mean, sib_back, far_back, hidden_slope_one]
            + [features_one, grad_self, inner, unit, slope_inner],
            one.pieces(),
            [nodes_low, sum_rows],
            leaving(3 * rows),
            [blocks(2 * rows), blocks(3 * rows), own_nodes, own_nodes, dma((3,))],
        ),
    )
    seven = Scatter(layout, kept, sent)
    five.advance()
    six.advance()
    seven.advance()
    grad_pre, grad_mean, far_out, sib_out, sums_pre_zero = tie(
        [five, six, seven], *norm("norm0", one, grad_inner, unit, scale, slope_pre)
    )
    seven.advance()
    far_back, sib_back = exchange(far_out), swap_cores(sib_out)
    grad_self, kept, sent = sides("sides0", one, features, mean_zero, grad_pre)
    far_back, sib_back, grad_self, kept, sent = tie(
        [six, seven], far_back, sib_back, grad_self, kept, sent
    )
    eight = Scatter(layout, kept, sent)

    def bottom_body(tables, ins, pieces, outs, leave, scratch):
        own, pick, grad_mean, sib_back, far_back, slope_hidden, features, grad_self = ins[:8]
        board, kinds, sums_one, pre_one, sums_zero, pre_zero = ins[8:]
        (grad_input,) = outs
        weights, grads, grad_hidden_pre, grad_board, sums, sems = scratch
        fetch(tables, pieces, proj_rows, weights, sems.at[0])
        back_hidden(own, pick, grad_mean, sib_back, far_back, slope_hidden, grad_hidden_pre)
        weight_grad(features, grad_hidden_pre, View(grads, 0, rows))
        column_sums(grad_hidden_pre, sums, 0)
        fetched(weights, sems.at[0])
        back_input(grad_self, grad_hidden_pre, View(weights, 0, rows), grad_input)
        for band in bands(width):
            grad_board[:, band] = low(jnp.where(kinds[...] == 1, 0.0, wide(grad_input[:, band])))
        weight_grad(board, grad_board, View(grads, rows, proj_rows))
        totals = [sums[0:1, :], sums_zero[0:1, :], pre_zero[0:1, :], pre_one[0:1, :]]
        totals += [sums_zero[2:3, :], sums_one[1:2, :], sums_zero[1:2, :], sums_one[0:1, :]]
        totals = low(jnp.concatenate([*totals, jnp.zeros((8, width), jnp.float32)]))
        for chip in range(layout.rows):
            for half in range(2):
                grads[chip, half, rows + proj_rows :, :] = totals
        send_off(tables, grads, *leave, (sems.at[1], sems.at[2]))
        sent_off(*leave, (sems.at[1], sems.at[2]))

    six.advance()
    seven.advance()
    eight.advance()
    grad_input, kept, sent = tie(
        [six, seven, eight],
        *call(
            "bottom",
            bottom_body,
            tables(zero),
            [mix_turned[0], pick_turned, grad_mean, sib_back, far_back, hidden_slope, features]
            + [grad_self, board_features, kinds, sums_one, sums_pre_one, sums_zero, sums_pre_zero],
            zero.pieces(),
            [nodes_low],
            leaving(rows + proj_rows + 16),
            [blocks(rows), blocks(rows + proj_rows + 16), own_nodes, own_nodes]
            + [pltpu.VMEM(*sum_rows), dma((3,))],
        ),
    )
    nine = Scatter(layout, kept, sent)
    chains = [five, six, seven, eight, nine]
    eight.advance()
    nine.advance()
    six.advance()
    tie([nine])
    nine.advance()
    tie([eight, six])
    eight.advance()
    seven.advance()
    tie([nine, eight, seven])
    nine.advance()
    eight.advance()
    tie([nine])
    nine.advance()
    is_pin = kinds == 1
    pin_grad = jnp.where(is_pin, wide(grad_input), 0.0)
    grad_board = jnp.where(is_pin, jnp.zeros_like(grad_input), grad_input)
    board_grad = dot_right(grad_board, proj_full)

    five, six, seven, eight, nine = (chain.result() for chain in chains)
    bias_sums = nine[rows + proj_rows :][:bias_count]
    bias_sums = lax.dynamic_slice_in_dim(bias_sums, device * own_bias, own_bias, 1)
    bias_sums = bias_sums.reshape(4, -1, own_bias)
    return (
        embeddings,
        pin_grad,
        board_grad,
        nine[rows : rows + proj_rows],
        jnp.stack([nine[:rows], seven[:rows]]),
        bias_sums[0],
        jnp.stack([eight, six])[:, None],
        bias_sums[1],
        jnp.stack([seven[2 * rows :], five[rows:]]),
        bias_sums[2],
        jnp.stack([seven[rows : 2 * rows], five[:rows]]),
        bias_sums[3],
    )


def solution(mesh):
    nodes = P(("rows", "half"), None)
    weight = P(None, ("rows", "half"), None)
    bias = P(None, ("rows", "half"))
    concat = P(None, "half", "rows", None)
    placed = (nodes, nodes, P(("rows", "half")), nodes, nodes, nodes, nodes)
    placed += (weight, bias, concat, bias, weight, bias, weight, bias, nodes)
    results = (nodes, nodes, nodes, nodes) + (weight, bias, concat, bias, weight, bias, weight, bias)

    def whole(*args):
        devices = mesh.shape["rows"] * mesh.shape["half"]
        shards = (args[6].shape[0] // devices, args[7].shape[1] // devices)
        fits = mesh.shape["rows"] % 4 == 0 and not any(count % 16 for count in shards)
        return jax.shard_map(
            local if fits else plain,
            mesh=mesh,
            in_specs=placed,
            out_specs=results,
            check_vma=False,
        )(*args)

    return whole
```

```python
import jax
import jax.numpy as jnp
from jax import lax
from jax.experimental import pallas as pl
from jax.experimental.pallas import tpu as pltpu
from jax.sharding import PartitionSpec as P

LOW = jnp.bfloat16
AXES = ("rows", "half")
CURVE = 0.7978845608028654
CUBIC = 0.044715
TILE = 256


def activate(value):
    return jax.nn.gelu(value, approximate=True)


def unit_map(value):
    scaled = activate(value)
    return scaled * lax.rsqrt(jnp.mean(scaled * scaled, axis=-1, keepdims=True) + 1e-06)


def matmul(left, right):
    return jnp.dot(left, right, preferred_element_type=jnp.float32)


def column_sum(value):
    return jnp.sum(value.astype(jnp.float32), axis=0)


def fetch_shared(
    neigh_weight, neigh_bias, concat_bias, weight_one, bias_one, weight_two, bias_two, board_proj
):
    return (
        lax.all_gather(neigh_weight, ("rows", "half"), axis=1, tiled=True),
        lax.all_gather(neigh_bias, ("rows", "half"), axis=1, tiled=True),
        lax.all_gather(concat_bias, ("rows", "half"), axis=1, tiled=True),
        lax.all_gather(weight_one, ("rows", "half"), axis=1, tiled=True),
        lax.all_gather(bias_one, ("rows", "half"), axis=1, tiled=True),
        lax.all_gather(weight_two, ("rows", "half"), axis=1, tiled=True),
        lax.all_gather(bias_two, ("rows", "half"), axis=1, tiled=True),
        lax.all_gather(board_proj, ("rows", "half"), axis=0, tiled=True),
    )


def fetch_half(own_half):
    return lax.all_gather(own_half, "rows", axis=1, tiled=True)


def refetch_shared(
    neigh_weight, neigh_bias, concat_bias, weight_one, bias_one, weight_two, bias_two, board_proj
):
    return (
        lax.all_gather(neigh_weight, ("rows", "half"), axis=1, tiled=True),
        lax.all_gather(neigh_bias, ("rows", "half"), axis=1, tiled=True),
        lax.all_gather(concat_bias, ("rows", "half"), axis=1, tiled=True),
        lax.all_gather(weight_one, ("rows", "half"), axis=1, tiled=True),
        lax.all_gather(bias_one, ("rows", "half"), axis=1, tiled=True),
        lax.all_gather(weight_two, ("rows", "half"), axis=1, tiled=True),
        lax.all_gather(bias_two, ("rows", "half"), axis=1, tiled=True),
        lax.all_gather(board_proj, ("rows", "half"), axis=0, tiled=True),
    )


def refetch_half(own_half):
    return lax.all_gather(own_half, "rows", axis=1, tiled=True)


def plain(
    pin_features,
    board_features,
    node_kinds,
    neighbours,
    visit_counts,
    served_rows,
    board_proj,
    neigh_weight,
    neigh_bias,
    concat_weight,
    concat_bias,
    mlp_weight_one,
    mlp_bias_one,
    mlp_weight_two,
    mlp_bias_two,
    out_grad,
):
    slice_rows, feature_width = pin_features.shape
    layer_count = neigh_weight.shape[0]
    peer_count, slot_count = served_rows.shape
    chip_rows = 2 * slice_rows
    table_rows = chip_rows + peer_count * slot_count
    counts = visit_counts.astype(jnp.float32)
    shares = (counts / jnp.sum(counts, axis=1, keepdims=True)).astype(jnp.bfloat16)
    positions = jnp.broadcast_to(jnp.arange(slice_rows, dtype=jnp.int32)[:, None], neighbours.shape)
    mixing = jnp.zeros((slice_rows, table_rows), jnp.bfloat16).at[positions, neighbours].set(shares)
    served_flat = served_rows.reshape(-1)
    is_pin = (node_kinds == 1)[:, None]
    to_low = jnp.bfloat16
    master_pieces = (
        neigh_weight.astype(to_low),
        neigh_bias.astype(to_low),
        concat_bias.astype(to_low),
        mlp_weight_one.astype(to_low),
        mlp_bias_one.astype(to_low),
        mlp_weight_two.astype(to_low),
        mlp_bias_two.astype(to_low),
        board_proj.astype(to_low),
    )
    own_half = concat_weight[:, 0].astype(to_low)
    shared_full = fetch_shared(*master_pieces)
    half_full = fetch_half(own_half)
    (
        neigh_full,
        nbias_full,
        cbias_full,
        first_full,
        fbias_full,
        second_full,
        sbias_full,
        proj_full,
    ) = shared_full
    projected = matmul(board_features, proj_full)
    features = jnp.where(is_pin, pin_features.astype(jnp.float32), projected).astype(to_low)
    saved = []
    result = None
    for layer_index in range(layer_count):
        hidden_pre = matmul(features, neigh_full[layer_index]) + nbias_full[layer_index].astype(
            jnp.float32
        )
        hidden_full, hidden_pull = jax.vjp(activate, hidden_pre)
        hidden = hidden_full.astype(to_low)
        chip_hidden = lax.all_gather(hidden, "half", axis=0, tiled=True)
        outgoing = hidden[served_rows]
        incoming = lax.all_to_all(outgoing, "rows", split_axis=0, concat_axis=0, tiled=True)
        lookup_table = jnp.concatenate([chip_hidden, incoming.reshape(-1, feature_width)], axis=0)
        neigh_mean = matmul(mixing, lookup_table).astype(to_low)
        paired = lax.all_to_all(
            jnp.stack([features, neigh_mean]), "half", split_axis=0, concat_axis=1, tiled=True
        )[0]
        partial_value = matmul(paired, half_full[layer_index])
        pre_sum = lax.psum_scatter(
            partial_value.astype(jnp.bfloat16), "half", scatter_dimension=0, tiled=True
        ).astype(jnp.float32) + cbias_full[layer_index].astype(jnp.float32)
        unit_full, unit_pull = jax.vjp(unit_map, pre_sum)
        unit_rows = unit_full.astype(to_low)
        inner_pre = matmul(unit_rows, first_full[layer_index]) + fbias_full[layer_index].astype(
            jnp.float32
        )
        inner_full, inner_pull = jax.vjp(activate, inner_pre)
        inner_act = inner_full.astype(to_low)
        result = matmul(inner_act, second_full[layer_index]) + sbias_full[layer_index].astype(
            jnp.float32
        )
        saved.append((features, hidden_pull, paired, unit_rows, unit_pull, inner_act, inner_pull))
        features = result.astype(to_low)
    embeddings = result.astype(to_low)
    (
        neigh_full,
        nbias_full,
        cbias_full,
        first_full,
        fbias_full,
        second_full,
        sbias_full,
        proj_full,
    ) = refetch_shared(*master_pieces)
    half_full = refetch_half(own_half)
    grad_result = out_grad
    grads_neigh = [None] * layer_count
    grads_nbias = [None] * layer_count
    grads_half = [None] * layer_count
    grads_cbias = [None] * layer_count
    grads_first = [None] * layer_count
    grads_fbias = [None] * layer_count
    grads_second = [None] * layer_count
    grads_sbias = [None] * layer_count
    grad_input = None
    for layer_index in reversed(range(layer_count)):
        features, hidden_pull, paired, unit_rows, unit_pull, inner_act, inner_pull = saved[
            layer_index
        ]
        grads_second[layer_index] = matmul(inner_act.T, grad_result)
        grads_sbias[layer_index] = column_sum(grad_result)
        grad_inner = inner_pull(matmul(grad_result, second_full[layer_index].T))[0].astype(to_low)
        grads_first[layer_index] = matmul(unit_rows.T, grad_inner)
        grads_fbias[layer_index] = column_sum(grad_inner)
        grad_pre = unit_pull(matmul(grad_inner, first_full[layer_index].T))[0].astype(to_low)
        grads_cbias[layer_index] = column_sum(grad_pre)
        grad_pre_full = lax.all_gather(grad_pre, "half", axis=0, tiled=True)
        grads_half[layer_index] = matmul(paired.T, grad_pre_full)
        grad_paired = matmul(grad_pre_full, half_full[layer_index].T)
        returned = lax.all_to_all(
            grad_paired[None].astype(jnp.bfloat16), "half", split_axis=1, concat_axis=0, tiled=True
        ).astype(jnp.float32)
        grad_self = returned[0]
        grad_mean = returned[1].astype(to_low)
        grad_table = matmul(mixing.T, grad_mean)
        grad_chip = lax.psum_scatter(
            grad_table[:chip_rows].astype(jnp.bfloat16), "half", scatter_dimension=0, tiled=True
        ).astype(jnp.float32)
        grad_far = lax.all_to_all(
            grad_table[chip_rows:]
            .reshape(peer_count, slot_count, feature_width)
            .astype(jnp.bfloat16),
            "rows",
            split_axis=0,
            concat_axis=0,
            tiled=True,
        ).astype(jnp.float32)
        grad_hidden = grad_chip.at[served_flat].add(grad_far.reshape(-1, feature_width))
        grad_hidden_pre = hidden_pull(grad_hidden)[0].astype(to_low)
        grads_neigh[layer_index] = matmul(features.T, grad_hidden_pre)
        grads_nbias[layer_index] = column_sum(grad_hidden_pre)
        grad_input = (grad_self + matmul(grad_hidden_pre, neigh_full[layer_index].T)).astype(to_low)
        grad_result = grad_input
    pin_grad = jnp.where(is_pin, grad_input.astype(jnp.float32), 0.0)
    grad_board = jnp.where(is_pin, jnp.zeros_like(grad_input), grad_input)
    board_grad = matmul(grad_board, proj_full.T)
    proj_grad = matmul(board_features.T, grad_board)
    summed = (
        lax.psum_scatter(jnp.stack(grads_neigh), ("rows", "half"), scatter_dimension=1, tiled=True),
        lax.psum_scatter(jnp.stack(grads_nbias), ("rows", "half"), scatter_dimension=1, tiled=True),
        lax.psum_scatter(jnp.stack(grads_cbias), ("rows", "half"), scatter_dimension=1, tiled=True),
        lax.psum_scatter(jnp.stack(grads_first), ("rows", "half"), scatter_dimension=1, tiled=True),
        lax.psum_scatter(jnp.stack(grads_fbias), ("rows", "half"), scatter_dimension=1, tiled=True),
        lax.psum_scatter(
            jnp.stack(grads_second), ("rows", "half"), scatter_dimension=1, tiled=True
        ),
        lax.psum_scatter(jnp.stack(grads_sbias), ("rows", "half"), scatter_dimension=1, tiled=True),
        lax.psum_scatter(proj_grad, ("rows", "half"), scatter_dimension=0, tiled=True),
    )
    half_summed = lax.psum_scatter(jnp.stack(grads_half), "rows", scatter_dimension=1, tiled=True)
    (
        neigh_grad,
        nbias_grad,
        cbias_grad,
        first_grad,
        fbias_grad,
        second_grad,
        sbias_grad,
        board_proj_grad,
    ) = summed
    return (
        embeddings,
        pin_grad,
        board_grad,
        board_proj_grad,
        neigh_grad,
        nbias_grad,
        half_summed[:, None],
        cbias_grad,
        first_grad,
        fbias_grad,
        second_grad,
        sbias_grad,
    )


def low(value):
    return value.astype(LOW)


def wide(value):
    return value.astype(jnp.float32)


class Layout:
    def __init__(self, row_count):
        self.rows = row_count
        self.deep = row_count // 4
        self.sizes = (2, 2, self.deep)

    def split(self, row):
        return [row % 2, (row // 2) % 2, row // 4]

    def join(self, place):
        return place[0] + 2 * (place[1] + 2 * place[2])

    def ring(self, dims, value, step=1):
        pairs = []
        for row in range(self.rows):
            for core in range(2):
                place = self.split(row)
                dim = dims[core]
                place[dim] = (place[dim] + step) % self.sizes[dim]
                pairs.append((row * 2 + core, self.join(place) * 2 + core))
        return lax.ppermute(value, AXES, pairs)

    def first(self, value):
        return self.ring((0, 1), value)

    def last(self, value):
        return self.ring((1, 0), value)

    def middle(self, value, step=1):
        return self.ring((2, 2), value, step)

    def orders(self, row, core, slots_in, slots_out):
        slots = jnp.array([slots_in, slots_in, slots_in, slots_out, slots_out], jnp.int32)
        line = lax.broadcasted_iota(jnp.int32, slots.shape[:2], 0)
        whose = jnp.where(line % 2 == 1, core, 1 - core)
        sign = jnp.where(line < 3, -1, 1)
        place = self.split(row)
        k, j, i = (slots[:, :, part] for part in range(3))
        ahead, aside = jnp.where(whose == 0, i, j), jnp.where(whose == 0, j, i)
        middle = (place[2] + sign * k + self.deep) % self.deep
        order = self.join(((place[0] + ahead) % 2, (place[1] + aside) % 2, middle))
        return jnp.where(line == 0, core, order).astype(jnp.int32)


def swap_cores(value):
    return lax.ppermute(value, "half", [(0, 1), (1, 0)])


class Gather:
    def __init__(self, layout, parts):
        self.layout = layout
        self.own = low(jnp.concatenate(parts))[None]
        self.levels, self.slots = [self.own], [[(0, 0, 0)]]
        self.squares, self.near, self.far = [], [], []

    @property
    def values(self):
        return (self.own, self.levels, self.squares, self.near, self.far)

    @values.setter
    def values(self, held):
        self.own = held[0]
        self.levels, self.squares, self.near, self.far = (list(item) for item in held[1:])

    def deepen(self, *steps):
        for k in steps:
            self.levels.append(self.layout.middle(self.own, k))
            self.slots.append([(k, 0, 0)])

    def join(self, begin):
        self.levels[begin:] = [jnp.concatenate(self.levels[begin:])]
        self.slots[begin:] = [sum(self.slots[begin:], [])]

    def ahead(self, number):
        item = self.levels[number]
        self.levels[number] = jnp.concatenate([item, self.layout.first(item)])
        self.slots[number] = self.slots[number] + [(k, j, 1) for k, j, _ in self.slots[number]]

    def aside(self, number):
        self.squares.append(self.layout.last(self.levels[number]))

    def swap(self, number):
        self.near.append(swap_cores(self.levels[number]))

    def swap_far(self, number):
        self.far.append(swap_cores(self.squares[number]))

    def pieces(self):
        own = [item for pair in zip(self.levels, self.squares) for item in pair]
        return own + [item for pair in zip(self.near, self.far) for item in pair]

    def order(self):
        result = []
        for slots in self.slots:
            result += slots + [(k, 1, i) for k, _, i in slots]
        return result


class Scatter:
    def __init__(self, layout, kept, sent):
        self.layout = layout
        self.values = [kept, sent]
        self.plan = [self.swap, self.aside, self.ahead, self.deepen]
        self.shape = (layout.deep, 2, *kept.shape[1:])

    def advance(self):
        self.plan.pop(0)()

    def near(self, *index):
        kept, got, came = self.values[:3]
        half = (2, *self.shape)
        return (
            wide(kept.reshape(half)[(0, *index)])
            + wide(got.reshape(half)[(0, *index)])
            + wide(came.reshape(self.shape)[index])
        )

    def swap(self):
        self.values = [self.values[0], swap_cores(self.values[1])]

    def aside(self):
        kept, got = self.values
        half = self.layout.rows // 2
        self.values = [kept, got, self.layout.last(low(wide(kept[half:]) + wide(got[half:])))]

    def ahead(self):
        self.values = [*self.values, self.layout.first(low(self.near(slice(None), 1)))]

    def level(self, k):
        return self.near(k, 0) + wide(self.values[3][k])

    def deepen(self):
        far_first = sorted(range(1, self.layout.deep), key=lambda k: abs(2 * k - self.layout.deep))
        got = [self.layout.middle(low(self.level(k)), k) for k in far_first]
        self.values = [*self.values, *got]

    def result(self):
        return self.level(0) + sum(wide(item) for item in self.values[4:])


def tie(chains, *values):
    held, values = lax.optimization_barrier(([chain.values for chain in chains], values))
    for chain, item in zip(chains, held):
        chain.values = item
    return values[0] if len(values) == 1 else values


def dot(left, right):
    return jnp.dot(left, right, preferred_element_type=jnp.float32)


def dot_right(left, right):
    return lax.dot_general(
        left, right, (((1,), (1,)), ((), ())), preferred_element_type=jnp.float32
    )


def dot_left(left, right):
    return lax.dot_general(
        left, right, (((0,), (0,)), ((), ())), preferred_element_type=jnp.float32
    )


def gelu_pair(value):
    square = value * value
    bend = jnp.tanh(value * (CURVE + CURVE * CUBIC * square))
    half = 0.5 + 0.5 * bend
    slope = half + value * (0.5 - 0.5 * bend * bend) * (CURVE + 3.0 * CURVE * CUBIC * square)
    return value * half, slope


def bands(size):
    return [slice(begin, begin + TILE) for begin in range(0, size, TILE)]


class View:
    def __init__(self, ref, offset, rows, half=None):
        self.ref, self.half = ref, slice(None) if half is None else half
        self.span = slice(offset, offset + rows)
        self.rows = rows * (2 if half is None else 1)
        self.size = ref.shape[0] * self.rows

    def columns(self, band):
        return self.ref[:, self.half, self.span, band].reshape(self.size, TILE)

    def chips(self, band):
        return slice(band.start // self.rows, band.stop // self.rows)

    def band(self, band):
        return self.ref[self.chips(band), self.half, self.span, :].reshape(TILE, -1)

    def store(self, band, value):
        place = (self.chips(band), self.half, self.span)
        self.ref[place] = value.reshape(self.ref[place].shape)


def call(name, body, tables, ins, far, outs, far_outs, scratch):
    counts = [len(group) for group in (tables, ins, far, outs, far_outs, scratch)]

    def kernel(*refs):
        groups = []
        for count in counts:
            groups.append(refs[:count])
            refs = refs[count:]
        body(*groups)

    def spec(space, count):
        return [pl.BlockSpec(memory_space=space)] * count

    return pl.pallas_call(
        kernel,
        in_specs=spec(pltpu.SMEM, counts[0]) + spec(pltpu.VMEM, counts[1]) + spec(pl.ANY, counts[2]),
        out_specs=spec(pltpu.VMEM, counts[3]) + spec(pl.ANY, counts[4]),
        out_shape=[jax.ShapeDtypeStruct(*item) for item in (*outs, *far_outs)],
        scratch_shapes=scratch,
        compiler_params=pltpu.CompilerParams(vmem_limit_bytes=60 << 20),
        cost_estimate=pl.CostEstimate(flops=1, bytes_accessed=1, transcendentals=0),
        name=name,
    )(*tables, *ins, *far)


def fetch(tables, pieces, offset, target, sem, only=None):
    (table,) = tables
    core = table[0, 0]
    count = len(pieces) // 2

    def start(group, line, half):
        blocks = [piece.at[number] for piece in group for number in range(piece.shape[0])]
        for index, block in enumerate(blocks):
            pltpu.make_async_copy(
                block.at[pl.ds(offset, target.shape[2])], target.at[table[line, index], half], sem
            ).start()

    for group, line, half in ((pieces[:count], 1, core), (pieces[count:], 2, 1 - core)):
        if only is None:
            start(group, line, half)
        else:
            pl.when(half == only)(lambda: start(group, line, 0))


def fetched(target, sem):
    pltpu.make_async_copy(target, target, sem).wait()


def send_off(tables, grads, kept, sent, sems):
    (table,) = tables
    core = table[0, 0]
    for out, line, half, sem in (
        (sent, 4, 1 - core, sems[1]),
        (kept, 3, core, sems[0]),
    ):
        for position in range(out.shape[0]):
            pltpu.make_async_copy(grads.at[table[line, position], half], out.at[position], sem).start()


def sent_off(kept, sent, sems):
    for out, sem in zip((kept, sent), sems):
        pltpu.make_async_copy(out, out, sem).wait()


def spread_hidden(features, weight, bias, picking, hidden, slope, outgoing):
    for band in bands(weight.size):
        value, bent = gelu_pair(dot(features[...], weight.columns(band)) + bias[:, band])
        hidden[:, band] = low(value)
        slope[:, band] = low(bent)
        outgoing[:, band] = low(dot(picking[...], low(value)))


def average(mixes, hidden, other, incoming, mean):
    own, sib, far = mixes
    for band in bands(mean.shape[1]):
        mean[:, band] = low(
            dot(own[...], hidden[:, band])
            + dot(sib[...], other[:, band])
            + dot(far[...], incoming[:, band])
        )


def lane_sums(value):
    return sum(value[:, begin : begin + 128] for begin in range(0, value.shape[1], 128))


def combine(features, mean, own, neigh, bias, gated, unit, slope, scale):
    width = features.shape[1]
    squares = 0.0
    for band in bands(width):
        pre = dot(features[...], own.columns(band)) + dot(mean[...], neigh.columns(band))
        value, bent = gelu_pair(pre + bias[:, band])
        gated[:, band] = value
        slope[:, band] = low(bent)
        squares = squares + lane_sums(value * value)
    total = jnp.sum(squares, axis=1, keepdims=True)
    scale[...] = lax.rsqrt(total * (1.0 / width) + 1e-06)
    for band in bands(width):
        unit[:, band] = low(gated[:, band] * scale[...])


def perceive(unit, first, first_bias, inner, slope):
    for band in bands(first.size):
        value, bent = gelu_pair(dot(unit[...], first.columns(band)) + first_bias[:, band])
        inner[:, band] = low(value)
        slope[:, band] = low(bent)


def conclude(inner, second, second_bias, result):
    for band in bands(second.size):
        result[:, band] = low(dot(inner[...], second.columns(band)) + second_bias[:, band])


def weight_grad(left, right, grad):
    for band in bands(left.shape[1]):
        grad.store(band, low(dot_left(left[:, band], right[...])))


def column_sums(value, sums, row):
    for band in bands(value.shape[1]):
        sums[row : row + 1, band] = jnp.sum(wide(value[:, band]), axis=0, keepdims=True)


def back_perceive(grad_result, second, slope, grad_inner):
    for band in bands(second.size):
        grad_inner[:, band] = low(dot_right(grad_result[...], second.band(band)) * wide(slope[:, band]))


def back_unit(grad_inner, first, unit, scale, slope, grad_unit, grad_pre):
    width = unit.shape[1]
    products = 0.0
    for band in bands(width):
        value = dot_right(grad_inner[...], first.band(band))
        grad_unit[:, band] = value
        products = products + lane_sums(value * wide(unit[:, band]))
    mean_dot = jnp.sum(products, axis=1, keepdims=True) * (1.0 / width)
    for band in bands(width):
        value = scale[...] * (grad_unit[:, band] - wide(unit[:, band]) * mean_dot)
        grad_pre[:, band] = low(value * wide(slope[:, band]))


def back_mean(grad_pre, neigh, mix_turned, grad_mean, far_out, sib_out):
    sib, far = mix_turned
    for band in bands(grad_mean.shape[1]):
        value = low(dot_right(grad_pre[...], neigh.band(band)))
        grad_mean[:, band] = value
        far_out[:, band] = low(dot(far[...], value))
        sib_out[:, band] = low(dot(sib[...], value))


def back_hidden(own, pick, grad_mean, sib_back, far_back, slope, grad_hidden_pre):
    for band in bands(grad_mean.shape[1]):
        value = dot(own[...], grad_mean[:, band]) + dot(pick[...], far_back[:, band])
        value = value + wide(sib_back[:, band])
        grad_hidden_pre[:, band] = low(value * wide(slope[:, band]))


def back_input(grad_self, grad_hidden_pre, weight, grad_input):
    for band in bands(grad_input.shape[1]):
        grad_input[:, band] = low(
            wide(grad_self[:, band]) + dot_right(grad_hidden_pre[...], weight.band(band))
        )


def mix_rows(neighbours, counts, spans, so_far, begin, end):
    node_count, count = neighbours.shape
    block = 16

    def kernel(index_ref, count_ref, *refs):
        outs = refs[-len(spans) :]
        index = index_ref[...]
        values = count_ref[...].astype(jnp.float32)
        shares = values / jnp.sum(values, axis=1, keepdims=True)
        for number, ((first, last), out_ref) in enumerate(zip(spans, outs)):
            column = first + lax.broadcasted_iota(jnp.int32, (block, last - first), 1)
            total = jnp.zeros((block, last - first), jnp.float32)
            far = number == len(spans) - 1
            for k in range(count // 2 if far else 0, count if far else count // 2):
                total = jnp.where(index[:, k : k + 1] == column, shares[:, k : k + 1], total)
            out_ref[...] = total.astype(LOW)

    start = begin // block
    rows = lambda n: (n + start, 0)
    shapes = [jax.ShapeDtypeStruct((node_count, last - first), LOW) for first, last in spans]
    return pl.pallas_call(
        kernel,
        grid=((end - begin) // block,),
        in_specs=[pl.BlockSpec((block, count), rows)] * 2
        + [pl.BlockSpec(memory_space=pl.ANY)] * len(so_far),
        out_specs=[pl.BlockSpec((block, last - first), rows) for first, last in spans],
        out_shape=shapes,
        input_output_aliases={2 + n: n for n in range(len(so_far))},
        cost_estimate=pl.CostEstimate(flops=1, bytes_accessed=1, transcendentals=0),
        name="mixing",
    )(neighbours, counts, *so_far)


def local(
    pin_features,
    board_features,
    node_kinds,
    neighbours,
    visit_counts,
    served_rows,
    board_proj,
    neigh_weight,
    neigh_bias,
    concat_weight,
    concat_bias,
    mlp_weight_one,
    mlp_bias_one,
    mlp_weight_two,
    mlp_bias_two,
    out_grad,
):
    slice_rows, width = pin_features.shape
    board_width = board_features.shape[1]
    peers, slots = served_rows.shape
    near_rows, far_rows = 2 * slice_rows, peers * slots
    layout = Layout(peers)
    row, core = lax.axis_index("rows"), lax.axis_index("half")
    device = row * 2 + core
    biases = jnp.concatenate([neigh_bias, concat_bias, mlp_bias_one, mlp_bias_two])
    bias_count, own_bias = biases.shape
    lane = lax.broadcasted_iota(jnp.int32, (bias_count, width), 1)
    bias_rows = jnp.where(lane // own_bias == device, jnp.tile(biases, (1, width // own_bias)), 0.0)
    halves = concat_weight[:, 0]
    proj_rows, rows, half_rows = board_proj.shape[0], neigh_weight.shape[1], halves.shape[1]

    turned = jnp.where(
        neighbours < near_rows, (neighbours + near_rows - core * slice_rows) % near_rows, neighbours
    )
    spans = ((0, slice_rows), (slice_rows, near_rows), (near_rows, near_rows + far_rows))
    mixing = []

    def mix_more(part):
        size = slice_rows // 4
        return mix_rows(turned, visit_counts, spans, mixing, part * size, (part + 1) * size)

    served = served_rows.reshape(-1)
    node = lax.broadcasted_iota(jnp.int32, (far_rows, slice_rows), 1)
    picking = (served[:, None] == node).astype(LOW)
    node = lax.broadcasted_iota(jnp.int32, (slice_rows, far_rows), 0)
    pick_turned = (served[None, :] == node).astype(LOW)
    kinds = node_kinds[:, None]

    zero = Gather(layout, [board_proj, neigh_weight[0], bias_rows])
    one = Gather(layout, [halves[0], mlp_weight_one[0], mlp_weight_two[0], neigh_weight[1]])
    two = Gather(layout, [halves[1], mlp_weight_one[1], mlp_weight_two[1]])

    slots_out = [(k, j, i) for j in range(2) for k in range(layout.deep) for i in range(2)]

    def tables(chain):
        return [layout.orders(row, core, chain.order(), slots_out)]

    nodes_low = ((slice_rows, width), LOW)
    nodes_wide = ((slice_rows, width), jnp.float32)
    far_low = ((far_rows, width), LOW)
    column = ((slice_rows, 1), jnp.float32)
    sum_rows = ((8, width), jnp.float32)
    blocks = lambda count: pltpu.VMEM((layout.rows, 2, count, width), LOW)
    half_blocks = pltpu.VMEM((layout.rows, 1, half_rows, width), LOW)
    own_nodes = pltpu.VMEM(*nodes_low)
    own_wide = pltpu.VMEM(*nodes_wide)
    own_column = pltpu.VMEM(*column)
    dma = pltpu.SemaphoreType.DMA

    def leaving(count):
        return [((layout.rows, count, width), LOW)] * 2

    def exchange(outgoing):
        far = lax.all_to_all(
            outgoing.reshape(peers, slots, width), "rows", split_axis=0, concat_axis=0, tiled=True
        )
        return far.reshape(far_rows, width)

    def bias_part(blocks):
        return sum(jnp.sum(wide(item[:, proj_rows + rows :]), 0) for item in blocks)

    depths = range(1, layout.deep)
    zero.deepen(*depths)
    one.ahead(0)
    mixing = tie([zero, one], mix_more(0))
    zero.join(0)
    zero.ahead(0)
    one.deepen(*depths[:1])
    one.aside(0)
    mixing, picking, kinds, zero_tables, pick_turned = tie(
        [zero, one], mix_more(1), picking, kinds, tables(zero), pick_turned
    )
    zero.aside(0)
    zero.swap(0)
    two.ahead(0)
    one.deepen(*depths[1:2])
    mixing = tie([zero, one, two], mix_more(2))
    zero.swap_far(0)
    two.aside(0)
    one.deepen(*depths[2:])
    two.deepen(*depths[:1])
    bias_full = bias_part(zero.levels + zero.squares + zero.near)
    mixing, bias_full = tie([zero, one, two], mix_more(3), bias_full)
    bias_full = bias_full + bias_part(zero.far)
    one.join(1)

    def hidden_body(tables, ins, pieces, outs, _, scratch):
        pin, board, kinds, bias, picking = ins
        features, hidden, slope, outgoing, proj_out = outs
        weights, sems = scratch
        fetch(tables, pieces, 0, weights, sems.at[0])
        fetched(weights, sems.at[0])
        proj, weight = View(weights, 0, proj_rows), View(weights, proj_rows, rows)
        for band in bands(width):
            projected = dot(board[...], proj.columns(band))
            features[:, band] = low(jnp.where(kinds[...] == 1, wide(pin[:, band]), projected))
        for band in bands(board_width):
            proj_out[band, :] = proj.band(band)
        spread_hidden(features, weight, bias.at[0:1], picking, hidden, slope, outgoing)

    one.ahead(1)
    one.swap(0)
    one.swap_far(0)
    two.deepen(*depths[1:])
    features, hidden, hidden_slope, outgoing, proj_full = tie(
        [one, two],
        *call(
            "hidden",
            hidden_body,
            zero_tables,
            [pin_features, board_features, kinds, bias_full, picking],
            zero.pieces(),
            [nodes_low] * 3 + [far_low, ((board_width, width), LOW)],
            [],
            [blocks(proj_rows + rows), dma((1,))],
        ),
    )
    incoming, other = exchange(outgoing), swap_cores(hidden)
    one.aside(1)
    one.swap(1)
    two.join(1)
    two.ahead(1)
    incoming, other = tie([one, two], incoming, other)
    one.swap_far(1)
    tie([one])

    def middle_body(tables, ins, pieces, outs, _, scratch):
        mixes, (hidden, other, incoming, features, bias, picking) = ins[:3], ins[3:]
        mean, unit, slope_pre, scale, inner, slope_inner, result, ahead, slope_ahead, outgoing = outs
        both, rest, gated, sems = scratch
        fetch(tables, pieces, 0, both, sems.at[0])
        fetch(tables, pieces, half_rows, rest, sems.at[1])
        first, second, weight = (View(rest, n * rows, rows) for n in range(3))
        own, neigh = (View(both, 0, half_rows, half) for half in range(2))
        average(mixes, hidden, other, incoming, mean)
        fetched(both, sems.at[0])
        combine(features, mean, own, neigh, bias.at[2:3], gated, unit, slope_pre, scale)
        fetched(rest, sems.at[1])
        perceive(unit, first, bias.at[4:5], inner, slope_inner)
        conclude(inner, second, bias.at[6:7], result)
        spread_hidden(result, weight, bias.at[1:2], picking, ahead, slope_ahead, outgoing)

    two.swap(0)
    two.swap_far(0)
    two.aside(1)
    two.swap(1)
    (
        mean_zero,
        unit,
        slope_pre,
        scale,
        inner,
        slope_inner,
        features_one,
        hidden_one,
        hidden_slope_one,
        outgoing,
    ) = tie(
        [two],
        *call(
            "middle",
            middle_body,
            tables(one),
            [*mixing, hidden, other, incoming, features, bias_full, picking],
            one.pieces(),
            [nodes_low] * 3 + [column] + [nodes_low] * 5 + [far_low],
            [],
            [blocks(half_rows), blocks(3 * rows), own_wide, dma((2,))],
        ),
    )
    incoming, other = exchange(outgoing), swap_cores(hidden_one)
    two.swap_far(1)
    mix_turned = [item.T for item in mixing]
    incoming, other, mix_turned = tie([two], incoming, other, mix_turned)

    def top_body(tables, ins, pieces, outs, leave, scratch):
        mixes, (hidden, other, incoming, features, bias, grad_result) = ins[:3], ins[3:]
        mean, result, unit, slope_pre, scale, grad_inner, sums = outs
        weights, grads, gated, inner, slope_inner, sems = scratch
        fetch(tables, pieces, 0, weights, sems.at[0])
        own, neigh = (View(weights, 0, half_rows, half) for half in range(2))
        first, second = View(weights, half_rows, rows), View(weights, half_rows + rows, rows)
        average(mixes, hidden, other, incoming, mean)
        fetched(weights, sems.at[0])
        combine(features, mean, own, neigh, bias.at[3:4], gated, unit, slope_pre, scale)
        perceive(unit, first, bias.at[5:6], inner, slope_inner)
        weight_grad(inner, grad_result, View(grads, 0, rows))
        back_perceive(grad_result, second, slope_inner, grad_inner)
        weight_grad(unit, grad_inner, View(grads, rows, rows))
        send_off(tables, grads, *leave, (sems.at[1], sems.at[2]))
        conclude(inner, second, bias.at[7:8], result)
        sums[...] = jnp.zeros_like(sums)
        column_sums(grad_result, sums, 0)
        column_sums(grad_inner, sums, 1)
        sent_off(*leave, (sems.at[1], sems.at[2]))

    mean_one, embeddings, unit_one, slope_pre_one, scale_one, grad_inner, sums_one, kept, sent = call(
        "top",
        top_body,
        tables(two),
        [*mixing, hidden_one, other, incoming, features_one, bias_full, out_grad],
        two.pieces(),
        [nodes_low] * 4 + [column, nodes_low, sum_rows],
        leaving(2 * rows),
        [blocks(half_rows + 2 * rows), blocks(2 * rows), own_wide, own_nodes, own_nodes, dma((3,))],
    )
    five = Scatter(layout, kept, sent)

    def norm_body(tables, ins, pieces, outs, _, scratch):
        grad_inner, unit, scale, slope_pre, *mix_turned = ins
        grad_pre, grad_mean, far_out, sib_out, sums = outs
        weights, halves, grad_unit, sems = scratch
        fetch(tables, pieces, half_rows, weights, sems.at[0])
        fetch(tables, pieces, 0, halves, sems.at[1], 1)
        fetched(weights, sems.at[0])
        first = View(weights, 0, rows)
        back_unit(grad_inner, first, unit, scale, slope_pre, grad_unit, grad_pre)
        fetched(halves, sems.at[1])
        neigh = View(halves, 0, half_rows, 0)
        back_mean(grad_pre, neigh, mix_turned, grad_mean, far_out, sib_out)
        sums[...] = jnp.zeros_like(sums)
        column_sums(grad_pre, sums, 0)

    def norm(name, chain, *ins):
        return call(
            name,
            norm_body,
            tables(chain),
            [*ins, *mix_turned[1:]],
            chain.pieces(),
            [nodes_low] * 2 + [far_low, nodes_low, sum_rows],
            [],
            [blocks(rows), half_blocks, own_wide, dma((2,))],
        )

    def sides(name, chain, features, mean, grad_pre):
        def body(tables, ins, pieces, outs, leave, scratch):
            features, mean, grad_pre = ins
            both, grads, sems = scratch
            fetch(tables, pieces, 0, both, sems.at[0], 0)
            weight_grad(features, grad_pre, View(grads, 0, half_rows, 0))
            weight_grad(mean, grad_pre, View(grads, 0, half_rows, 1))
            send_off(tables, grads, *leave, (sems.at[1], sems.at[2]))
            fetched(both, sems.at[0])
            own = View(both, 0, half_rows, 0)
            for band in bands(width):
                outs[0][:, band] = low(dot_right(grad_pre[...], own.band(band)))
            sent_off(*leave, (sems.at[1], sems.at[2]))

        return call(
            name,
            body,
            tables(chain),
            [features, mean, grad_pre],
            chain.pieces(),
            [nodes_low],
            leaving(half_rows),
            [half_blocks, blocks(half_rows), dma((3,))],
        )

    five.advance()
    grad_pre, grad_mean, far_out, sib_out, sums_pre_one = tie(
        [five], *norm("norm1", two, grad_inner, unit_one, scale_one, slope_pre_one)
    )
    five.advance()
    far_back, sib_back = exchange(far_out), swap_cores(sib_out)
    grad_self, kept, sent = sides("sides1", two, features_one, mean_one, grad_pre)
    far_back, sib_back, grad_self, kept, sent = tie([five], far_back, sib_back, grad_self, kept, sent)
    six = Scatter(layout, kept, sent)

    def bridge_body(tables, ins, pieces, outs, leave, scratch):
        own, pick, grad_mean, sib_back, far_back, slope_hidden, features, grad_self = ins[:8]
        inner, unit, slope_inner = ins[8:]
        grad_inner, sums = outs
        weights, grads, grad_hidden_pre, grad_input, sems = scratch
        fetch(tables, pieces, half_rows + rows, weights, sems.at[0])
        back_hidden(own, pick, grad_mean, sib_back, far_back, slope_hidden, grad_hidden_pre)
        weight_grad(features, grad_hidden_pre, View(grads, 0, rows))
        fetched(weights, sems.at[0])
        back_input(grad_self, grad_hidden_pre, View(weights, rows, rows), grad_input)
        weight_grad(inner, grad_input, View(grads, rows, rows))
        back_perceive(grad_input, View(weights, 0, rows), slope_inner, grad_inner)
        weight_grad(unit, grad_inner, View(grads, 2 * rows, rows))
        send_off(tables, grads, *leave, (sems.at[1], sems.at[2]))
        sums[...] = jnp.zeros_like(sums)
        column_sums(grad_hidden_pre, sums, 0)
        column_sums(grad_input, sums, 1)
        column_sums(grad_inner, sums, 2)
        sent_off(*leave, (sems.at[1], sems.at[2]))

    five.advance()
    six.advance()
    grad_inner, sums_zero, kept, sent = tie(
        [five, six],
        *call(
            "bridge",
            bridge_body,
            tables(one),
            [mix_turned[0], pick_turned, grad_mean, sib_back, far_back, hidden_slope_one]
            + [features_one, grad_self, inner, unit, slope_inner],
            one.pieces(),
            [nodes_low, sum_rows],
            leaving(3 * rows),
            [blocks(2 * rows), blocks(3 * rows), own_nodes, own_nodes, dma((3,))],
        ),
    )
    seven = Scatter(layout, kept, sent)
    five.advance()
    six.advance()
    seven.advance()
    grad_pre, grad_mean, far_out, sib_out, sums_pre_zero = tie(
        [five, six, seven], *norm("norm0", one, grad_inner, unit, scale, slope_pre)
    )
    seven.advance()
    far_back, sib_back = exchange(far_out), swap_cores(sib_out)
    grad_self, kept, sent = sides("sides0", one, features, mean_zero, grad_pre)
    far_back, sib_back, grad_self, kept, sent = tie(
        [six, seven], far_back, sib_back, grad_self, kept, sent
    )
    eight = Scatter(layout, kept, sent)

    def bottom_body(tables, ins, pieces, outs, leave, scratch):
        own, pick, grad_mean, sib_back, far_back, slope_hidden, features, grad_self = ins[:8]
        board, kinds, sums_one, pre_one, sums_zero, pre_zero = ins[8:]
        (grad_input,) = outs
        weights, grads, grad_hidden_pre, grad_board, sums, sems = scratch
        fetch(tables, pieces, proj_rows, weights, sems.at[0])
        back_hidden(own, pick, grad_mean, sib_back, far_back, slope_hidden, grad_hidden_pre)
        weight_grad(features, grad_hidden_pre, View(grads, 0, rows))
        column_sums(grad_hidden_pre, sums, 0)
        fetched(weights, sems.at[0])
        back_input(grad_self, grad_hidden_pre, View(weights, 0, rows), grad_input)
        for band in bands(width):
            grad_board[:, band] = low(jnp.where(kinds[...] == 1, 0.0, wide(grad_input[:, band])))
        weight_grad(board, grad_board, View(grads, rows, proj_rows))
        totals = [sums[0:1, :], sums_zero[0:1, :], pre_zero[0:1, :], pre_one[0:1, :]]
        totals += [sums_zero[2:3, :], sums_one[1:2, :], sums_zero[1:2, :], sums_one[0:1, :]]
        totals = low(jnp.concatenate([*totals, jnp.zeros((8, width), jnp.float32)]))
        for chip in range(layout.rows):
            for half in range(2):
                grads[chip, half, rows + proj_rows :, :] = totals
        send_off(tables, grads, *leave, (sems.at[1], sems.at[2]))
        sent_off(*leave, (sems.at[1], sems.at[2]))

    six.advance()
    seven.advance()
    eight.advance()
    grad_input, kept, sent = tie(
        [six, seven, eight],
        *call(
            "bottom",
            bottom_body,
            zero_tables,
            [mix_turned[0], pick_turned, grad_mean, sib_back, far_back, hidden_slope, features]
            + [grad_self, board_features, kinds, sums_one, sums_pre_one, sums_zero, sums_pre_zero],
            zero.pieces(),
            [nodes_low],
            leaving(rows + proj_rows + 16),
            [blocks(rows), blocks(rows + proj_rows + 16), own_nodes, own_nodes]
            + [pltpu.VMEM(*sum_rows), dma((3,))],
        ),
    )
    nine = Scatter(layout, kept, sent)
    chains = [five, six, seven, eight, nine]
    eight.advance()
    nine.advance()
    six.advance()
    tie([nine])
    nine.advance()
    tie([eight, six])
    eight.advance()
    seven.advance()
    tie([nine, eight, seven])
    nine.advance()
    eight.advance()
    tie([nine])
    nine.advance()
    is_pin = kinds == 1
    pin_grad = jnp.where(is_pin, wide(grad_input), 0.0)
    grad_board = jnp.where(is_pin, jnp.zeros_like(grad_input), grad_input)
    board_grad = dot_right(grad_board, proj_full)

    five, six, seven, eight, nine = (chain.result() for chain in chains)
    bias_sums = nine[rows + proj_rows :][:bias_count]
    bias_sums = lax.dynamic_slice_in_dim(bias_sums, device * own_bias, own_bias, 1)
    bias_sums = bias_sums.reshape(4, -1, own_bias)
    return (
        embeddings,
        pin_grad,
        board_grad,
        nine[rows : rows + proj_rows],
        jnp.stack([nine[:rows], seven[:rows]]),
        bias_sums[0],
        jnp.stack([eight, six])[:, None],
        bias_sums[1],
        jnp.stack([seven[2 * rows :], five[rows:]]),
        bias_sums[2],
        jnp.stack([seven[rows : 2 * rows], five[:rows]]),
        bias_sums[3],
    )


def solution(mesh):
    nodes = P(("rows", "half"), None)
    weight = P(None, ("rows", "half"), None)
    bias = P(None, ("rows", "half"))
    concat = P(None, "half", "rows", None)
    placed = (nodes, nodes, P(("rows", "half")), nodes, nodes, nodes, nodes)
    placed += (weight, bias, concat, bias, weight, bias, weight, bias, nodes)
    results = (nodes, nodes, nodes, nodes) + (weight, bias, concat, bias, weight, bias, weight, bias)

    def whole(*args):
        devices = mesh.shape["rows"] * mesh.shape["half"]
        shards = (args[6].shape[0] // devices, args[7].shape[1] // devices)
        fits = mesh.shape["rows"] % 4 == 0 and not any(count % 16 for count in shards)
        return jax.shard_map(
            local if fits else plain,
            mesh=mesh,
            in_specs=placed,
            out_specs=results,
            check_vma=False,
        )(*args)

    return whole
```
